32 devices in a mesh: dp: 16 (over z, y, x), head: 2 (over core).
Axes of the slice: x: 2, y: 2, z: 4, core: 2. Of those that a mesh axis runs over, the one named last changes fastest.
Arguments:
- hidden: bfloat16 [30720, 768], P('dp'), may hold values from -6 to 6
- cotangent: bfloat16 [30720, 768], P('dp'), may hold values from -6 to 6
- counts: int32 [16, 2, 4], P('dp'), may hold values from 0 to 1, as said below
- lengths: int32 [16, 2, 4], P('dp'), may hold values from 33 to 512, as said below
- qkv_weight: bfloat16 [768, 3, 768], P(None, None, 'head'), may hold values from -0.21875 to 0.21875
- qv_bias: float32 [2, 768], P(None, 'head'), may hold values from -1.25 to 1.25
- out_weight: bfloat16 [768, 768], P('head'), may hold values from -1.75 to 1.75
- out_bias: float32 [768], replicated, may hold values from -3 to 3
- ln1_gain: float32 [768], replicated, may hold values from 0.25 to 1.75
- ln1_bias: float32 [768], replicated, may hold values from -3 to 3
- in_weight: bfloat16 [768, 3072], P(None, 'head'), may hold values from -0.21875 to 0.21875
- in_bias: float32 [3072], P('head'), may hold values from -3 to 3
- ffn_out_weight: bfloat16 [3072, 768], P('head'), may hold values from -0.3125 to 0.3125
- ffn_out_bias: float32 [768], replicated, may hold values from -3 to 3
- ln2_gain: float32 [768], replicated, may hold values from 0.25 to 1.75
- ln2_bias: float32 [768], replicated, may hold values from -3 to 3
- head_gate: float32 [12], P('head'), may hold values from 0.25 to 1
- head_mask: int32 [12], P('head'), may hold values 0 or 1
- ffn_gate: float32 [3072], P('head'), may hold values from 0.25 to 1
- ffn_mask: int32 [3072], P('head'), may hold values 0 or 1
- hidden_gate: float32 [768], replicated, may hold values from 0.5 to 1
- hidden_mask: int32 [768], replicated, may hold values 0 or 1
Outputs:
- layer_out: bfloat16 [30720, 768], P(('dp', 'head'))
- grad_hidden: float32 [30720, 768], P(('dp', 'head'))
- grad_qkv_weight: float32 [768, 3, 768], P(None, None, 'head')
- grad_qv_bias: float32 [2, 768], P(None, 'head')
- grad_out_weight: float32 [768, 768], P('head')
- grad_out_bias: float32 [768], replicated
- grad_ln1_gain: float32 [768], replicated
- grad_ln1_bias: float32 [768], replicated
- grad_in_weight: float32 [768, 3072], P(None, 'head')
- grad_in_bias: float32 [3072], P('head')
- grad_ffn_out_weight: float32 [3072, 768], P('head')
- grad_ffn_out_bias: float32 [768], replicated
- grad_ln2_gain: float32 [768], replicated
- grad_ln2_bias: float32 [768], replicated
- grad_head_gate: float32 [12], P('head')
- grad_ffn_gate: float32 [3072], P('head')
- grad_hidden_gate: float32 [768], replicated
The draws below stay inside these ranges and needn't reach their ends.
Inputs may be any that keep to these rules, and one draw needn't show every extreme that they name: counts[i, j, b] is 1 where bucket b of set j of data index i holds a sequence and 0 where it is empty; some data index has all four buckets of its first set live. lengths[i, j, b] lies above half of its bucket's length (512, 256, 128, 64) and at most at it; some data index holds a live sequence of exactly 512 tokens.
All inputs are finite; a program needn't handle non-finite values. No bound on the sum of `head_mask` or of `ffn_mask` on one device may be relied on, other than what follows from the above.
Results may differ from the reference program's by a relative error of at most 0.012.
Values may be sent and summed in bfloat16 or wider, within the bound.
No kernel may reach another device: no remote copies, remote signals or barrier semaphores. Data moves between devices by JAX's collectives and lax.ppermute only.
A program may use at most 256 MiB of HBM per device.

```python
import jax
import jax.numpy as jnp
import numpy as np
from jax import lax

D = 768
HEADS = 12
HEAD_DIM = 64
FF = 3072
BASE = 64
SETS = 2
TOKENS = 30720
N_DP = 16


def chosen_index(key):
    return jax.random.randint(jax.random.fold_in(key, 5), (), 0, N_DP)


def draw_counts(key, part):
    chosen = chosen_index(key)
    key = jax.random.fold_in(key, 11)
    live_draw = jax.random.randint(key, (N_DP, SETS, 4), 0, 4)
    picked = (jnp.arange(N_DP)[:, None, None] == chosen) & (jnp.arange(SETS)[None, :, None] == 0)
    return jnp.where(picked | (live_draw > 0), 1, 0).astype(jnp.int32)


def draw_lengths(key, part):
    chosen = chosen_index(key)
    key = jax.random.fold_in(key, 23)
    bucket = jnp.array([8 * BASE, 4 * BASE, 2 * BASE, BASE], jnp.int32)
    below_top = jax.random.randint(key, (N_DP, SETS, 4), 0, 1 << 20) % (bucket // 2)[None, None, :]
    picked = (jnp.arange(N_DP)[:, None, None] == chosen) & (jnp.arange(SETS)[None, :, None] == 0) & (jnp.arange(4)[None, None, :] == 0)
    return jnp.where(picked, bucket[None, None, :], bucket[None, None, :] - below_top).astype(jnp.int32)


def plant(values, key, low, top_value):
    index_at = [jax.random.randint(jax.random.fold_in(key, axis), (), 0, length) for axis, length in enumerate(values.shape)]
    widest = values.shape.index(max(values.shape))
    neighbour = index_at[:widest] + [(index_at[widest] + 1) % values.shape[widest]] + index_at[widest + 1:]
    return values.at[tuple(index_at)].set(low).at[tuple(neighbour)].set(top_value)


def level_of(own_key, extent, cuts, smallest, largest):
    level, own = 1.0, jax.random.fold_in(own_key, 6)
    for axis_at, shards_of in cuts:
        steps = jnp.exp(jax.random.uniform(jax.random.fold_in(own, axis_at), (shards_of,), jnp.float32, smallest / len(cuts), largest / len(cuts)))
        level = level * jnp.repeat(steps, extent[axis_at] // shards_of).reshape([-1 if axis == axis_at else 1 for axis in range(len(extent))])
    return level


def gaussian(rng, extent, deviation, bound, shards=(), dtype=jnp.bfloat16):
    drawn = deviation * jax.random.normal(rng, extent, jnp.float32)
    if shards:
        drawn = drawn * level_of(rng, extent, shards, -0.22, 0.18)
    return jnp.clip(drawn, -bound, bound).astype(dtype)


def setup_inputs(seed: int = 0) -> dict:
    key_of = jax.random.split(jax.random.key(seed), 23)
    hidden = gaussian(key_of[0], (TOKENS, D), 1.0, 6.0, ((0, 16),))
    cotangent = gaussian(key_of[1], (TOKENS, D), 1.0, 6.0, ((0, 16),))
    counts = draw_counts(jax.random.fold_in(key_of[22], 71), 0)
    lengths = draw_lengths(jax.random.fold_in(key_of[22], 71), 0)
    qkv_weight = gaussian(key_of[4], (D, 3, HEADS * HEAD_DIM), D ** -0.5, 0.21875, ((2, 2),))
    qv_bias = gaussian(key_of[5], (2, HEADS * HEAD_DIM), 0.2, 1.25, ((1, 2),), jnp.float32)
    out_weight = gaussian(key_of[6], (HEADS * HEAD_DIM, D), (D // 64) ** -0.5, 1.75, ((0, 2),))
    out_bias = gaussian(key_of[7], (D,), 0.5, 3.0, (), jnp.float32)
    ln1_gain = jnp.clip(1.0 + 0.15 * jax.random.normal(key_of[8], (D,), jnp.float32), 0.25, 1.75)
    ln1_bias = gaussian(key_of[9], (D,), 0.5, 3.0, (), jnp.float32)
    in_weight = gaussian(key_of[10], (D, FF), D ** -0.5, 0.21875, ((1, 2),))
    in_bias = gaussian(key_of[11], (FF,), 0.5, 3.0, ((0, 2),), jnp.float32)
    ffn_out_weight = gaussian(key_of[12], (FF, D), (FF // 8) ** -0.5, 0.3125, ((0, 2),))
    ffn_out_bias = gaussian(key_of[13], (D,), 0.5, 3.0, (), jnp.float32)
    ln2_gain = jnp.clip(1.0 + 0.15 * jax.random.normal(key_of[14], (D,), jnp.float32), 0.25, 1.75)
    ln2_bias = gaussian(key_of[15], (D,), 0.5, 3.0, (), jnp.float32)
    head_gate = jnp.clip(0.25 + 0.75 * jax.random.uniform(key_of[16], (HEADS,), jnp.float32) ** level_of(key_of[16], (HEADS,), ((0, 2),), -0.2, 0.2), 0.25, 1.0)
    head_mask = plant((jax.random.randint(key_of[17], (HEADS,), 0, 3) < 2).astype(jnp.int32), jax.random.fold_in(key_of[17], 1), 0, 1)
    ffn_gate = jnp.clip(0.25 + 0.75 * jax.random.uniform(key_of[18], (FF,), jnp.float32) ** level_of(key_of[18], (FF,), ((0, 2),), -0.2, 0.2), 0.25, 1.0)
    ffn_mask = plant((jax.random.randint(key_of[19], (FF,), 0, 4) < 3).astype(jnp.int32), jax.random.fold_in(key_of[19], 1), 0, 1)
    hidden_gate = jnp.clip(jax.random.uniform(key_of[20], (D,), jnp.float32, 0.5, 1.0), 0.5, 1.0)
    hidden_mask = plant((jax.random.randint(key_of[21], (D,), 0, 8) < 7).astype(jnp.int32), jax.random.fold_in(key_of[21], 1), 0, 1)
    return dict(hidden=hidden, cotangent=cotangent, counts=counts, lengths=lengths, qkv_weight=qkv_weight, qv_bias=qv_bias, out_weight=out_weight, out_bias=out_bias, ln1_gain=ln1_gain, ln1_bias=ln1_bias, in_weight=in_weight, in_bias=in_bias, ffn_out_weight=ffn_out_weight, ffn_out_bias=ffn_out_bias, ln2_gain=ln2_gain, ln2_bias=ln2_bias, head_gate=head_gate, head_mask=head_mask, ffn_gate=ffn_gate, ffn_mask=ffn_mask, hidden_gate=hidden_gate, hidden_mask=hidden_mask)


@jax.custom_vjp
def low(v):
    return lax.optimization_barrier(v.astype(jnp.bfloat16)).astype(jnp.float32)

@jax.custom_vjp
def low_back(v):
    return v

def low_keep(v):
    return (low(v), None)

def low_pass(kept, grad):
    return (grad,)

def back_keep(v):
    return (v, None)

def back_low(kept, grad):
    return (low(grad),)
low.defvjp(low_keep, low_pass)
low_back.defvjp(back_keep, back_low)
EPSILON = 1e-12
MASKED = -1000000000.0
HIGHEST = lax.Precision.HIGHEST

def row_masks(live_flags, seq_lengths):
    set_rows = 15 * BASE
    slot_of_row = np.repeat(np.arange(4), [8 * BASE, 4 * BASE, 2 * BASE, BASE])
    offset = np.arange(set_rows) - np.array([0, 8 * BASE, 12 * BASE, 14 * BASE])[slot_of_row]
    picker = jnp.asarray(slot_of_row[:, None] == np.arange(4)[None, :], jnp.int32)
    live_row = lax.optimization_barrier(jnp.sum(picker[None] * live_flags[:, None, :], 2))
    length_row = lax.optimization_barrier(jnp.sum(picker[None] * seq_lengths[:, None, :], 2))
    valid_rows = (live_row > 0) & (jnp.asarray(offset, jnp.int32)[None] < length_row)
    long_rows = 8 * BASE
    same_slot = jnp.asarray(slot_of_row[long_rows:, None] == slot_of_row[None, long_rows:])
    mask_long = jnp.broadcast_to(valid_rows[:, None, :long_rows], (SETS, long_rows, long_rows))
    mask_short = same_slot[None] & valid_rows[:, None, long_rows:]
    return (valid_rows.reshape(-1).astype(jnp.float32), mask_long, mask_short)

def layer_norm(resid, gain, shift):
    centred = resid - lax.optimization_barrier(jnp.mean(resid, -1, keepdims=True))
    spread = lax.rsqrt(lax.optimization_barrier(jnp.mean(centred * centred, -1, keepdims=True)) + EPSILON)
    return centred * spread * gain + shift

def attend_block(queries, key_rows, value_rows, allowed):
    raw = jnp.einsum('bqhd,bkhd->bhqk', queries, key_rows, precision=HIGHEST) * float(HEAD_DIM) ** (-0.5)
    scores = jnp.where(allowed[:, None], low_back(raw), MASKED)
    row_top = lax.optimization_barrier(jnp.max(scores, -1, keepdims=True))
    exponent = jnp.exp(scores - row_top)
    weights = exponent / lax.optimization_barrier(jnp.sum(exponent, -1, keepdims=True))
    return low_back(jnp.einsum('bhqk,bkhd->bqhd', low(weights), value_rows, precision=HIGHEST))

def forward(params, hidden_rows, valid_rows, mask_long, mask_short, head_flags, ffn_flags, hidden_flags):
    qkv_weight, qv_bias, out_weight, out_bias, ln1_gain, ln1_bias, in_weight, in_bias, ffn_out_weight, ffn_out_bias, ln2_gain, ln2_bias, head_gate, ffn_gate, hidden_gate = params
    row_total = hidden_rows.shape[0]
    long_rows = 8 * BASE
    head_eff = head_gate * head_flags
    ffn_eff = ffn_gate * ffn_flags
    hid_eff = hidden_gate * hidden_flags
    mixed = low_back(jnp.dot(hidden_rows, qkv_weight.reshape(D, -1), precision=HIGHEST)).reshape(row_total, 3, -1)
    bias_three = jnp.stack([qv_bias[0], jnp.zeros_like(qv_bias[0]), qv_bias[1]])
    qkv = low(mixed + bias_three[None]).reshape(SETS, 15 * BASE, 3, HEADS, HEAD_DIM)
    long_part = qkv[:, :long_rows]
    short_part = qkv[:, long_rows:]
    checked = jax.checkpoint(attend_block)
    context_long = checked(long_part[:, :, 0], long_part[:, :, 1], long_part[:, :, 2], mask_long)
    context_short = checked(short_part[:, :, 0], short_part[:, :, 1], short_part[:, :, 2], mask_short)
    context = jnp.concatenate([context_long, context_short], 1).reshape(row_total, HEADS, HEAD_DIM)
    gated = low(context * head_eff[None, :, None]).reshape(row_total, -1)
    attn_out = low_back(jnp.dot(gated, out_weight, precision=HIGHEST)) + out_bias
    first = layer_norm(hidden_rows + attn_out * hid_eff, ln1_gain, ln1_bias)
    pre = low_back(jnp.dot(low(first), in_weight, precision=HIGHEST)) + in_bias
    inner = low(jax.nn.gelu(pre, approximate=False) * ffn_eff)
    ffn_out = low_back(jnp.dot(inner, ffn_out_weight, precision=HIGHEST)) + ffn_out_bias
    return layer_norm(first + ffn_out * hid_eff, ln2_gain, ln2_bias) * valid_rows[:, None]

def reference(hidden, cotangent, counts, lengths, qkv_weight, qv_bias, out_weight, out_bias, ln1_gain, ln1_bias, in_weight, in_bias, ffn_out_weight, ffn_out_bias, ln2_gain, ln2_bias, head_gate, head_mask, ffn_gate, ffn_mask, hidden_gate, hidden_mask):
    params = jax.tree.map(lambda weight_part: weight_part.astype(jnp.float32), (qkv_weight, qv_bias, out_weight, out_bias, ln1_gain, ln1_bias, in_weight, in_bias, ffn_out_weight, ffn_out_bias, ln2_gain, ln2_bias, head_gate, ffn_gate, hidden_gate))
    head_flags = head_mask.astype(jnp.float32)
    ffn_flags = ffn_mask.astype(jnp.float32)
    hidden_flags = hidden_mask.astype(jnp.float32)
    row_total = 15 * BASE * SETS
    blocks = (hidden.astype(jnp.float32).reshape(N_DP, row_total, D), cotangent.astype(jnp.float32).reshape(N_DP, row_total, D), counts, lengths)

    def device_step(carried, pieces):
        hidden_rows, cot_rows, live_flags, seq_lengths = pieces
        valid_rows, mask_long, mask_short = row_masks(live_flags, seq_lengths)

        def layer(weights, rows_in):
            return forward(weights, rows_in, valid_rows, mask_long, mask_short, head_flags, ffn_flags, hidden_flags)
        layer_rows, pull = jax.vjp(layer, params, hidden_rows)
        grad_params, grad_rows = pull(cot_rows)
        carried = jax.tree.map(jnp.add, carried, grad_params)
        return (carried, (layer_rows, grad_rows))
    zero_grads = jax.tree.map(jnp.zeros_like, params)
    totals, (layer_rows, grad_rows) = lax.scan(device_step, zero_grads, blocks)
    return (layer_rows.reshape(TOKENS, D).astype(jnp.bfloat16), grad_rows.reshape(TOKENS, D), totals[0], totals[1], totals[2], totals[3], totals[4], totals[5], totals[6], totals[7], totals[8], totals[9], totals[10], totals[11], totals[12], totals[13], totals[14])
```

```python
from functools import partial

import jax
import jax.numpy as jnp
import numpy as np
from jax import lax
from jax.sharding import PartitionSpec as P

BASE = 64
SETS = 2


EPSILON = 1e-12
MASKED = -1000000000.0


def row_masks(live_flags, seq_lengths):
    set_rows = 15 * BASE
    slot_of_row = np.repeat(np.arange(4), [8 * BASE, 4 * BASE, 2 * BASE, BASE])
    offset = np.arange(set_rows) - np.array([0, 8 * BASE, 12 * BASE, 14 * BASE])[slot_of_row]
    picker = jnp.asarray(slot_of_row[:, None] == np.arange(4)[None, :], jnp.int32)
    live_row = jnp.sum(picker[None] * live_flags[:, None, :], 2)
    length_row = jnp.sum(picker[None] * seq_lengths[:, None, :], 2)
    valid_rows = (live_row > 0) & (jnp.asarray(offset, jnp.int32)[None] < length_row)
    long_rows = 8 * BASE
    same_slot = jnp.asarray(slot_of_row[long_rows:, None] == slot_of_row[None, long_rows:])
    mask_long = jnp.broadcast_to(valid_rows[:, None, :long_rows], (SETS, long_rows, long_rows))
    mask_short = same_slot[None] & valid_rows[:, None, long_rows:]
    return (valid_rows.reshape(-1).astype(jnp.float32), mask_long, mask_short)


def split_sets(values):
    shaped = values.reshape((1, 15 * BASE) + values.shape[1:])
    return (shaped[:, : 8 * BASE], shaped[:, 8 * BASE :])


def join_sets(long_part, short_part):
    return jnp.concatenate([long_part, short_part], 1).reshape((-1,) + long_part.shape[2:])


def by_rows(left, right):
    return lax.dot_general(
        left, right, (((0,), (0,)), ((), ())), preferred_element_type=jnp.float32
    )


def by_cols(left, right):
    return lax.dot_general(
        left, right, (((1,), (1,)), ((), ())), preferred_element_type=jnp.float32
    )


def norm_forward(resid, gain, shift):
    centred = resid - jnp.mean(resid, -1, keepdims=True)
    spread = lax.rsqrt(jnp.mean(centred * centred, -1, keepdims=True) + EPSILON)
    normed = centred * spread
    return (normed * gain + shift, normed, spread)


def norm_backward(grad_out, normed, spread, gain):
    grad_normed = grad_out * gain
    first_mean = jnp.mean(grad_normed, -1, keepdims=True)
    second_mean = jnp.mean(grad_normed * normed, -1, keepdims=True)
    return spread * (grad_normed - first_mean - normed * second_mean)


def masked_scores(queries, key_rows, allowed, score_scale):
    raw = (
        jnp.einsum("bqhd,bkhd->bhqk", queries, key_rows, preferred_element_type=jnp.float32)
        * score_scale
    )
    return jnp.where(allowed[:, None], raw, MASKED)


def attend(queries, key_rows, value_rows, allowed, score_scale):
    scores = masked_scores(queries, key_rows, allowed, score_scale)
    row_top = jnp.max(scores, -1, keepdims=True)
    exponent = jnp.exp(scores - row_top)
    row_sum = jnp.sum(exponent, -1, keepdims=True)
    weights = (exponent / row_sum).astype(jnp.bfloat16)
    context = jnp.einsum("bhqk,bkhd->bqhd", weights, value_rows, preferred_element_type=jnp.float32)
    return (context, row_top + jnp.log(row_sum))


def attend_back(queries, key_rows, value_rows, allowed, score_scale, log_total, grad_context):
    weights = jnp.exp(masked_scores(queries, key_rows, allowed, score_scale) - log_total)
    grad_weights = jnp.einsum(
        "bqhd,bkhd->bhqk", grad_context, value_rows, preferred_element_type=jnp.float32
    )
    grad_values = jnp.einsum(
        "bhqk,bqhd->bkhd",
        weights.astype(jnp.bfloat16),
        grad_context,
        preferred_element_type=jnp.float32,
    )
    grad_scores = (
        weights * (grad_weights - jnp.sum(weights * grad_weights, -1, keepdims=True))
    ).astype(jnp.bfloat16)
    grad_queries = (
        jnp.einsum("bhqk,bkhd->bqhd", grad_scores, key_rows, preferred_element_type=jnp.float32)
        * score_scale
    )
    grad_keys = (
        jnp.einsum("bhqk,bqhd->bkhd", grad_scores, queries, preferred_element_type=jnp.float32)
        * score_scale
    )
    return (grad_queries, grad_keys, grad_values)


def gelu_and_slope(z):
    size = jnp.abs(z)
    density = jnp.exp(-0.5 * z * z)
    t = 1.0 / (1.0 + (0.3275911 * 0.5**0.5) * size)
    series = t * (
        0.254829592
        + t * (-0.284496736 + t * (1.421413741 + t * (-1.453152027 + t * 1.061405429)))
    )
    tail = 0.5 * series * density
    below = jnp.where(z < 0, tail, 1.0 - tail)
    return (z * below, below + z * density * (0.5 / np.pi) ** 0.5)


def bit_order(dp_size, turn):
    bits = dp_size.bit_length() - 1
    return [(place + turn) % bits for place in range(bits)]


def swap_bit(values, dp_size, bit):
    return lax.ppermute(values, "dp", [(at, at ^ (1 << bit)) for at in range(dp_size)])


def reduce_pieces(values, dp_size, turn):
    for bit in bit_order(dp_size, turn):
        side = (lax.axis_index("dp") >> bit) & 1
        half = values.shape[0] // 2
        kept = lax.dynamic_slice_in_dim(values, side * half, half, 0)
        sent = lax.dynamic_slice_in_dim(values, (1 - side) * half, half, 0)
        arrived = swap_bit(sent.astype(jnp.bfloat16), dp_size, bit)
        values = (kept.astype(jnp.float32) + arrived.astype(jnp.float32)).astype(jnp.bfloat16)
    return values


def gather_pieces(values, dp_size, turn):
    for bit in reversed(bit_order(dp_size, turn)):
        side = (lax.axis_index("dp") >> bit) & 1
        arrived = swap_bit(values, dp_size, bit)
        values = jnp.concatenate(
            [jnp.where(side == 0, values, arrived), jnp.where(side == 0, arrived, values)], 0
        )
    return values.astype(jnp.float32)


def per_device(
    dp_size,
    hidden,
    cotangent,
    counts,
    lengths,
    qkv_weight,
    qv_bias,
    out_weight,
    out_bias,
    ln1_gain,
    ln1_bias,
    in_weight,
    in_bias,
    ffn_out_weight,
    ffn_out_bias,
    ln2_gain,
    ln2_bias,
    head_gate,
    head_mask,
    ffn_gate,
    ffn_mask,
    hidden_gate,
    hidden_mask,
):
    width = hidden.shape[1]
    half_rows = hidden.shape[0] // 2
    own_heads = head_gate.shape[0]
    local_heads = 2 * own_heads
    half_width = qkv_weight.shape[2]
    half_units = in_weight.shape[1]
    head_width = half_width // own_heads
    score_scale = float(head_width) ** (-0.5)
    head_at = lax.axis_index("head")

    def other(values):
        return lax.ppermute(values, "head", [(0, 1), (1, 0)])

    def both(values, axis):
        return jnp.concatenate([values, other(values)], axis)

    def own_part(values):
        return lax.dynamic_slice_in_dim(values, head_at * half_rows, half_rows, 0)

    small = jnp.concatenate(
        [
            qv_bias.reshape(-1),
            in_bias,
            head_gate * head_mask.astype(jnp.float32),
            head_mask.astype(jnp.float32),
            ffn_gate * ffn_mask.astype(jnp.float32),
            ffn_mask.astype(jnp.float32),
        ]
    )
    cuts = np.cumsum([2 * half_width, half_units, own_heads, own_heads, half_units])
    pairs = [
        jnp.stack(pair)
        for pair in zip(jnp.split(small, cuts), jnp.split(other(small), cuts), strict=True)
    ]
    qv_bias_all = pairs[0].reshape(2, 2, half_width).transpose(1, 0, 2).reshape(2, -1)
    in_bias_all, head_eff, head_flags, ffn_eff, ffn_flags = (p.reshape(-1) for p in pairs[1:])
    qkv_flat = both(qkv_weight, 2).reshape(width, -1)
    out_all = both(out_weight, 0)
    in_all = both(in_weight, 1)
    ffn_out_all = both(ffn_out_weight, 0)
    hidden = own_part(hidden)
    cotangent = own_part(cotangent)
    row_total = half_rows
    valid_rows, mask_long, mask_short = row_masks(counts[0], lengths[0])
    valid_rows = own_part(valid_rows)
    mask_long = lax.dynamic_slice_in_dim(mask_long, head_at, 1, 0)
    mask_short = lax.dynamic_slice_in_dim(mask_short, head_at, 1, 0)
    hid_eff = hidden_gate * hidden_mask.astype(jnp.float32)

    mixed = jnp.dot(hidden, qkv_flat, preferred_element_type=jnp.float32).reshape(row_total, 3, -1)
    bias_three = jnp.stack([qv_bias_all[0], jnp.zeros_like(qv_bias_all[0]), qv_bias_all[1]])
    qkv = (
        (mixed + bias_three[None])
        .astype(jnp.bfloat16)
        .reshape(row_total, 3, local_heads, head_width)
    )
    query_long, query_short = split_sets(qkv[:, 0])
    key_long, key_short = split_sets(qkv[:, 1])
    value_long, value_short = split_sets(qkv[:, 2])
    context_long, log_long = attend(query_long, key_long, value_long, mask_long, score_scale)
    context_short, log_short = attend(query_short, key_short, value_short, mask_short, score_scale)
    context = join_sets(context_long, context_short)
    gated = (context * head_eff[None, :, None]).astype(jnp.bfloat16).reshape(row_total, -1)
    attn_out = jnp.dot(gated, out_all, preferred_element_type=jnp.float32) + out_bias
    first, normed_one, spread_one = norm_forward(
        hidden.astype(jnp.float32) + attn_out * hid_eff, ln1_gain, ln1_bias
    )
    first_low = first.astype(jnp.bfloat16)
    pre = jnp.dot(first_low, in_all, preferred_element_type=jnp.float32) + in_bias_all
    activation, slope = gelu_and_slope(pre)
    inner = (activation * ffn_eff).astype(jnp.bfloat16)
    ffn_out = jnp.dot(inner, ffn_out_all, preferred_element_type=jnp.float32) + ffn_out_bias
    final, normed_two, spread_two = norm_forward(first + ffn_out * hid_eff, ln2_gain, ln2_bias)
    mine_valid = valid_rows[:, None]
    layer_out = (final * mine_valid).astype(jnp.bfloat16)
    grad_final = cotangent.astype(jnp.float32) * mine_valid
    grad_two = norm_backward(grad_final, normed_two, spread_two, ln2_gain)
    grad_ffn = grad_two * hid_eff
    grad_ffn_low = grad_ffn.astype(jnp.bfloat16)

    def head_sum(grad_mine, grad_other):
        return grad_mine + other(grad_other.astype(jnp.bfloat16)).astype(jnp.float32)

    def head_sum_rows(left, right, axis, side):
        if side == 0:
            cut = left.shape[1] // 2
            mine, theirs = by_rows(left[:, :cut], right), by_rows(left[:, cut:], right)
        else:
            cut = right.shape[1] // 2
            mine, theirs = by_rows(left, right[:, :cut]), by_rows(left, right[:, cut:])
        return head_sum(mine, theirs)

    grad_ffn_out_weight = head_sum_rows(inner, grad_ffn_low, 0, 0)
    grad_inner = by_cols(grad_ffn_low, ffn_out_all)
    grad_ffn_gate = jnp.sum(activation * grad_inner, 0) * ffn_flags
    grad_pre = grad_inner * ffn_eff * slope
    grad_in_bias = jnp.sum(grad_pre, 0)
    grad_pre_low = grad_pre.astype(jnp.bfloat16)
    grad_in_weight = head_sum_rows(first_low, grad_pre_low, 1, 1)
    ffn_out_pieces = reduce_pieces(grad_ffn_out_weight, dp_size, 0)
    in_pieces = reduce_pieces(grad_in_weight, dp_size, 1)
    grad_first = grad_two + by_cols(grad_pre_low, in_all)
    grad_one = norm_backward(grad_first, normed_one, spread_one, ln1_gain)
    grad_attn = grad_one * hid_eff
    grad_attn_low = grad_attn.astype(jnp.bfloat16)
    grad_out_bias = jnp.sum(grad_attn, 0)
    grad_ln1_gain = jnp.sum(grad_first * normed_one, 0)
    grad_ln1_bias = jnp.sum(grad_first, 0)
    grad_ffn_out_bias = jnp.sum(grad_ffn, 0)
    grad_ln2_gain = jnp.sum(grad_final * normed_two, 0)
    grad_ln2_bias = jnp.sum(grad_final, 0)
    gate_terms = grad_one * attn_out + grad_two * ffn_out
    grad_hidden_gate = jnp.sum(gate_terms, 0) * hidden_mask.astype(jnp.float32)
    grad_out_weight = head_sum_rows(gated, grad_attn_low, 0, 0)
    grad_gated = by_cols(grad_attn_low, out_all).reshape(row_total, local_heads, head_width)
    grad_head_gate = jnp.sum(grad_gated * context, (0, 2)) * head_flags
    grad_context = (grad_gated * head_eff[None, :, None]).astype(jnp.bfloat16)
    grad_long, grad_short = split_sets(grad_context)
    back_long = attend_back(
        query_long, key_long, value_long, mask_long, score_scale, log_long, grad_long
    )
    back_short = attend_back(
        query_short, key_short, value_short, mask_short, score_scale, log_short, grad_short
    )
    grad_queries = join_sets(back_long[0], back_short[0])
    grad_keys = join_sets(back_long[1], back_short[1])
    grad_values = join_sets(back_long[2], back_short[2])
    grad_qv_bias = jnp.stack([jnp.sum(grad_queries, 0), jnp.sum(grad_values, 0)]).reshape(2, -1)
    grad_three = (
        jnp.stack([grad_queries, grad_keys, grad_values], 1)
        .astype(jnp.bfloat16)
        .reshape(row_total, 3, -1)
    )
    half_three = (
        grad_three[:, :, :half_width].reshape(row_total, -1),
        grad_three[:, :, half_width:].reshape(row_total, -1),
    )
    grad_qkv_weight = head_sum(by_rows(hidden, half_three[0]), by_rows(hidden, half_three[1]))
    grad_hidden = by_cols(grad_three.reshape(row_total, -1), qkv_flat) + grad_one

    whole = jnp.concatenate(
        [
            grad_out_bias,
            grad_ln1_gain,
            grad_ln1_bias,
            grad_ffn_out_bias,
            grad_ln2_gain,
            grad_ln2_bias,
            grad_hidden_gate,
        ]
    )

    def small_half(part):
        pad = width - own_heads
        return jnp.concatenate(
            [
                whole,
                grad_qv_bias.reshape(2, 2, -1)[:, part].reshape(-1),
                grad_in_bias.reshape(2, -1)[part],
                grad_ffn_gate.reshape(2, -1)[part],
                grad_head_gate.reshape(2, -1)[part],
                jnp.zeros((pad,), jnp.float32),
            ]
        )

    small = small_half(0) + other(small_half(1))
    small_rows = small.shape[0] // width
    small = jnp.pad(small.reshape(small_rows, width), ((0, -small_rows % 128), (0, 0)))
    grad_out_weight = jnp.concatenate([grad_out_weight, small], 0)
    qkv_pieces = reduce_pieces(grad_qkv_weight, dp_size, 2)
    out_pieces = reduce_pieces(grad_out_weight, dp_size, 0)
    grad_ffn_out_weight = gather_pieces(ffn_out_pieces, dp_size, 0)
    grad_in_weight = gather_pieces(in_pieces, dp_size, 1)
    grad_qkv_weight = gather_pieces(qkv_pieces, dp_size, 2).reshape(width, 3, -1)
    grad_out_weight = gather_pieces(out_pieces, dp_size, 0)
    small = grad_out_weight[half_width:].reshape(-1)
    grad_out_weight = grad_out_weight[:half_width]
    (
        grad_out_bias,
        grad_ln1_gain,
        grad_ln1_bias,
        grad_ffn_out_bias,
        grad_ln2_gain,
        grad_ln2_bias,
        grad_hidden_gate,
    ) = small[: 7 * width].reshape(7, width)
    small = small[7 * width :]
    grad_qv_bias = small[:width].reshape(2, half_width)
    grad_in_bias = small[width : width + half_units]
    grad_ffn_gate = small[width + half_units : width + 2 * half_units]
    grad_head_gate = small[width + 2 * half_units : width + 2 * half_units + own_heads]
    return (
        layer_out,
        grad_hidden,
        grad_qkv_weight,
        grad_qv_bias,
        grad_out_weight,
        grad_out_bias,
        grad_ln1_gain,
        grad_ln1_bias,
        grad_in_weight,
        grad_in_bias,
        grad_ffn_out_weight,
        grad_ffn_out_bias,
        grad_ln2_gain,
        grad_ln2_bias,
        grad_head_gate,
        grad_ffn_gate,
        grad_hidden_gate,
    )


def solution(mesh):
    placed = (
        P("dp", None),
        P("dp", None),
        P("dp", None, None),
        P("dp", None, None),
        P(None, None, "head"),
        P(None, "head"),
        P("head", None),
        P(),
        P(),
        P(),
        P(None, "head"),
        P("head"),
        P("head", None),
        P(),
        P(),
        P(),
        P("head"),
        P("head"),
        P("head"),
        P("head"),
        P(),
        P(),
    )
    return jax.shard_map(
        partial(per_device, mesh.shape["dp"]),
        mesh=mesh,
        in_specs=placed,
        out_specs=(
            P(("dp", "head"), None),
            P(("dp", "head"), None),
            P(None, None, "head"),
            P(None, "head"),
            P("head", None),
            P(),
            P(),
            P(),
            P(None, "head"),
            P("head"),
            P("head", None),
            P(),
            P(),
            P(),
            P("head"),
            P("head"),
            P(),
        ),
        check_vma=False,
    )
```

```python
from functools import partial

import jax
import jax.numpy as jnp
from jax import lax
from jax.experimental import pallas as pl
from jax.experimental.pallas import tpu as pltpu
from jax.sharding import PartitionSpec as P

BASE = 64
ROWS = 15 * BASE
EPSILON = 1e-12
MASKED = -1e9
LOG2E = 1.4426950408889634
BUCKETS = ((0, 8 * BASE), (8 * BASE, 4 * BASE), (12 * BASE, 2 * BASE), (14 * BASE, BASE))
F32 = jnp.float32
BF16 = jnp.bfloat16
MEBI = 1 << 20


def dot(left, right):
    return jnp.dot(left, right, preferred_element_type=F32)


def by_rows(left, right):
    return lax.dot_general(left, right, (((0,), (0,)), ((), ())), preferred_element_type=F32)


def by_cols(left, right):
    return lax.dot_general(left, right, (((1,), (1,)), ((), ())), preferred_element_type=F32)


def f32(*shape):
    return jax.ShapeDtypeStruct(shape, F32)


def bf16(*shape):
    return jax.ShapeDtypeStruct(shape, BF16)


def call(name, body, ins, outs, vmem, scalars=(), scratch=(), after=()):
    after = [value for value in after if value is not None]
    total = len(scalars) + len(ins)

    def run(*refs):
        body(*refs[:total], *refs[total + len(after) :])

    return pl.pallas_call(
        run,
        in_specs=[pl.BlockSpec(memory_space=pltpu.SMEM)] * len(scalars)
        + [pl.BlockSpec(memory_space=pltpu.VMEM)] * len(ins)
        + [pl.BlockSpec(memory_space=pl.ANY)] * len(after),
        out_specs=[pl.BlockSpec(memory_space=pltpu.VMEM)] * len(outs),
        out_shape=list(outs),
        scratch_shapes=list(scratch),
        compiler_params=pltpu.CompilerParams(vmem_limit_bytes=vmem * MEBI),
        cost_estimate=pl.CostEstimate(flops=1000000, bytes_accessed=10000, transcendentals=0),
        name=name,
    )(*scalars, *ins, *after)


def row_of(vectors, at):
    return vectors[at : at + 1, :]


def column_sum(values):
    return jnp.sum(values, 0, keepdims=True)


PACK_IN_BIAS, PACK_FFN, PACK_QV, PACK_HEAD = range(4)


def side_masks(lanes):
    low = lax.broadcasted_iota(jnp.int32, (1, lanes), 1) < lanes // 2
    return low, low.astype(BF16), 1 - low.astype(BF16)


def attend_body(pairs, lanes, meta, hidden, weight, pack, qkv, gated, logs, columns):
    half = pairs * lanes
    for part in range(3):
        cols = slice(part * half, (part + 1) * half)
        mixed = dot(hidden[...], weight[:, cols])
        if part != 1:
            mixed += pack[PACK_QV : PACK_QV + 1, part // 2 * half : (part // 2 + 1) * half]
        qkv[:, cols] = mixed.astype(BF16)
    scale = LOG2E * (lanes // 2) ** -0.5
    low_side, *masks = side_masks(lanes)
    lane = lax.broadcasted_iota(jnp.int32, (1, 128), 1)

    def per_pair(pair, carry):
        at = pl.multiple_of(pair * lanes, lanes)
        for place, (start, size) in enumerate(BUCKETS):
            rows = slice(start, start + size)
            seen = lax.broadcasted_iota(jnp.int32, (1, size), 1) < meta[place]
            shut = jnp.where(seen, 0.0, MASKED).astype(F32)
            queries = qkv[rows, pl.ds(at, lanes)]
            keys = qkv[rows, pl.ds(half + at, lanes)]
            values = qkv[rows, pl.ds(2 * half + at, lanes)]
            found = []
            column = columns[rows, :]
            for side, mask in enumerate(masks):
                scores = by_cols(queries * mask, keys) + shut
                top = jnp.max(scores, -1, keepdims=True)
                power = jnp.exp2((scores - top) * scale)
                total = jnp.sum(power, -1, keepdims=True)
                found.append(dot(power.astype(BF16), values) * (1.0 / total))
                column = jnp.where(
                    lane == 2 * pair + side, top * scale + jnp.log2(total), column
                )
            columns[rows, :] = column
            context = jnp.where(low_side, found[0], found[1])
            gated[rows, pl.ds(at, lanes)] = (
                context * pack[PACK_HEAD : PACK_HEAD + 1, pl.ds(at, lanes)]
            ).astype(BF16)
        return carry

    lax.fori_loop(0, pairs, per_pair, 0)
    for start, size in BUCKETS:
        rows = slice(start, start + size)
        logs[:, rows] = columns[rows, :].T[0:8, :]


def attend(meta, hidden, weight, pack, head_width, after=()):
    half = weight.shape[1] // 3
    pairs = half // (2 * head_width)
    return call(
        "attend",
        partial(attend_body, pairs, 2 * head_width),
        [hidden, weight, pack],
        [bf16(ROWS, 3 * half), bf16(ROWS, half), f32(8, ROWS)],
        24,
        scalars=[meta],
        scratch=[pltpu.VMEM((ROWS, 128), F32)],
        after=after,
    )


def pick_row(values, at):
    place = lax.broadcasted_iota(jnp.int32, values.shape, 0)
    return column_sum(jnp.where(place == at, values, 0.0))


def attend_back_body(pairs, lanes, meta, qkv, grad_context, logs, means, mixed, bias_sums):
    half = pairs * lanes
    scale = LOG2E * (lanes // 2) ** -0.5
    final = (lanes // 2) ** -0.5
    low_side, *masks = side_masks(lanes)

    def per_pair(pair, carry):
        at = pl.multiple_of(pair * lanes, lanes)
        query_sum = jnp.zeros((1, lanes), F32)
        value_sum = jnp.zeros((1, lanes), F32)
        for place, (start, size) in enumerate(BUCKETS):
            rows = slice(start, start + size)
            seen = lax.broadcasted_iota(jnp.int32, (size, 1), 0) < meta[place]
            shut = jnp.where(seen, 0.0, MASKED).astype(F32)
            queries = qkv[rows, pl.ds(at, lanes)]
            keys = qkv[rows, pl.ds(half + at, lanes)]
            values = qkv[rows, pl.ds(2 * half + at, lanes)]
            grads = grad_context[rows, pl.ds(at, lanes)]
            grad_query = grad_key = grad_value = None
            for side, mask in enumerate(masks):
                log = pick_row(logs[:, rows], 2 * pair + side)
                mean = pick_row(means[:, rows], 2 * pair + side)
                side_queries = queries * mask
                side_grads = grads * mask
                scores = by_cols(keys, side_queries) + shut
                weights = jnp.exp2(scores * scale - log)
                change = (weights * (by_cols(values, side_grads) - mean)).astype(BF16)
                part_value = dot(weights.astype(BF16), side_grads)
                part_key = dot(change, side_queries)
                part_query = by_rows(change, keys * mask)
                if side == 0:
                    grad_query, grad_key, grad_value = part_query, part_key, part_value
                else:
                    grad_query += part_query
                    grad_key += part_key
                    grad_value += part_value
            grad_query *= final
            query_sum += column_sum(grad_query)
            value_sum += column_sum(grad_value)
            mixed[rows, pl.ds(at, lanes)] = grad_query.astype(BF16)
            mixed[rows, pl.ds(half + at, lanes)] = (grad_key * final).astype(BF16)
            mixed[rows, pl.ds(2 * half + at, lanes)] = grad_value.astype(BF16)
        bias_sums[0:1, pl.ds(at, lanes)] = query_sum
        bias_sums[1:2, pl.ds(at, lanes)] = value_sum
        return carry

    bias_sums[...] = jnp.zeros_like(bias_sums)
    lax.fori_loop(0, pairs, per_pair, 0)


def attend_back(meta, qkv, grad_context, logs, means, head_width, after=()):
    half = grad_context.shape[1]
    pairs = half // (2 * head_width)
    return call(
        "attend_back",
        partial(attend_back_body, pairs, 2 * head_width),
        [qkv, grad_context, logs, means],
        [bf16(ROWS, 3 * half), f32(8, half)],
        24,
        scalars=[meta],
        after=after,
    )


(OUT_BIAS, LN1_GAIN, LN1_BIAS, FFN_OUT_BIAS, LN2_GAIN, LN2_BIAS, HID_EFF) = range(7)


def valid_column(meta):
    at = lax.broadcasted_iota(jnp.int32, (ROWS, 1), 0)
    found = jnp.zeros((ROWS, 1), F32)
    for place, (start, size) in enumerate(BUCKETS):
        found = jnp.where((at >= start) & (at < start + meta[place]), 1.0, found)
    return found


def norm_stats(resid):
    centred = resid - jnp.mean(resid, -1, keepdims=True)
    spread = lax.rsqrt(jnp.mean(centred * centred, -1, keepdims=True) + EPSILON)
    return (centred * spread, spread)


def norm_back(grad_out, normed, spread, gain):
    grad_normed = grad_out * gain
    first_mean = jnp.mean(grad_normed, -1, keepdims=True)
    second_mean = jnp.mean(grad_normed * normed, -1, keepdims=True)
    return spread * (grad_normed - first_mean - normed * second_mean)


def blocks_of(step):
    return [slice(at, at + step) for at in range(0, ROWS, step)]


def join_body(
    hidden, gated_own, gated_other, out_own, out_other, vectors, first, first_low, normed_one, spread_one, attn_out
):
    for block in blocks_of(240):
        attn = (
            dot(gated_own[block, :], out_own[...])
            + dot(gated_other[block, :], out_other[...])
            + row_of(vectors, OUT_BIAS)
        )
        attn_out[block, :] = attn.astype(BF16)
        normed, spread = norm_stats(
            hidden[block, :].astype(F32) + attn * row_of(vectors, HID_EFF)
        )
        normed_one[block, :] = normed.astype(BF16)
        spread_one[block, :] = jnp.broadcast_to(spread, (240, 128))
        value = normed * row_of(vectors, LN1_GAIN) + row_of(vectors, LN1_BIAS)
        first[block, :] = value
        first_low[block, :] = value.astype(BF16)


def join_heads(hidden, gated, out_weight, vectors, after=()):
    width = hidden.shape[1]
    low = bf16(ROWS, width)
    return call(
        "join_heads",
        join_body,
        [hidden, *gated, *out_weight, vectors],
        [f32(ROWS, width), low, low, f32(ROWS, 128), low],
        20,
        after=after,
    )


def turn_body(meta, first, ffn_total, cotangent, vectors, layer_out, grad_low, grad_two, sums):
    gain = row_of(vectors, LN2_GAIN)
    valid = valid_column(meta)
    hid_eff = row_of(vectors, HID_EFF)
    totals = [jnp.zeros((1, first.shape[1]), F32)] * 4
    for block in blocks_of(120):
        ffn_out = ffn_total[block, :] + row_of(vectors, FFN_OUT_BIAS)
        normed, spread = norm_stats(first[block, :] + ffn_out * hid_eff)
        layer_out[block, :] = (
            (normed * gain + row_of(vectors, LN2_BIAS)) * valid[block]
        ).astype(BF16)
        grad_final = cotangent[block, :].astype(F32) * valid[block]
        grad = norm_back(grad_final, normed, spread, gain)
        grad_ffn = grad * hid_eff
        grad_two[block, :] = grad
        grad_low[block, :] = grad_ffn.astype(BF16)
        terms = (grad_ffn, grad_final * normed, grad_final, grad * ffn_out)
        totals = [total + column_sum(term) for total, term in zip(totals, terms, strict=True)]
    sums[...] = jnp.zeros_like(sums)
    for place, total in enumerate(totals):
        sums[place : place + 1, :] = total


def turn(meta, first, ffn_total, cotangent, vectors, after=()):
    width = first.shape[1]
    low = bf16(ROWS, width)
    return call(
        "turn",
        turn_body,
        [first, ffn_total, cotangent, vectors],
        [low, low, f32(ROWS, width), f32(8, width)],
        20,
        scalars=[meta],
        after=after,
    )


def part_body(
    head_width,
    grad_first,
    normed_one,
    spread_one,
    attn_out,
    vectors,
    gated_own,
    gated_other,
    out_own,
    out_other,
    pack_own,
    pack_other,
    grad_one,
    context_own,
    context_other,
    means_own,
    means_other,
    weight_mine,
    weight_other,
    sums,
    head_sums_own,
    head_sums_other,
    low,
):
    gain = row_of(vectors, LN1_GAIN)
    hid_eff = row_of(vectors, HID_EFF)
    totals = [jnp.zeros((1, grad_first.shape[1]), F32)] * 4
    for block in blocks_of(120):
        grad = grad_first[block, :]
        normed = normed_one[block, :].astype(F32)
        one = norm_back(grad, normed, spread_one[block, 0:1], gain)
        grad_one[block, :] = one
        attn = one * hid_eff
        low[block, :] = attn.astype(BF16)
        terms = (attn, grad * normed, grad, one * attn_out[block, :].astype(F32))
        totals = [total + column_sum(term) for total, term in zip(totals, terms, strict=True)]
    sums[...] = jnp.zeros_like(sums)
    for place, total in enumerate(totals):
        sums[place : place + 1, :] = total
    weight_other[...] = by_rows(gated_other[...], low[...]).astype(BF16)
    weight_mine[...] = by_rows(gated_own[...], low[...]).astype(BF16)
    half = gated_own.shape[1]
    lane = lax.broadcasted_iota(jnp.int32, (1, 128), 1)
    for gated, weight, pack, context, means, head_sums in (
        (gated_own, out_own, pack_own, context_own, means_own, head_sums_own),
        (gated_other, out_other, pack_other, context_other, means_other, head_sums_other),
    ):
        head_sums[...] = jnp.zeros_like(head_sums)
        for start, size in BUCKETS:
            rows = slice(start, start + size)
            grads = by_cols(low[rows, :], weight[...])
            context[rows, :] = (
                grads * pack[PACK_HEAD : PACK_HEAD + 1, 0:half]
            ).astype(BF16)
            terms = grads * gated[rows, :].astype(F32)
            head_sums[0:1, :] += column_sum(terms)
            columns = jnp.zeros((size, 128), F32)
            for head in range(half // head_width):
                total = jnp.sum(
                    terms[:, head * head_width : (head + 1) * head_width], -1, keepdims=True
                )
                columns = jnp.where(lane == head, total, columns)
            means[:, rows] = columns.T[0:8, :]


def part_heads(
    grad_first, normed_one, spread_one, attn_out, vectors, gated, out_weight, packs, head_width, after=()
):
    width = grad_first.shape[1]
    half = gated[0].shape[1]
    return call(
        "part_heads",
        partial(part_body, head_width),
        [grad_first, normed_one, spread_one, attn_out, vectors, *gated, *out_weight, *packs],
        [
            f32(ROWS, width),
            bf16(ROWS, half),
            bf16(ROWS, half),
            f32(8, ROWS),
            f32(8, ROWS),
            bf16(half, width),
            bf16(half, width),
            f32(8, width),
            f32(8, half),
            f32(8, half),
        ],
        26,
        scratch=[pltpu.VMEM((ROWS, width), BF16)],
        after=after,
    )


def gelu_and_slope(z):
    below = 0.5 + 0.5 * lax.erf(z * 0.5**0.5)
    density = jnp.exp2((-0.5 * LOG2E) * (z * z)) * (0.5 / 3.141592653589793) ** 0.5
    return (z * below, below + z * density)


def expand_body(chunk, row_step, started, first_low, weight_in, weight_out, pack, *rest):
    before = rest[0] if started else None
    inner, slope, total = rest[1:] if started else rest
    units = weight_in.shape[1]

    def per_chunk(place, carry):
        cols = pl.ds(pl.multiple_of(place * chunk, chunk), chunk)
        bias = pack[PACK_IN_BIAS : PACK_IN_BIAS + 1, cols]
        eff = pack[PACK_FFN : PACK_FFN + 1, cols]
        for block in blocks_of(row_step):
            pre = dot(first_low[block, :], weight_in[:, cols]) + bias
            value, steep = gelu_and_slope(pre)
            low = (value * eff).astype(BF16)
            inner[block, cols] = low
            slope[block, cols] = (steep * eff).astype(BF16)
            total[block, :] += dot(low, weight_out[cols, :])
        return carry

    if started:
        total[...] = before[...]
    else:
        total[...] = jnp.zeros_like(total)
    lax.fori_loop(0, units // chunk, per_chunk, 0)


def expand(first_low, weight_in, weight_out, pack, before=None, after=(), chunk=512, row_step=480):
    width, units = weight_in.shape
    started = before is not None
    return call(
        "expand",
        partial(expand_body, chunk, row_step, started),
        [first_low, weight_in, weight_out, pack] + ([before] if started else []),
        [bf16(ROWS, units), bf16(ROWS, units), f32(ROWS, width)],
        24,
        after=after,
    )


def outer_body(chunk, left, right, out):
    def per_chunk(place, carry):
        cols = pl.ds(pl.multiple_of(place * chunk, chunk), chunk)
        out[cols, :] = by_rows(left[:, cols], right[...]).astype(BF16)
        return carry

    lax.fori_loop(0, left.shape[1] // chunk, per_chunk, 0)


def outer(left, right, after=(), chunk=512):
    return call(
        "outer",
        partial(outer_body, chunk),
        [left, right],
        [bf16(left.shape[1], right.shape[1])],
        16,
        after=after,
    )[0]


def shrink_body(
    chunk,
    row_step,
    grad_low,
    first_low,
    inner,
    slope,
    weight_in,
    weight_out,
    before,
    weight_grad,
    grad_first,
    unit_sums,
    kept,
):
    units = weight_in.shape[1]

    def per_chunk(place, carry):
        cols = pl.ds(pl.multiple_of(place * chunk, chunk), chunk)
        bias_sum = jnp.zeros((1, chunk), F32)
        gate_sum = jnp.zeros((1, chunk), F32)
        for block in blocks_of(row_step):
            grad_inner = by_cols(grad_low[block, :], weight_out[cols, :])
            grad_pre = grad_inner * slope[block, cols].astype(F32)
            bias_sum += column_sum(grad_pre)
            gate_sum += column_sum(inner[block, cols].astype(F32) * grad_inner)
            low = grad_pre.astype(BF16)
            kept[block, :] = low
            grad_first[block, :] += by_cols(low, weight_in[:, cols])
        weight_grad[:, cols] = by_rows(first_low[...], kept[...]).astype(BF16)
        unit_sums[0:1, cols] = bias_sum
        unit_sums[1:2, cols] = gate_sum
        return carry

    unit_sums[...] = jnp.zeros_like(unit_sums)
    grad_first[...] = before[...]
    lax.fori_loop(0, units // chunk, per_chunk, 0)


def shrink(grad_low, first_low, inner, slope, weight_in, weight_out, before, after=(), chunk=512, row_step=960):
    width, units = weight_in.shape
    return call(
        "shrink",
        partial(shrink_body, chunk, row_step),
        [grad_low, first_low, inner, slope, weight_in, weight_out, before],
        [bf16(width, units), f32(ROWS, width), f32(8, units)],
        28,
        scratch=[pltpu.VMEM((ROWS, chunk), BF16)],
        after=after,
    )


def swap_bit(values, dp_size, bit):
    return lax.ppermute(values, "dp", [(at, at ^ (1 << bit)) for at in range(dp_size)])


class Stream:
    def __init__(self, values, dp_size, turn):
        bits = dp_size.bit_length() - 1
        self.dp_size = dp_size
        self.order = [(place + turn) % bits for place in range(bits)]
        self.reduced = 0
        self.gathered = 0
        self.values = values

    def side(self, bit):
        return (lax.axis_index("dp") >> bit) & 1

    def reduce(self, steps=1):
        for _ in range(steps):
            if self.reduced == len(self.order):
                return self
            bit = self.order[self.reduced]
            self.reduced += 1
            side = self.side(bit)
            half = self.values.shape[0] // 2
            kept = lax.dynamic_slice_in_dim(self.values, side * half, half, 0)
            sent = lax.dynamic_slice_in_dim(self.values, (1 - side) * half, half, 0)
            arrived = swap_bit(sent, self.dp_size, bit)
            total = kept.astype(F32) + arrived.astype(F32)
            self.values = total.astype(self.values.dtype)
        return self

    def gather(self, steps=1):
        self.reduce(len(self.order))
        for _ in range(steps):
            if self.gathered == len(self.order):
                return self
            self.gathered += 1
            bit = self.order[-self.gathered]
            first = self.side(bit) == 0
            arrived = swap_bit(self.values, self.dp_size, bit)
            self.values = jnp.concatenate(
                [jnp.where(first, self.values, arrived), jnp.where(first, arrived, self.values)], 0
            )
        return self

    def done(self):
        return self.gather(len(self.order)).values.astype(F32)


def streams_of(values, dp_size, cuts):
    found, at = [], 0
    for turn, share in cuts:
        rows = values.shape[0] * share // 12
        found.append(Stream(lax.slice_in_dim(values, at, at + rows, axis=0), dp_size, turn))
        at += rows
    return found


def joined(streams):
    return jnp.concatenate([stream.done() for stream in streams], 0)


def per_device(
    dp_size,
    hidden,
    cotangent,
    counts,
    lengths,
    qkv_weight,
    qv_bias,
    out_weight,
    out_bias,
    ln1_gain,
    ln1_bias,
    in_weight,
    in_bias,
    ffn_out_weight,
    ffn_out_bias,
    ln2_gain,
    ln2_bias,
    head_gate,
    head_mask,
    ffn_gate,
    ffn_mask,
    hidden_gate,
    hidden_mask,
):
    width = hidden.shape[1]
    own_heads = head_gate.shape[0]
    half = qkv_weight.shape[2]
    units = in_weight.shape[1]
    head_width = half // own_heads
    head_at = lax.axis_index("head")

    def other(values):
        return lax.ppermute(values, "head", [(0, 1), (1, 0)])

    def own_rows(values):
        return lax.dynamic_slice_in_dim(values, head_at * ROWS, ROWS, 0)

    def pad_to(values, size):
        return jnp.pad(values, (0, size - values.shape[0]))

    hidden = own_rows(hidden)
    cotangent = own_rows(cotangent)
    meta = lax.dynamic_index_in_dim(
        jnp.where(counts[0] > 0, lengths[0], 0), head_at, 0, keepdims=False
    )
    head_flags = head_mask.astype(F32)
    ffn_flags = ffn_mask.astype(F32)
    hidden_flags = hidden_mask.astype(F32)
    pack = jnp.stack(
        [
            in_bias,
            ffn_gate * ffn_flags,
            pad_to(qv_bias.reshape(-1), units),
            pad_to(jnp.repeat(head_gate * head_flags, head_width), units),
        ]
    )
    vectors = jnp.stack(
        [
            out_bias,
            ln1_gain,
            ln1_bias,
            ffn_out_bias,
            ln2_gain,
            ln2_bias,
            hidden_gate * hidden_flags,
        ]
    )
    qkv_own = qkv_weight.reshape(width, -1)
    qkv_other = other(qkv_own)
    packs = (pack, other(pack))
    outs = (out_weight, other(out_weight))
    ins = (in_weight, other(in_weight))
    ffns = (ffn_out_weight, other(ffn_out_weight))

    qkv0, gated0, logs0 = attend(meta, hidden, qkv_own, packs[0], head_width)
    qkv1, gated1, logs1 = attend(meta, hidden, qkv_other, packs[1], head_width, [qkv0])
    gated = (gated0, gated1)
    first, first_low, normed_one, spread_one, attn_out = join_heads(hidden, gated, outs, vectors)
    inner0, slope0, total = expand(first_low, ins[0], ffns[0], packs[0])
    inner1, slope1, total = expand(first_low, ins[1], ffns[1], packs[1], total)
    layer_out, grad_low, grad_two, turn_sums = turn(meta, first, total, cotangent, vectors)

    def added(mine, theirs):
        return (mine.astype(F32) + theirs.astype(F32)).astype(BF16)

    cuts = ((0, 6), (1, 4), (2, 2))
    theirs = other(outer(inner1, grad_low))
    mine = outer(inner0, grad_low)
    ffn_out_grad = added(mine, theirs)
    ffn_streams = streams_of(ffn_out_grad, dp_size, cuts)

    def values_of(streams):
        return [stream.values for stream in streams]

    in_grad_other, grad_first, unit_sums1 = shrink(
        grad_low, first_low, inner1, slope1, ins[1], ffns[1], grad_two, [ffn_out_grad]
    )
    theirs = other(in_grad_other)
    for stream in ffn_streams[1:]:
        stream.reduce()
    in_grad_mine, grad_first, unit_sums0 = shrink(
        grad_low,
        first_low,
        inner0,
        slope0,
        ins[0],
        ffns[0],
        grad_first,
        values_of(ffn_streams[1:]),
    )
    in_grad = added(in_grad_mine, theirs)
    in_streams = streams_of(in_grad, dp_size, cuts)
    for stream in ffn_streams:
        stream.reduce()
    (
        grad_one,
        grad_context0,
        grad_context1,
        means0,
        means1,
        out_grad_mine,
        out_grad_other,
        part_sums,
        head_sums0,
        head_sums1,
    ) = part_heads(
        grad_first,
        normed_one,
        spread_one,
        attn_out,
        vectors,
        gated,
        outs,
        packs,
        head_width,
        [in_grad] + values_of(ffn_streams),
    )
    for stream in ffn_streams + in_streams[1:]:
        stream.reduce()
    mixed1, bias_sums1 = attend_back(
        meta,
        qkv1,
        grad_context1,
        logs1,
        means1,
        head_width,
        values_of(ffn_streams + in_streams[1:]),
    )
    for stream in ffn_streams + in_streams:
        stream.reduce()
    mixed0, bias_sums0 = attend_back(
        meta,
        qkv0,
        grad_context0,
        logs0,
        means0,
        head_width,
        values_of(ffn_streams + in_streams) + [mixed1],
    )
    theirs = other(by_rows(hidden, mixed1).astype(BF16))
    qkv_grad = added(by_rows(hidden, mixed0), theirs)

    def small_of(bias_sums, head_sums, unit_sums):
        return jnp.concatenate(
            [
                part_sums[:4],
                turn_sums[:4],
                bias_sums[:2].reshape(1, -1),
                jnp.pad(head_sums[:1], ((0, 0), (0, half))),
                unit_sums[:2].reshape(-1, width),
            ],
            0,
        )

    small = small_of(bias_sums0, head_sums0, unit_sums0) + other(
        small_of(bias_sums1, head_sums1, unit_sums1)
    )
    small_shape = small.shape
    small = small.reshape(-1)
    small = jnp.pad(small, (0, -small.shape[0] % (128 * 128))).reshape(128, -1)
    small_stream = Stream(small, dp_size, 0)
    out_grad = added(out_grad_mine, other(out_grad_other))
    qkv_streams = streams_of(qkv_grad, dp_size, cuts)
    out_stream = Stream(out_grad, dp_size, 2)
    grad_hidden = grad_one + by_cols(mixed0, qkv_own) + by_cols(mixed1, qkv_other)
    grad_ffn_out_weight = joined(ffn_streams)
    grad_in_weight = joined(in_streams)
    grad_qkv_weight = joined(qkv_streams).reshape(width, 3, half)
    grad_out_weight = out_stream.done()
    small = small_stream.done().reshape(-1)[: small_shape[0] * width].reshape(small_shape)
    (
        grad_out_bias,
        grad_ln1_gain,
        grad_ln1_bias,
        gate_one,
        grad_ffn_out_bias,
        grad_ln2_gain,
        grad_ln2_bias,
        gate_two,
    ) = small[:8]
    unit_rows = units // width
    return (
        layer_out,
        grad_hidden,
        grad_qkv_weight,
        small[8].reshape(2, half),
        grad_out_weight,
        grad_out_bias,
        grad_ln1_gain,
        grad_ln1_bias,
        grad_in_weight,
        small[10 : 10 + unit_rows].reshape(-1),
        grad_ffn_out_weight,
        grad_ffn_out_bias,
        grad_ln2_gain,
        grad_ln2_bias,
        jnp.sum(small[9, :half].reshape(own_heads, head_width), 1) * head_flags / head_gate,
        small[10 + unit_rows : 10 + 2 * unit_rows].reshape(-1) * ffn_flags / ffn_gate,
        (gate_one + gate_two) * hidden_flags,
    )


def solution(mesh):
    placed = (
        P("dp", None),
        P("dp", None),
        P("dp", None, None),
        P("dp", None, None),
        P(None, None, "head"),
        P(None, "head"),
        P("head", None),
        P(),
        P(),
        P(),
        P(None, "head"),
        P("head"),
        P("head", None),
        P(),
        P(),
        P(),
        P("head"),
        P("head"),
        P("head"),
        P("head"),
        P(),
        P(),
    )
    return jax.shard_map(
        partial(per_device, mesh.shape["dp"]),
        mesh=mesh,
        in_specs=placed,
        out_specs=(
            P(("dp", "head"), None),
            P(("dp", "head"), None),
            P(None, None, "head"),
            P(None, "head"),
            P("head", None),
            P(),
            P(),
            P(),
            P(None, "head"),
            P("head"),
            P("head", None),
            P(),
            P(),
            P(),
            P("head"),
            P("head"),
            P(),
        ),
        check_vma=False,
    )
```

```python
from functools import partial

import jax
import jax.numpy as jnp
from jax import lax
from jax.experimental import pallas as pl
from jax.experimental.pallas import tpu as pltpu
from jax.sharding import PartitionSpec as P

BASE = 64
ROWS = 15 * BASE
EPSILON = 1e-12
MASKED = -1e9
LOG2E = 1.4426950408889634
BUCKETS = ((0, 8 * BASE), (8 * BASE, 4 * BASE), (12 * BASE, 2 * BASE), (14 * BASE, BASE))
F32 = jnp.float32
BF16 = jnp.bfloat16
MEBI = 1 << 20
HBM = pl.BlockSpec(memory_space=pl.ANY)


def dot(left, right):
    return jnp.dot(left, right, preferred_element_type=F32)


def by_rows(left, right):
    return lax.dot_general(left, right, (((0,), (0,)), ((), ())), preferred_element_type=F32)


def by_cols(left, right):
    return lax.dot_general(left, right, (((1,), (1,)), ((), ())), preferred_element_type=F32)


def f32(*shape):
    return jax.ShapeDtypeStruct(shape, F32)


def bf16(*shape):
    return jax.ShapeDtypeStruct(shape, BF16)


def whole(*shape):
    return pl.BlockSpec(shape, lambda *_: (0,) * len(shape))


def call(name, body, grid, micros, scalars, ins, outs, scratch=(), after=(), vmem=58):
    first = len(scalars) + len(ins)

    def run(*refs):
        body(*refs[:first], *refs[first + len(after) :])

    return pl.pallas_call(
        run,
        grid_spec=pltpu.PrefetchScalarGridSpec(
            num_scalar_prefetch=len(scalars),
            grid=grid,
            in_specs=[spec for _, spec in ins] + [HBM] * len(after),
            out_specs=[spec for _, spec in outs],
            scratch_shapes=list(scratch),
        ),
        out_shape=[shape for shape, _ in outs],
        compiler_params=pltpu.CompilerParams(
            dimension_semantics=("arbitrary",) * len(grid), vmem_limit_bytes=vmem * MEBI
        ),
        cost_estimate=pl.CostEstimate(
            flops=int(micros * 5e9), bytes_accessed=1 << 20, transcendentals=0
        ),
        name=name,
    )(*scalars, *[value for value, _ in ins], *after)


def row_of(vectors, at):
    return vectors[at : at + 1, :]


def column_sum(values):
    return jnp.sum(values, 0, keepdims=True)


def own_rows(width):
    return pl.BlockSpec((ROWS, width), lambda i, meta: (meta[4], 0))


PACK_IN_BIAS, PACK_FFN, PACK_QV, PACK_HEAD = range(4)


def side_masks(lanes):
    low = lax.broadcasted_iota(jnp.int32, (1, lanes), 1) < lanes // 2
    return low, low.astype(BF16), 1 - low.astype(BF16)


def attend_body(
    pairs, lanes, meta, hidden, weight_q, weight_k, weight_v, bias_q, bias_v, gate, query, key, value, gated, logs, columns
):
    pair = pl.program_id(0)
    weight = jnp.concatenate([weight_q[...], weight_k[...], weight_v[...]], 1)
    mixed = dot(hidden[...], weight)
    query[...] = (mixed[:, :lanes] + bias_q[PACK_QV : PACK_QV + 1, :]).astype(BF16)
    key[...] = mixed[:, lanes : 2 * lanes].astype(BF16)
    value[...] = (mixed[:, 2 * lanes :] + bias_v[PACK_QV : PACK_QV + 1, :]).astype(BF16)
    scale = LOG2E * (lanes // 2) ** -0.5
    low_side, *masks = side_masks(lanes)
    lane = lax.broadcasted_iota(jnp.int32, (1, 128), 1)
    for place, (start, size) in enumerate(BUCKETS):
        rows = slice(start, start + size)
        seen = lax.broadcasted_iota(jnp.int32, (1, size), 1) < meta[place]
        shut = jnp.where(seen, 0.0, MASKED).astype(F32)
        queries, keys, values = query[rows, :], key[rows, :], value[rows, :]
        found = []
        column = columns[rows, :]
        for side, mask in enumerate(masks):
            scores = by_cols(queries * mask, keys) + shut
            top = jnp.max(scores, -1, keepdims=True)
            power = jnp.exp2((scores - top) * scale)
            total = jnp.sum(power, -1, keepdims=True)
            found.append(dot(power.astype(BF16), values) * (1.0 / total))
            column = jnp.where(lane == 2 * pair + side, top * scale + jnp.log2(total), column)
        columns[rows, :] = column
        context = jnp.where(low_side, found[0], found[1])
        gated[rows, :] = (context * gate[PACK_HEAD : PACK_HEAD + 1, :]).astype(BF16)

    @pl.when(pair == pairs - 1)
    def _():
        for start, size in BUCKETS:
            rows = slice(start, start + size)
            logs[:, rows] = columns[rows, :].T[0:8, :]


def attend(meta, hidden, weights, pack, head_width, after=()):
    width, half = weights[0].shape
    lanes = 2 * head_width
    pairs = half // lanes
    column = pl.BlockSpec((ROWS, lanes), lambda i, meta: (0, i))
    weight = pl.BlockSpec((width, lanes), lambda i, meta: (0, i))

    def vector(shift):
        return pl.BlockSpec((pack.shape[0], lanes), lambda i, meta: (0, i + shift))

    return call(
        "attend",
        partial(attend_body, pairs, lanes),
        (pairs,),
        9,
        [meta],
        [(hidden, own_rows(width))]
        + [(part, weight) for part in weights]
        + [(pack, vector(0)), (pack, vector(pairs)), (pack, vector(0))],
        [(bf16(ROWS, half), column)] * 4 + [(f32(8, ROWS), whole(8, ROWS))],
        scratch=[pltpu.VMEM((ROWS, 128), F32)],
        after=after,
    )


def pick_row(values, at):
    place = lax.broadcasted_iota(jnp.int32, values.shape, 0)
    return column_sum(jnp.where(place == at, values, 0.0))


def attend_back_body(
    lanes, meta, hidden, query, key, value, grad_context, logs, means, grad_q, grad_k, grad_v, weight_grad, bias_sums
):
    pair = pl.program_id(0)
    scale = LOG2E * (lanes // 2) ** -0.5
    final = (lanes // 2) ** -0.5
    _, *masks = side_masks(lanes)
    query_sum = jnp.zeros((1, lanes), F32)
    value_sum = jnp.zeros((1, lanes), F32)
    for place, (start, size) in enumerate(BUCKETS):
        rows = slice(start, start + size)
        seen = lax.broadcasted_iota(jnp.int32, (size, 1), 0) < meta[place]
        shut = jnp.where(seen, 0.0, MASKED).astype(F32)
        queries, keys, values = query[rows, :], key[rows, :], value[rows, :]
        grads = grad_context[rows, :]
        grad_query = grad_key = grad_value = 0.0
        for side, mask in enumerate(masks):
            log = pick_row(logs[:, rows], 2 * pair + side)
            mean = pick_row(means[:, rows], 2 * pair + side)
            side_queries = queries * mask
            side_grads = grads * mask
            scores = by_cols(keys, side_queries) + shut
            weights = jnp.exp2(scores * scale - log)
            change = (weights * (by_cols(values, side_grads) - mean)).astype(BF16)
            grad_value += dot(weights.astype(BF16), side_grads)
            grad_key += dot(change, side_queries)
            grad_query += by_rows(change, keys * mask)
        grad_query *= final
        query_sum += column_sum(grad_query)
        value_sum += column_sum(grad_value)
        grad_q[rows, :] = grad_query.astype(BF16)
        grad_k[rows, :] = (grad_key * final).astype(BF16)
        grad_v[rows, :] = grad_value.astype(BF16)
    grads = jnp.concatenate([grad_q[...], grad_k[...], grad_v[...]], 1)
    weight_grad[...] = by_rows(hidden[...], grads).astype(BF16)
    bias_sums[...] = jnp.zeros_like(bias_sums)
    bias_sums[0:1, :] = query_sum
    bias_sums[1:2, :] = value_sum


def attend_back(meta, hidden, parts, grad_context, logs, means, head_width, after=()):
    half = grad_context.shape[1]
    width = hidden.shape[1]
    lanes = 2 * head_width
    pairs = half // lanes
    column = pl.BlockSpec((ROWS, lanes), lambda i, meta: (0, i))
    return call(
        "attend_back",
        partial(attend_back_body, lanes),
        (pairs,),
        11,
        [meta],
        [(hidden, own_rows(width))]
        + [(part, column) for part in (*parts, grad_context)]
        + [(logs, whole(8, ROWS)), (means, whole(8, ROWS))],
        [(bf16(ROWS, half), column)] * 3
        + [
            (
                bf16(width, 3 * half),
                pl.BlockSpec((width, 3 * lanes), lambda i, meta: (0, i)),
            ),
            (f32(8, half), pl.BlockSpec((8, lanes), lambda i, meta: (0, i))),
        ],
        after=after,
    )


(OUT_BIAS, LN1_GAIN, LN1_BIAS, FFN_OUT_BIAS, LN2_GAIN, LN2_BIAS, HID_EFF) = range(7)


def valid_column(meta):
    at = lax.broadcasted_iota(jnp.int32, (ROWS, 1), 0)
    found = jnp.zeros((ROWS, 1), F32)
    for place, (start, size) in enumerate(BUCKETS):
        found = jnp.where((at >= start) & (at < start + meta[place]), 1.0, found)
    return found


def norm_stats(resid):
    centred = resid - jnp.mean(resid, -1, keepdims=True)
    spread = lax.rsqrt(jnp.mean(centred * centred, -1, keepdims=True) + EPSILON)
    return (centred * spread, spread)


def norm_back(grad_out, normed, spread, gain):
    grad_normed = grad_out * gain
    first_mean = jnp.mean(grad_normed, -1, keepdims=True)
    second_mean = jnp.mean(grad_normed * normed, -1, keepdims=True)
    return spread * (grad_normed - first_mean - normed * second_mean)


def blocks_of(step):
    return [slice(at, at + step) for at in range(0, ROWS, step)]


def gelu_and_slope(z):
    below = 0.5 + 0.5 * lax.erf(z * 0.5**0.5)
    density = jnp.exp2((-0.5 * LOG2E) * (z * z)) * (0.5 / 3.141592653589793) ** 0.5
    return (z * below, below + z * density)


def ffn_body(
    chunks,
    row_step,
    meta,
    hidden,
    cotangent_all,
    gated_own,
    gated_other,
    out_own,
    out_other,
    vectors,
    pack_own,
    pack_other,
    in_own,
    in_other,
    ffn_own,
    ffn_other,
    layer_out_hbm,
    first_low_hbm,
    normed_hbm,
    attn_hbm,
    grad_low_hbm,
    grad_two_hbm,
    spread_one,
    inner_out,
    slope_out,
    weight_other,
    sums,
    first,
    total,
    inner,
    cotangent,
    layer_out,
    first_low,
    normed_one,
    attn_out,
    grad_low,
    grad_two,
    done,
):
    step = pl.program_id(0)
    cols = inner_out.shape[1]
    early = ((first_low, first_low_hbm), (normed_one, normed_hbm), (attn_out, attn_hbm))
    late = ((layer_out, layer_out_hbm), (grad_low, grad_low_hbm), (grad_two, grad_two_hbm))
    early = [pltpu.make_async_copy(*pair, done.at[at]) for at, pair in enumerate(early)]
    late = [pltpu.make_async_copy(*pair, done.at[3 + at]) for at, pair in enumerate(late)]
    mine = pl.ds(pl.multiple_of(meta[4] * ROWS, ROWS), ROWS)
    fetch = pltpu.make_async_copy(cotangent_all.at[mine, :], cotangent, done.at[6])

    @pl.when(step == 0)
    def _():
        fetch.start()
        for block in blocks_of(240):
            attn = (
                dot(gated_own[block, :], out_own[...])
                + dot(gated_other[block, :], out_other[...])
                + row_of(vectors, OUT_BIAS)
            )
            attn_out[block, :] = attn.astype(BF16)
            normed, spread = norm_stats(
                hidden[block, :].astype(F32) + attn * row_of(vectors, HID_EFF)
            )
            normed_one[block, :] = normed.astype(BF16)
            spread_one[block, :] = jnp.broadcast_to(spread, (240, 128))
            value = normed * row_of(vectors, LN1_GAIN) + row_of(vectors, LN1_BIAS)
            first[block, :] = value
            first_low[block, :] = value.astype(BF16)
            total[block, :] = jnp.broadcast_to(row_of(vectors, FFN_OUT_BIAS), value.shape)
        for copy in early:
            copy.start()

    def forward(pack, weight_in, weight_out):
        bias = pack[PACK_IN_BIAS : PACK_IN_BIAS + 1, :]
        eff = pack[PACK_FFN : PACK_FFN + 1, :]
        at = pl.multiple_of(step * cols, cols)
        for block in blocks_of(row_step):
            pre = dot(first_low[block, :], weight_in[...]) + bias
            value, slope = gelu_and_slope(pre)
            low = (value * eff).astype(BF16)
            inner_out[block, :] = low
            inner[block, pl.ds(at, cols)] = low
            slope_out[block, :] = (slope * eff).astype(BF16)
            total[block, :] += dot(low, weight_out[...])

    pl.when(step < chunks)(lambda: forward(pack_own, in_own, ffn_own))
    pl.when((step >= chunks) & (step < 2 * chunks))(
        lambda: forward(pack_other, in_other, ffn_other)
    )

    @pl.when(step == 2 * chunks)
    def _():
        for copy in early:
            copy.wait()
        fetch.wait()
        gain = row_of(vectors, LN2_GAIN)
        valid = valid_column(meta)
        hid_eff = row_of(vectors, HID_EFF)
        totals = [jnp.zeros((1, first.shape[1]), F32)] * 4
        for block in blocks_of(120):
            ffn_out = total[block, :]
            normed, spread = norm_stats(first[block, :] + ffn_out * hid_eff)
            layer_out[block, :] = (
                (normed * gain + row_of(vectors, LN2_BIAS)) * valid[block]
            ).astype(BF16)
            grad_final = cotangent[block, :].astype(F32) * valid[block]
            grad = norm_back(grad_final, normed, spread, gain)
            grad_ffn = grad * hid_eff
            grad_two[block, :] = grad
            grad_low[block, :] = grad_ffn.astype(BF16)
            terms = (grad_ffn, grad_final * normed, grad_final, grad * ffn_out)
            totals = [part + column_sum(term) for part, term in zip(totals, terms, strict=True)]
        sums[...] = jnp.zeros_like(sums)
        for place, part in enumerate(totals):
            sums[place : place + 1, :] = part
        for copy in late:
            copy.start()

    def backward(chunk, out):
        at = pl.multiple_of(chunk * cols, cols)
        out[...] = by_rows(inner[:, pl.ds(at, cols)], grad_low[...]).astype(BF16)

    pl.when(step >= 2 * chunks)(lambda: backward(step - chunks, weight_other))

    @pl.when(step == 3 * chunks - 1)
    def _():
        for copy in late:
            copy.wait()


def feed_forward(
    meta, hidden, cotangent, gated, outs, vectors, packs, ins, ffns, cols=768, row_step=480, after=()
):
    width = hidden.shape[1]
    half = gated[0].shape[1]
    units = ins[0].shape[1]
    chunks = units // cols
    column = pl.BlockSpec((ROWS, cols), lambda i, meta: (0, jnp.minimum(i, 2 * chunks - 1)))

    def part(first, i):
        return jnp.clip(i - first, 0, chunks - 1)

    def across(first, rows):
        return pl.BlockSpec((rows, cols), lambda i, meta: (0, part(first, i)))

    def down(first):
        return pl.BlockSpec((cols, width), lambda i, meta: (part(first, i), 0))

    low = bf16(ROWS, width)
    held = pltpu.VMEM((ROWS, width), BF16)
    wide = pltpu.VMEM((ROWS, width), F32)
    return call(
        "feed_forward",
        partial(ffn_body, chunks, row_step),
        (3 * chunks,),
        32,
        [meta],
        [
            (hidden, own_rows(width)),
            (cotangent, HBM),
            (gated[0], whole(ROWS, half)),
            (gated[1], whole(ROWS, half)),
            (outs[0], whole(half, width)),
            (outs[1], whole(half, width)),
            (vectors, whole(*vectors.shape)),
            (packs[0], across(0, packs[0].shape[0])),
            (packs[1], across(chunks, packs[1].shape[0])),
            (ins[0], across(0, width)),
            (ins[1], across(chunks, width)),
            (ffns[0], down(0)),
            (ffns[1], down(chunks)),
        ],
        [(low, HBM)] * 5
        + [
            (f32(ROWS, width), HBM),
            (f32(ROWS, 128), whole(ROWS, 128)),
            (bf16(ROWS, 2 * units), column),
            (bf16(ROWS, 2 * units), column),
            (bf16(units, width), down(2 * chunks)),
            (f32(8, width), whole(8, width)),
        ],
        scratch=[
            wide,
            wide,
            pltpu.VMEM((ROWS, 2 * units), BF16),
            held,
            held,
            held,
            held,
            held,
            held,
            wide,
            pltpu.SemaphoreType.DMA((7,)),
        ],
        after=after,
    )


def outer_body(left, right, out):
    out[...] = by_rows(left[...], right[...]).astype(BF16)


def outer(left, right, cols, after=(), step=512):
    width = right.shape[1]
    first = cols.start // step
    size = cols.stop - cols.start
    return call(
        "outer",
        outer_body,
        (size // step,),
        5,
        [],
        [
            (left, pl.BlockSpec((ROWS, step), lambda i: (0, i + first))),
            (right, whole(ROWS, width)),
        ],
        [(bf16(size, width), pl.BlockSpec((step, width), lambda i: (i, 0)))],
        after=after,
    )[0]


def shrink_body(
    chunks,
    row_step,
    grad_low,
    first_low_hbm,
    before_hbm,
    inner,
    slope,
    weight_in,
    weight_out,
    weight_grad,
    grad_first,
    unit_sums,
    kept,
    total,
    first_low,
    before,
    done,
):
    step = pl.program_id(0)
    fetch_low = pltpu.make_async_copy(first_low_hbm, first_low, done.at[0])
    fetch_before = pltpu.make_async_copy(before_hbm, before, done.at[1])

    @pl.when(step == 0)
    def _():
        fetch_low.start()
        fetch_before.start()

    bias_sum = jnp.zeros((1, inner.shape[1]), F32)
    gate_sum = jnp.zeros((1, inner.shape[1]), F32)
    for block in blocks_of(row_step):
        grad_inner = by_cols(grad_low[block, :], weight_out[...])
        grad_pre = grad_inner * slope[block, :].astype(F32)
        bias_sum += column_sum(grad_pre)
        gate_sum += column_sum(inner[block, :].astype(F32) * grad_inner)
        low = grad_pre.astype(BF16)
        kept[block, :] = low
        back = by_cols(low, weight_in[...])

        @pl.when(step == 0)
        def _(block=block, back=back):
            total[block, :] = back

        @pl.when((step > 0) & (step < chunks - 1))
        def _(block=block, back=back):
            total[block, :] += back

        @pl.when(step == chunks - 1)
        def _(block=block, back=back):
            if block.start == 0:
                fetch_before.wait()
            grad_first[block, :] = total[block, :] + back + before[block, :]

    unit_sums[...] = jnp.zeros_like(unit_sums)
    unit_sums[0:1, :] = bias_sum
    unit_sums[1:2, :] = gate_sum
    pl.when(step == 0)(fetch_low.wait)
    weight_grad[...] = by_rows(first_low[...], kept[...]).astype(BF16)


def shrink(
    side, grad_low, first_low, before, inner, slope, weight_in, weight_out, cols=512, row_step=960, after=()
):
    width, units = weight_in.shape
    chunks = units // cols
    full = whole(ROWS, width)
    across = pl.BlockSpec((width, cols), lambda i: (0, i))
    column = pl.BlockSpec((ROWS, cols), lambda i: (0, i + side * chunks))
    return call(
        "shrink",
        partial(shrink_body, chunks, row_step),
        (chunks,),
        12,
        [],
        [
            (grad_low, full),
            (first_low, HBM),
            (before, HBM),
            (inner, column),
            (slope, column),
            (weight_in, across),
            (weight_out, pl.BlockSpec((cols, width), lambda i: (i, 0))),
        ],
        [
            (bf16(width, units), across),
            (f32(ROWS, width), full),
            (f32(8, units), pl.BlockSpec((8, cols), lambda i: (0, i))),
        ],
        scratch=[
            pltpu.VMEM((ROWS, cols), BF16),
            pltpu.VMEM((ROWS, width), F32),
            pltpu.VMEM((ROWS, width), BF16),
            pltpu.VMEM((ROWS, width), F32),
            pltpu.SemaphoreType.DMA((2,)),
        ],
        after=after,
    )


def part_body(
    head_width,
    grad_first,
    normed_one,
    spread_one,
    attn_out,
    vectors,
    gated_own,
    gated_other,
    out_own,
    out_other,
    pack_own,
    pack_other,
    grad_one,
    context_own,
    context_other,
    means_own,
    means_other,
    weight_mine,
    weight_other,
    sums,
    low,
):
    gain = row_of(vectors, LN1_GAIN)
    hid_eff = row_of(vectors, HID_EFF)
    totals = [jnp.zeros((1, grad_first.shape[1]), F32)] * 4
    for block in blocks_of(120):
        grad = grad_first[block, :]
        normed = normed_one[block, :].astype(F32)
        one = norm_back(grad, normed, spread_one[block, 0:1], gain)
        grad_one[block, :] = one
        attn = one * hid_eff
        low[block, :] = attn.astype(BF16)
        terms = (attn, grad * normed, grad, one * attn_out[block, :].astype(F32))
        totals = [part + column_sum(term) for part, term in zip(totals, terms, strict=True)]
    sums[...] = jnp.zeros_like(sums)
    for place, part in enumerate(totals):
        sums[place : place + 1, :] = part
    half = gated_own.shape[1]
    head = lax.broadcasted_iota(jnp.int32, (8, half), 1) // head_width
    pick = (head == lax.broadcasted_iota(jnp.int32, (8, half), 0)).astype(BF16)
    for place, (gated, weight, pack, context, means, weight_grad) in enumerate(
        (
            (gated_other, out_other, pack_other, context_other, means_other, weight_other),
            (gated_own, out_own, pack_own, context_own, means_own, weight_mine),
        )
    ):
        weight_grad[...] = by_rows(gated[...], low[...]).astype(BF16)
        column = jnp.zeros((1, half), F32)
        for start, size in BUCKETS:
            rows = slice(start, start + size)
            grads = by_cols(low[rows, :], weight[...])
            context[rows, :] = (grads * pack[PACK_HEAD : PACK_HEAD + 1, 0:half]).astype(BF16)
            terms = grads * gated[rows, :].astype(F32)
            column += column_sum(terms)
            high = terms.astype(BF16)
            rest = (terms - high.astype(F32)).astype(BF16)
            means[:, rows] = by_cols(pick, high) + by_cols(pick, rest)
        sums[5 - place : 6 - place, 0:half] = column


def part_heads(
    grad_first, normed_one, spread_one, attn_out, vectors, gated, outs, packs, head_width, after=()
):
    width = grad_first.shape[1]
    half = gated[0].shape[1]
    values = [grad_first, normed_one, spread_one, attn_out, vectors, *gated, *outs, *packs]
    made = [
        f32(ROWS, width),
        bf16(ROWS, half),
        bf16(ROWS, half),
        f32(8, ROWS),
        f32(8, ROWS),
        bf16(half, width),
        bf16(half, width),
        f32(8, width),
    ]
    return call(
        "part_heads",
        partial(part_body, head_width),
        (1,),
        9,
        [],
        [(value, whole(*value.shape)) for value in values],
        [(shape, whole(*shape.shape)) for shape in made],
        scratch=[pltpu.VMEM((ROWS, width), BF16)],
        after=after,
    )


def add_back_body(start, *refs):
    grads, weights, out = refs[:6], refs[6:12], refs[12]
    total = start[...]
    for side in (0, 3):
        left = jnp.concatenate([part[...] for part in grads[side : side + 3]], 1)
        right = jnp.concatenate([part[...] for part in weights[side : side + 3]], 1)
        total += by_cols(left, right)
    out[...] = total


def add_back(start, grads, weights, after=()):
    width = start.shape[1]
    half = grads[0].shape[1]
    step = ROWS // 4
    return call(
        "add_back",
        add_back_body,
        (4,),
        6,
        [],
        [(start, pl.BlockSpec((step, width), lambda i: (i, 0)))]
        + [(part, pl.BlockSpec((step, half), lambda i: (i, 0))) for part in grads]
        + [(part, whole(width, half)) for part in weights],
        [(f32(ROWS, width), pl.BlockSpec((step, width), lambda i: (i, 0)))],
        after=after,
    )[0]


def swap_bit(values, dp_size, bit):
    return lax.ppermute(values, "dp", [(at, at ^ (1 << bit)) for at in range(dp_size)])


TAIL = 128


def load(ref, rows, tail):
    values = ref[rows, :].astype(F32)
    if not tail:
        return values, None
    cut = values.shape[1] - TAIL
    return values[:, :cut], values[:, cut : cut + TAIL // 2] + values[:, cut + TAIL // 2 :]


def store(ref, main, extra):
    if extra is None:
        ref[...] = main.astype(ref.dtype)
        return
    cut = main.shape[1]
    high = extra.astype(BF16)
    ref[:, :cut] = main.astype(BF16)
    ref[:, cut : cut + TAIL // 2] = high
    ref[:, cut + TAIL // 2 :] = (extra - high.astype(F32)).astype(BF16)


def split_by(side, totals, kept, sent):
    for part, total in enumerate(totals):

        @pl.when(side == part)
        def _(total=total):
            store(kept, *total)

        @pl.when(side != part)
        def _(total=total):
            store(sent, *total)


def add(left, right):
    return tuple(None if a is None else a + b for a, b in zip(left, right, strict=True))


class Stream:
    def __init__(self, ins, shape, first, order, tail=False):
        self.ins = ins
        self.rows, self.cols = shape
        self.first = first
        self.order = order
        self.tail = tail
        self.stage = 0
        self.kept = self.value = self.arrived = None

    def job(self):
        stages = len(self.order)
        stage, tail = self.stage, self.tail
        size = self.rows >> stage if stage <= stages else self.value.shape[0]
        if stage < stages:
            half = size // 2
            ins = list(self.ins) if stage == 0 else [self.kept, self.arrived]

            def body(sides, *refs):
                *given, kept, sent = refs
                totals = []
                for at in (0, half):
                    rows = slice(at, at + half)
                    if stage == 0:
                        totals.append(self.first(given, rows))
                    else:
                        totals.append(add(*[load(ref, rows, tail) for ref in given]))
                split_by(sides[self.order[stage]], totals, kept, sent)

            return ins, [bf16(half, self.cols)] * 2, body
        if stage == stages:

            def body(sides, kept, arrived, value):
                rows = slice(0, size)
                store(value, *add(load(kept, rows, tail), load(arrived, rows, tail)))

            return [self.kept, self.arrived], [bf16(size, self.cols)], body
        bit = self.order[2 * stages - stage]

        def body(sides, own, arrived, value):
            for first, halves in in_order(sides[bit], own, arrived):

                @pl.when(first)
                def _(halves=halves):
                    for place, half in enumerate(halves):
                        value[place * size : place * size + size, :] = half[...]

        return [self.value, self.arrived], [bf16(2 * size, self.cols)], body

    def take(self, outs, dp_size):
        stages = len(self.order)
        if self.stage < stages:
            self.kept, sent = outs
            self.arrived = swap_bit(sent, dp_size, self.order[self.stage])
        else:
            (self.value,) = outs
            bit = self.order[2 * stages - 1 - self.stage]
            self.arrived = swap_bit(self.value, dp_size, bit)
        self.stage += 1

    def last(self):
        return self.stage == 2 * len(self.order)


def in_order(side, own, arrived):
    return (side == 0, (own, arrived)), (side == 1, (arrived, own))


def small_call(name, body, ins, outs, sides, after=()):
    return call(
        name,
        body,
        (1,),
        2,
        [sides],
        [(value, whole(*value.shape)) for value in ins],
        [(shape, whole(*shape.shape)) for shape in outs],
        after=after,
        vmem=24,
    )


def advance(streams, dp_size, sides, after=()):
    jobs = [stream.job() for stream in streams]
    ins = [value for job in jobs for value in job[0]]
    outs = [shape for job in jobs for shape in job[1]]

    def body(sides, *refs):
        given, made = refs[: len(ins)], refs[len(ins) :]
        for inputs, shapes, work in jobs:
            work(sides, *given[: len(inputs)], *made[: len(shapes)])
            given, made = given[len(inputs) :], made[len(shapes) :]

    found = small_call("advance", body, ins, outs, sides, after)
    for stream, job in zip(streams, jobs, strict=True):
        stream.take(found[: len(job[1])], dp_size)
        found = found[len(job[1]) :]


def states(streams):
    return [stream.kept if stream.stage <= len(stream.order) else stream.value for stream in streams]


def finish(streams, sides, by_cols, after=()):
    rows, cols = streams[0].rows, streams[0].cols
    size = rows // 2

    def body(sides, *refs):
        out = refs[-1]
        for at, stream in enumerate(streams):
            pair = refs[2 * at : 2 * at + 2]
            row, col = (0, at * cols) if by_cols else (at * rows, 0)
            for first, halves in in_order(sides[stream.order[0]], *pair):

                @pl.when(first)
                def _(row=row, col=col, halves=halves):
                    for place, half in enumerate(halves):
                        top = row + place * size
                        out[top : top + size, col : col + cols] = half[...].astype(F32)

    ins = [value for stream in streams for value in (stream.value, stream.arrived)]
    shape = (rows, cols * len(streams)) if by_cols else (rows * len(streams), cols)
    return small_call("finish", body, ins, [f32(*shape)], sides, after)[0]


def orders_of(dp_size):
    bits = dp_size.bit_length() - 1
    if bits == 4:
        plain = (0, 1, 2, 3), (1, 0, 2, 3)
        return *plain, (2, 0, 1, 3), (0, 2, 3, 1), (0, 1, 2, 3), (1, 0, 2, 3)
    return tuple(tuple((at + turn) % bits for at in range(bits)) for turn in range(6))


def late_streams(qkv, out, small, orders):
    rows, cols = qkv[0].shape
    half = out[0].shape[0]
    cut = -(-cols // 384) * 128 * 2
    places = small[0].shape[1] // (TAIL // 2)
    depth = small[0].shape[0]

    def front(given, where):
        return sum(ref[where, 0:cut].astype(F32) for ref in given), None

    def back(given, where):
        first, size = where.start, where.stop - where.start
        left = sum(ref[where, cut:cols].astype(F32) for ref in given[0:2])
        side = first // half
        lines = slice(first - side * half, first - side * half + size)
        right = sum(
            ref[lines, side * half : side * half + half].astype(F32) for ref in given[2:4]
        )
        extra = []
        for place in range(first // depth, (first + size) // depth):
            if place < places:
                at = slice(place * TAIL // 2, (place + 1) * TAIL // 2)
                extra.append(sum(ref[:, at] for ref in given[4:6]))
        used = depth * len(extra)
        if used < size:
            extra.append(jnp.zeros((size - used, TAIL // 2), F32))
        return jnp.concatenate([left, right], 1), jnp.concatenate(extra, 0)

    return [
        Stream(qkv, (rows, cut), front, orders[0]),
        Stream((*qkv, *out, *small), (rows, cols - cut + half + TAIL), back, orders[1], True),
    ]


def finish_late(streams, sides, lanes, small_shape, after=()):
    front, back = streams
    rows = front.rows
    size = rows // 2
    depth, width = small_shape
    cut = front.cols
    half = (cut + back.cols - TAIL) // 4
    places = width // (TAIL // 2)

    def body(sides, own0, arrived0, own1, arrived1, qkv_out, out_out, small_out):
        def qkv_part(values, which, first):
            for at in range(0, values.shape[1], lanes):
                pair, kind = divmod((first + at) // lanes, 3)
                columns = slice(pair * lanes, (pair + 1) * lanes)
                qkv_out[which * size : (which + 1) * size, kind, columns] = values[
                    :, at : at + lanes
                ].astype(F32)

        for first, halves in in_order(sides[front.order[0]], own0, arrived0):

            @pl.when(first)
            def _(halves=halves):
                for which, values in enumerate(halves):
                    qkv_part(values, which, 0)

        for first, halves in in_order(sides[back.order[0]], own1, arrived1):

            @pl.when(first)
            def _(halves=halves):
                for which, values in enumerate(halves):
                    qkv_part(values[:, 0 : 3 * half - cut], which, cut)
                    out_out[:, which * half : (which + 1) * half] = values[
                        :, 3 * half - cut : 4 * half - cut
                    ].astype(F32)
                    for place in range(which * size // depth, (which + 1) * size // depth):
                        if place < places:
                            at = place * depth - which * size
                            _, extra = load(values, slice(at, at + depth), True)
                            small_out[:, place * TAIL // 2 : (place + 1) * TAIL // 2] = extra

    ins = [front.value, front.arrived, back.value, back.arrived]
    outs = [f32(rows, 3, half), f32(half, rows), f32(depth, width)]
    return small_call("finish_late", body, ins, outs, sides, after)


def pack_sums(part_sums, turn_sums, bias_sums, unit_sums):
    width = part_sums.shape[1]
    half = bias_sums[0].shape[1]
    unit_rows = unit_sums[0].shape[1] // width

    def body(part, turned, bias_own, bias_other, unit_own, unit_other, mine, theirs):
        sides = ((mine, bias_own, unit_own), (theirs, bias_other, unit_other))
        for side, (out, bias, unit) in enumerate(sides):
            out[...] = jnp.zeros_like(out)
            out[0:4, :] = part[0:4, :]
            out[4:8, :] = turned[0:4, :]
            out[8:9, 0:half] = bias[0:1, :]
            out[8:9, half : 2 * half] = bias[1:2, :]
            out[9:10, :] = part[4 + side : 5 + side, :]
            for kind in (0, 1):
                for row in range(unit_rows):
                    place = 10 + kind * unit_rows + row
                    out[place : place + 1, :] = unit[
                        kind : kind + 1, row * width : (row + 1) * width
                    ]

    values = [part_sums, turn_sums, *bias_sums, *unit_sums]
    rows = -(-(10 + 2 * unit_rows) // 8) * 8
    return call(
        "pack_sums",
        body,
        (1,),
        1,
        [],
        [(value, whole(*value.shape)) for value in values],
        [(f32(rows, width), whole(rows, width))] * 2,
        vmem=24,
    )


def per_device(
    dp_size,
    hidden,
    cotangent,
    counts,
    lengths,
    qkv_weight,
    qv_bias,
    out_weight,
    out_bias,
    ln1_gain,
    ln1_bias,
    in_weight,
    in_bias,
    ffn_out_weight,
    ffn_out_bias,
    ln2_gain,
    ln2_bias,
    head_gate,
    head_mask,
    ffn_gate,
    ffn_mask,
    hidden_gate,
    hidden_mask,
):
    width = hidden.shape[1]
    own_heads = head_gate.shape[0]
    half = qkv_weight.shape[2]
    units = in_weight.shape[1]
    head_width = half // own_heads
    head_at = lax.axis_index("head")

    def other(values):
        return lax.ppermute(values, "head", [(0, 1), (1, 0)])

    def pad_to(values, size):
        return jnp.pad(values, (0, size - values.shape[0]))

    meta = jnp.concatenate(
        [
            lax.dynamic_index_in_dim(
                jnp.where(counts[0] > 0, lengths[0], 0), head_at, 0, keepdims=False
            ),
            head_at[None],
        ]
    )
    head_flags = head_mask.astype(F32)
    ffn_flags = ffn_mask.astype(F32)
    hidden_flags = hidden_mask.astype(F32)
    pack = jnp.stack(
        [
            in_bias,
            ffn_gate * ffn_flags,
            pad_to(qv_bias.reshape(-1), units),
            pad_to(jnp.repeat(head_gate * head_flags, head_width), units),
        ]
    )
    vectors = jnp.stack(
        [
            out_bias,
            ln1_gain,
            ln1_bias,
            ffn_out_bias,
            ln2_gain,
            ln2_bias,
            hidden_gate * hidden_flags,
        ]
    )
    qkv_own = [qkv_weight[:, at] for at in range(3)]
    qkv_other = [other(part) for part in qkv_own]
    packs = (pack, other(pack))
    outs = (out_weight, other(out_weight))
    ins = (in_weight, other(in_weight))
    ffns = (ffn_out_weight, other(ffn_out_weight))
    sides = jnp.stack([(lax.axis_index("dp") >> bit) & 1 for bit in range(dp_size.bit_length() - 1)])
    orders = orders_of(dp_size)
    step = partial(advance, dp_size=dp_size, sides=sides)

    def halves(size, at):
        return slice(at * size // 2, (at + 1) * size // 2)

    def sum_stream(left, right, order, rows=None, cols=None):
        rows = rows or slice(0, left.shape[0])
        cols = cols or slice(0, left.shape[1])

        def first(given, at):
            at = slice(rows.start + at.start, rows.start + at.stop)
            return sum(ref[at, cols].astype(F32) for ref in given), None

        shape = (rows.stop - rows.start, cols.stop - cols.start)
        return Stream((left, right), shape, first, order)

    *qkv0, gated0, logs0 = attend(meta, hidden, qkv_own, packs[0], head_width)
    *qkv1, gated1, logs1 = attend(meta, hidden, qkv_other, packs[1], head_width, [gated0])
    gated = (gated0, gated1)
    (
        layer_out,
        first_low,
        normed_one,
        attn_out,
        grad_low,
        grad_two,
        spread_one,
        inner,
        slope,
        ffn_grad_other,
        turn_sums,
    ) = feed_forward(meta, hidden, cotangent, gated, outs, vectors, packs, ins, ffns)
    ffn_grad_theirs = other(ffn_grad_other)
    ffn_grad_mine = outer(inner, grad_low, slice(0, units))
    streams = [
        sum_stream(ffn_grad_mine, ffn_grad_theirs, orders[at], rows=halves(units, at))
        for at in (0, 1)
    ]
    step(streams)
    in_grad_other, grad_first, unit_sums1 = shrink(
        1, grad_low, first_low, grad_two, inner, slope, ins[1], ffns[1], after=states(streams)
    )
    in_grad_theirs = other(in_grad_other)
    step(streams, after=[grad_first])
    in_grad_mine, grad_first, unit_sums0 = shrink(
        0, grad_low, first_low, grad_first, inner, slope, ins[0], ffns[0], after=states(streams)
    )
    streams += [
        sum_stream(in_grad_mine, in_grad_theirs, orders[2 + at], cols=halves(units, at))
        for at in (0, 1)
    ]
    step(streams)
    (
        grad_one,
        grad_context0,
        grad_context1,
        means0,
        means1,
        out_grad_mine,
        out_grad_other,
        part_sums,
    ) = part_heads(
        grad_first,
        normed_one,
        spread_one,
        attn_out,
        vectors,
        gated,
        outs,
        packs,
        head_width,
        after=states(streams),
    )
    out_grad_theirs = other(out_grad_other)
    step(streams, after=[grad_one])
    *mixed1, qkv_grad_other, bias_sums1 = attend_back(
        meta,
        hidden,
        qkv1,
        grad_context1,
        logs1,
        means1,
        head_width,
        after=states(streams),
    )
    qkv_grad_theirs = other(qkv_grad_other)
    step(streams, after=[mixed1[0]])
    *mixed0, qkv_grad_mine, bias_sums0 = attend_back(
        meta,
        hidden,
        qkv0,
        grad_context0,
        logs0,
        means0,
        head_width,
        after=states(streams) + [mixed1[0]],
    )
    small = pack_sums(part_sums, turn_sums, (bias_sums0, bias_sums1), (unit_sums0, unit_sums1))
    late = late_streams(
        (qkv_grad_mine, qkv_grad_theirs),
        (out_grad_mine, out_grad_theirs),
        (small[0], other(small[1])),
        orders[4:6],
    )
    step([*streams, *late], after=[mixed0[0]])
    grad_hidden = add_back(
        grad_one, mixed0 + mixed1, qkv_own + qkv_other, after=states(streams + late)
    )
    while not late[0].last():
        step([stream for stream in streams if not stream.last()] + late, after=[grad_hidden])
    grad_ffn_out_weight = finish(streams[0:2], sides, by_cols=False)
    grad_in_weight = finish(streams[2:4], sides, by_cols=True)
    grad_qkv_weight, grad_out_weight, small = finish_late(
        late, sides, 2 * head_width, small[0].shape
    )
    (
        grad_out_bias,
        grad_ln1_gain,
        grad_ln1_bias,
        gate_one,
        grad_ffn_out_bias,
        grad_ln2_gain,
        grad_ln2_bias,
        gate_two,
    ) = small[:8]
    unit_rows = units // width
    return (
        layer_out,
        grad_hidden,
        grad_qkv_weight,
        small[8].reshape(2, half),
        grad_out_weight,
        grad_out_bias,
        grad_ln1_gain,
        grad_ln1_bias,
        grad_in_weight,
        small[10 : 10 + unit_rows].reshape(-1),
        grad_ffn_out_weight,
        grad_ffn_out_bias,
        grad_ln2_gain,
        grad_ln2_bias,
        jnp.sum(small[9, :half].reshape(own_heads, head_width), 1) * head_flags / head_gate,
        small[10 + unit_rows : 10 + 2 * unit_rows].reshape(-1) * ffn_flags / ffn_gate,
        (gate_one + gate_two) * hidden_flags,
    )


def solution(mesh):
    placed = (
        P("dp", None),
        P("dp", None),
        P("dp", None, None),
        P("dp", None, None),
        P(None, None, "head"),
        P(None, "head"),
        P("head", None),
        P(),
        P(),
        P(),
        P(None, "head"),
        P("head"),
        P("head", None),
        P(),
        P(),
        P(),
        P("head"),
        P("head"),
        P("head"),
        P("head"),
        P(),
        P(),
    )
    return jax.shard_map(
        partial(per_device, mesh.shape["dp"]),
        mesh=mesh,
        in_specs=placed,
        out_specs=(
            P(("dp", "head"), None),
            P(("dp", "head"), None),
            P(None, None, "head"),
            P(None, "head"),
            P("head", None),
            P(),
            P(),
            P(),
            P(None, "head"),
            P("head"),
            P("head", None),
            P(),
            P(),
            P(),
            P("head"),
            P("head"),
            P(),
        ),
        check_vma=False,
    )
```

```python
from functools import partial

import jax
import jax.numpy as jnp
from jax import lax
from jax.experimental import pallas as pl
from jax.experimental.pallas import tpu as pltpu
from jax.sharding import PartitionSpec as P

BASE = 64
ROWS = 15 * BASE
EPSILON = 1e-12
MASKED = -1e9
LOG2E = 1.4426950408889634
BUCKETS = ((0, 8 * BASE), (8 * BASE, 4 * BASE), (12 * BASE, 2 * BASE), (14 * BASE, BASE))
F32 = jnp.float32
BF16 = jnp.bfloat16
MEBI = 1 << 20
HBM = pl.BlockSpec(memory_space=pl.ANY)


def dot(left, right):
    return jnp.dot(left, right, preferred_element_type=F32)


def by_rows(left, right):
    return lax.dot_general(left, right, (((0,), (0,)), ((), ())), preferred_element_type=F32)


def by_cols(left, right):
    return lax.dot_general(left, right, (((1,), (1,)), ((), ())), preferred_element_type=F32)


def f32(*shape):
    return jax.ShapeDtypeStruct(shape, F32)


def bf16(*shape):
    return jax.ShapeDtypeStruct(shape, BF16)


def whole(*shape):
    return pl.BlockSpec(shape, lambda *_: (0,) * len(shape))


def call(name, body, grid, micros, scalars, ins, outs, scratch=(), after=(), vmem=58):
    first = len(scalars) + len(ins)

    def run(*refs):
        body(*refs[:first], *refs[first + len(after) :])

    return pl.pallas_call(
        run,
        grid_spec=pltpu.PrefetchScalarGridSpec(
            num_scalar_prefetch=len(scalars),
            grid=grid,
            in_specs=[spec for _, spec in ins] + [HBM] * len(after),
            out_specs=[spec for _, spec in outs],
            scratch_shapes=list(scratch),
        ),
        out_shape=[shape for shape, _ in outs],
        compiler_params=pltpu.CompilerParams(
            dimension_semantics=("arbitrary",) * len(grid), vmem_limit_bytes=vmem * MEBI
        ),
        cost_estimate=pl.CostEstimate(
            flops=int(micros * 5e9), bytes_accessed=1 << 20, transcendentals=0
        ),
        name=name,
    )(*scalars, *[value for value, _ in ins], *after)


def row_of(vectors, at):
    return vectors[at : at + 1, :]


def column_sum(values):
    return jnp.sum(values, 0, keepdims=True)


def own_rows(width):
    return pl.BlockSpec((ROWS, width), lambda i, meta: (meta[4], 0))


PACK_IN_BIAS, PACK_FFN, PACK_QV, PACK_HEAD = range(4)


def side_masks(lanes):
    low = lax.broadcasted_iota(jnp.int32, (1, lanes), 1) < lanes // 2
    return low, low.astype(BF16), 1 - low.astype(BF16)


def kept_head(gate, side):
    half = gate.shape[1] // 2
    return jnp.max(gate[PACK_HEAD : PACK_HEAD + 1, side * half : (side + 1) * half]) > 0


def attend_body(
    pairs, lanes, meta, hidden, weight_q, weight_k, weight_v, bias_q, bias_v, gate, query, key, value, gated, logs, columns, context
):
    pair = pl.program_id(0)
    weight = jnp.concatenate([weight_q[...], weight_k[...], weight_v[...]], 1)
    mixed = dot(hidden[...], weight)
    query[...] = (mixed[:, :lanes] + bias_q[PACK_QV : PACK_QV + 1, :]).astype(BF16)
    key[...] = mixed[:, lanes : 2 * lanes].astype(BF16)
    value[...] = (mixed[:, 2 * lanes :] + bias_v[PACK_QV : PACK_QV + 1, :]).astype(BF16)
    scale = LOG2E * (lanes // 2) ** -0.5
    low_side, *masks = side_masks(lanes)
    lane = lax.broadcasted_iota(jnp.int32, (1, 128), 1)
    context[...] = jnp.zeros_like(context)
    for side, mask in enumerate(masks):

        @pl.when(kept_head(gate, side))
        def _(side=side, mask=mask):
            for place, (start, size) in enumerate(BUCKETS):
                rows = slice(start, start + size)
                seen = lax.broadcasted_iota(jnp.int32, (1, size), 1) < meta[place]
                shut = jnp.where(seen, 0.0, MASKED).astype(F32)
                scores = by_cols(query[rows, :] * mask, key[rows, :]) + shut
                top = jnp.max(scores, -1, keepdims=True)
                power = jnp.exp2((scores - top) * scale)
                total = jnp.sum(power, -1, keepdims=True)
                found = dot(power.astype(BF16), value[rows, :]) * (1.0 / total)
                log = top * scale + jnp.log2(total)
                columns[rows, :] = jnp.where(lane == 2 * pair + side, log, columns[rows, :])
                context[rows, :] = jnp.where(low_side == (side == 0), found, context[rows, :])

    gated[...] = (context[...] * gate[PACK_HEAD : PACK_HEAD + 1, :]).astype(BF16)

    @pl.when(pair == pairs - 1)
    def _():
        for start, size in BUCKETS:
            rows = slice(start, start + size)
            logs[:, rows] = columns[rows, :].T[0:8, :]


def attend(meta, hidden, weights, pack, head_width, after=()):
    width, half = weights[0].shape
    lanes = 2 * head_width
    pairs = half // lanes
    column = pl.BlockSpec((ROWS, lanes), lambda i, meta: (0, i))
    weight = pl.BlockSpec((width, lanes), lambda i, meta: (0, i))

    def vector(shift):
        return pl.BlockSpec((pack.shape[0], lanes), lambda i, meta: (0, i + shift))

    return call(
        "attend",
        partial(attend_body, pairs, lanes),
        (pairs,),
        9,
        [meta],
        [(hidden, own_rows(width))]
        + [(part, weight) for part in weights]
        + [(pack, vector(0)), (pack, vector(pairs)), (pack, vector(0))],
        [(bf16(ROWS, half), column)] * 4 + [(f32(8, ROWS), whole(8, ROWS))],
        scratch=[pltpu.VMEM((ROWS, 128), F32), pltpu.VMEM((ROWS, lanes), F32)],
        after=after,
        vmem=58,
    )


def pick_row(values, at):
    place = lax.broadcasted_iota(jnp.int32, values.shape, 0)
    return column_sum(jnp.where(place == at, values, 0.0))


def attend_back_body(
    lanes, meta, hidden, query, key, value, grad_context, logs, means, gate, grad_q, grad_k, grad_v, weight_grad, bias_sums, *totals
):
    pair = pl.program_id(0)
    scale = LOG2E * (lanes // 2) ** -0.5
    final = (lanes // 2) ** -0.5
    _, *masks = side_masks(lanes)
    for part in totals:
        part[...] = jnp.zeros_like(part)
    for side, mask in enumerate(masks):

        @pl.when(kept_head(gate, side))
        def _(side=side, mask=mask):
            for place, (start, size) in enumerate(BUCKETS):
                rows = slice(start, start + size)
                seen = lax.broadcasted_iota(jnp.int32, (size, 1), 0) < meta[place]
                shut = jnp.where(seen, 0.0, MASKED).astype(F32)
                keys = key[rows, :]
                log = pick_row(logs[:, rows], 2 * pair + side)
                mean = pick_row(means[:, rows], 2 * pair + side)
                queries = query[rows, :] * mask
                grads = grad_context[rows, :] * mask
                scores = by_cols(keys, queries) + shut
                weights = jnp.exp2(scores * scale - log)
                change = (weights * (by_cols(value[rows, :], grads) - mean)).astype(BF16)
                totals[0][rows, :] += by_rows(change, keys * mask)
                totals[1][rows, :] += dot(change, queries)
                totals[2][rows, :] += dot(weights.astype(BF16), grads)

    grad_query = totals[0][...] * final
    grad_q[...] = grad_query.astype(BF16)
    grad_k[...] = (totals[1][...] * final).astype(BF16)
    grad_v[...] = totals[2][...].astype(BF16)
    query_sum = column_sum(grad_query)
    value_sum = column_sum(totals[2][...])
    grads = jnp.concatenate([grad_q[...], grad_k[...], grad_v[...]], 1)
    weight_grad[...] = by_rows(hidden[...], grads).astype(BF16)
    bias_sums[...] = jnp.zeros_like(bias_sums)
    bias_sums[0:1, :] = query_sum
    bias_sums[1:2, :] = value_sum


def attend_back(meta, hidden, parts, grad_context, logs, means, pack, head_width, after=()):
    half = grad_context.shape[1]
    width = hidden.shape[1]
    lanes = 2 * head_width
    pairs = half // lanes
    column = pl.BlockSpec((ROWS, lanes), lambda i, meta: (0, i))
    return call(
        "attend_back",
        partial(attend_back_body, lanes),
        (pairs,),
        11,
        [meta],
        [(hidden, own_rows(width))]
        + [(part, column) for part in (*parts, grad_context)]
        + [(logs, whole(8, ROWS)), (means, whole(8, ROWS))]
        + [(pack, pl.BlockSpec((pack.shape[0], lanes), lambda i, meta: (0, i)))],
        [(bf16(ROWS, half), column)] * 3
        + [
            (
                bf16(width, 3 * half),
                pl.BlockSpec((width, 3 * lanes), lambda i, meta: (0, i)),
            ),
            (f32(8, half), pl.BlockSpec((8, lanes), lambda i, meta: (0, i))),
        ],
        scratch=[pltpu.VMEM((ROWS, lanes), F32)] * 3,
        after=after,
        vmem=24,
    )


(OUT_BIAS, LN1_GAIN, LN1_BIAS, FFN_OUT_BIAS, LN2_GAIN, LN2_BIAS, HID_EFF) = range(7)


def valid_column(meta):
    at = lax.broadcasted_iota(jnp.int32, (ROWS, 1), 0)
    found = jnp.zeros((ROWS, 1), F32)
    for place, (start, size) in enumerate(BUCKETS):
        found = jnp.where((at >= start) & (at < start + meta[place]), 1.0, found)
    return found


def norm_stats(resid):
    centred = resid - jnp.mean(resid, -1, keepdims=True)
    spread = lax.rsqrt(jnp.mean(centred * centred, -1, keepdims=True) + EPSILON)
    return (centred * spread, spread)


def norm_back(grad_out, normed, spread, gain):
    grad_normed = grad_out * gain
    first_mean = jnp.mean(grad_normed, -1, keepdims=True)
    second_mean = jnp.mean(grad_normed * normed, -1, keepdims=True)
    return spread * (grad_normed - first_mean - normed * second_mean)


def blocks_of(step):
    return [slice(at, at + step) for at in range(0, ROWS, step)]


def gelu_and_slope(z):
    below = 0.5 + 0.5 * lax.erf(z * 0.5**0.5)
    density = jnp.exp2((-0.5 * LOG2E) * (z * z)) * (0.5 / 3.141592653589793) ** 0.5
    return (z * below, below + z * density)


def ffn_body(
    chunks,
    row_step,
    meta,
    hidden,
    cotangent_all,
    gated_own,
    gated_other,
    out_own,
    out_other,
    vectors,
    pack_own,
    pack_other,
    in_own,
    in_other,
    ffn_own,
    ffn_other,
    layer_out_hbm,
    first_low_hbm,
    normed_hbm,
    attn_hbm,
    grad_low_hbm,
    grad_two_hbm,
    spread_one,
    inner_out,
    slope_out,
    weight_other,
    sums,
    first,
    total,
    inner,
    cotangent,
    layer_out,
    first_low,
    normed_one,
    attn_out,
    grad_low,
    grad_two,
    done,
):
    step = pl.program_id(0)
    cols = inner_out.shape[1]
    early = ((first_low, first_low_hbm), (normed_one, normed_hbm), (attn_out, attn_hbm))
    late = ((layer_out, layer_out_hbm), (grad_low, grad_low_hbm), (grad_two, grad_two_hbm))
    early = [pltpu.make_async_copy(*pair, done.at[at]) for at, pair in enumerate(early)]
    late = [pltpu.make_async_copy(*pair, done.at[3 + at]) for at, pair in enumerate(late)]
    mine = pl.ds(pl.multiple_of(meta[4] * ROWS, ROWS), ROWS)
    fetch = pltpu.make_async_copy(cotangent_all.at[mine, :], cotangent, done.at[6])

    @pl.when(step == 0)
    def _():
        fetch.start()
        for block in blocks_of(240):
            attn = (
                dot(gated_own[block, :], out_own[...])
                + dot(gated_other[block, :], out_other[...])
                + row_of(vectors, OUT_BIAS)
            )
            attn_out[block, :] = attn.astype(BF16)
            normed, spread = norm_stats(
                hidden[block, :].astype(F32) + attn * row_of(vectors, HID_EFF)
            )
            normed_one[block, :] = normed.astype(BF16)
            spread_one[block, :] = jnp.broadcast_to(spread, (240, 128))
            value = normed * row_of(vectors, LN1_GAIN) + row_of(vectors, LN1_BIAS)
            first[block, :] = value
            first_low[block, :] = value.astype(BF16)
            total[block, :] = jnp.broadcast_to(row_of(vectors, FFN_OUT_BIAS), value.shape)
        for copy in early:
            copy.start()

    def forward(pack, weight_in, weight_out):
        bias = pack[PACK_IN_BIAS : PACK_IN_BIAS + 1, :]
        eff = pack[PACK_FFN : PACK_FFN + 1, :]
        at = pl.multiple_of(step * cols, cols)
        for block in blocks_of(row_step):
            pre = dot(first_low[block, :], weight_in[...]) + bias
            value, slope = gelu_and_slope(pre)
            low = (value * eff).astype(BF16)
            inner_out[block, :] = low
            inner[block, pl.ds(at, cols)] = low
            slope_out[block, :] = (slope * eff).astype(BF16)
            total[block, :] += dot(low, weight_out[...])

    pl.when(step < chunks)(lambda: forward(pack_own, in_own, ffn_own))
    pl.when((step >= chunks) & (step < 2 * chunks))(
        lambda: forward(pack_other, in_other, ffn_other)
    )

    @pl.when(step == 2 * chunks)
    def _():
        for copy in early:
            copy.wait()
        fetch.wait()
        gain = row_of(vectors, LN2_GAIN)
        valid = valid_column(meta)
        hid_eff = row_of(vectors, HID_EFF)
        totals = [jnp.zeros((1, first.shape[1]), F32)] * 4
        for block in blocks_of(120):
            ffn_out = total[block, :]
            normed, spread = norm_stats(first[block, :] + ffn_out * hid_eff)
            layer_out[block, :] = (
                (normed * gain + row_of(vectors, LN2_BIAS)) * valid[block]
            ).astype(BF16)
            grad_final = cotangent[block, :].astype(F32) * valid[block]
            grad = norm_back(grad_final, normed, spread, gain)
            grad_ffn = grad * hid_eff
            grad_two[block, :] = grad
            grad_low[block, :] = grad_ffn.astype(BF16)
            terms = (grad_ffn, grad_final * normed, grad_final, grad * ffn_out)
            totals = [part + column_sum(term) for part, term in zip(totals, terms, strict=True)]
        sums[...] = jnp.zeros_like(sums)
        for place, part in enumerate(totals):
            sums[place : place + 1, :] = part
        for copy in late:
            copy.start()

    def backward(chunk, out):
        at = pl.multiple_of(chunk * cols, cols)
        out[...] = by_rows(inner[:, pl.ds(at, cols)], grad_low[...]).astype(BF16)

    pl.when(step >= 2 * chunks)(lambda: backward(step - chunks, weight_other))

    @pl.when(step == 3 * chunks - 1)
    def _():
        for copy in late:
            copy.wait()


def feed_forward(
    meta, hidden, cotangent, gated, outs, vectors, packs, ins, ffns, cols=768, row_step=480, after=()
):
    width = hidden.shape[1]
    half = gated[0].shape[1]
    units = ins[0].shape[1]
    chunks = units // cols
    column = pl.BlockSpec((ROWS, cols), lambda i, meta: (0, jnp.minimum(i, 2 * chunks - 1)))

    def part(first, i):
        return jnp.clip(i - first, 0, chunks - 1)

    def across(first, rows):
        return pl.BlockSpec((rows, cols), lambda i, meta: (0, part(first, i)))

    def down(first):
        return pl.BlockSpec((cols, width), lambda i, meta: (part(first, i), 0))

    low = bf16(ROWS, width)
    held = pltpu.VMEM((ROWS, width), BF16)
    wide = pltpu.VMEM((ROWS, width), F32)
    return call(
        "feed_forward",
        partial(ffn_body, chunks, row_step),
        (3 * chunks,),
        32,
        [meta],
        [
            (hidden, own_rows(width)),
            (cotangent, HBM),
            (gated[0], whole(ROWS, half)),
            (gated[1], whole(ROWS, half)),
            (outs[0], whole(half, width)),
            (outs[1], whole(half, width)),
            (vectors, whole(*vectors.shape)),
            (packs[0], across(0, packs[0].shape[0])),
            (packs[1], across(chunks, packs[1].shape[0])),
            (ins[0], across(0, width)),
            (ins[1], across(chunks, width)),
            (ffns[0], down(0)),
            (ffns[1], down(chunks)),
        ],
        [(low, HBM)] * 5
        + [
            (f32(ROWS, width), HBM),
            (f32(ROWS, 128), whole(ROWS, 128)),
            (bf16(ROWS, 2 * units), column),
            (bf16(ROWS, 2 * units), column),
            (bf16(units, width), down(2 * chunks)),
            (f32(8, width), whole(8, width)),
        ],
        scratch=[
            wide,
            wide,
            pltpu.VMEM((ROWS, 2 * units), BF16),
            held,
            held,
            held,
            held,
            held,
            held,
            wide,
            pltpu.SemaphoreType.DMA((7,)),
        ],
        after=after,
    )


def outer_body(left, right, out):
    out[...] = by_rows(left[...], right[...]).astype(BF16)


def outer(left, right, cols, after=(), step=512):
    width = right.shape[1]
    first = cols.start // step
    size = cols.stop - cols.start
    return call(
        "outer",
        outer_body,
        (size // step,),
        5,
        [],
        [
            (left, pl.BlockSpec((ROWS, step), lambda i: (0, i + first))),
            (right, whole(ROWS, width)),
        ],
        [(bf16(size, width), pl.BlockSpec((step, width), lambda i: (i, 0)))],
        after=after,
        vmem=16,
    )[0]


def shrink_body(
    chunks,
    row_step,
    grad_low,
    first_low_hbm,
    before_hbm,
    inner,
    slope,
    weight_in,
    weight_out,
    weight_grad,
    grad_first,
    unit_sums,
    kept,
    total,
    first_low,
    before,
    done,
):
    step = pl.program_id(0)
    fetch_low = pltpu.make_async_copy(first_low_hbm, first_low, done.at[0])
    fetch_before = pltpu.make_async_copy(before_hbm, before, done.at[1])

    @pl.when(step == 0)
    def _():
        fetch_low.start()
        fetch_before.start()

    bias_sum = jnp.zeros((1, inner.shape[1]), F32)
    gate_sum = jnp.zeros((1, inner.shape[1]), F32)
    for block in blocks_of(row_step):
        grad_inner = by_cols(grad_low[block, :], weight_out[...])
        grad_pre = grad_inner * slope[block, :].astype(F32)
        bias_sum += column_sum(grad_pre)
        gate_sum += column_sum(inner[block, :].astype(F32) * grad_inner)
        low = grad_pre.astype(BF16)
        kept[block, :] = low
        back = by_cols(low, weight_in[...])

        @pl.when(step == 0)
        def _(block=block, back=back):
            total[block, :] = back

        @pl.when((step > 0) & (step < chunks - 1))
        def _(block=block, back=back):
            total[block, :] += back

        @pl.when(step == chunks - 1)
        def _(block=block, back=back):
            if block.start == 0:
                fetch_before.wait()
            grad_first[block, :] = total[block, :] + back + before[block, :]

    unit_sums[...] = jnp.zeros_like(unit_sums)
    unit_sums[0:1, :] = bias_sum
    unit_sums[1:2, :] = gate_sum
    pl.when(step == 0)(fetch_low.wait)
    weight_grad[...] = by_rows(first_low[...], kept[...]).astype(BF16)


def shrink(
    side, grad_low, first_low, before, inner, slope, weight_in, weight_out, cols=512, row_step=960, after=()
):
    width, units = weight_in.shape
    chunks = units // cols
    full = whole(ROWS, width)
    across = pl.BlockSpec((width, cols), lambda i: (0, i))
    column = pl.BlockSpec((ROWS, cols), lambda i: (0, i + side * chunks))
    return call(
        "shrink",
        partial(shrink_body, chunks, row_step),
        (chunks,),
        12,
        [],
        [
            (grad_low, full),
            (first_low, HBM),
            (before, HBM),
            (inner, column),
            (slope, column),
            (weight_in, across),
            (weight_out, pl.BlockSpec((cols, width), lambda i: (i, 0))),
        ],
        [
            (bf16(width, units), across),
            (f32(ROWS, width), full),
            (f32(8, units), pl.BlockSpec((8, cols), lambda i: (0, i))),
        ],
        scratch=[
            pltpu.VMEM((ROWS, cols), BF16),
            pltpu.VMEM((ROWS, width), F32),
            pltpu.VMEM((ROWS, width), BF16),
            pltpu.VMEM((ROWS, width), F32),
            pltpu.SemaphoreType.DMA((2,)),
        ],
        after=after,
        vmem=36,
    )


def part_body(
    grad_first, normed_one, spread_one, attn_out, vectors, gated_own, gated_other, grad_one, low, weight_mine, weight_other, sums
):
    gain = row_of(vectors, LN1_GAIN)
    hid_eff = row_of(vectors, HID_EFF)
    totals = [jnp.zeros((1, grad_first.shape[1]), F32)] * 4
    for block in blocks_of(120):
        grad = grad_first[block, :]
        normed = normed_one[block, :].astype(F32)
        one = norm_back(grad, normed, spread_one[block, 0:1], gain)
        grad_one[block, :] = one
        attn = one * hid_eff
        low[block, :] = attn.astype(BF16)
        terms = (attn, grad * normed, grad, one * attn_out[block, :].astype(F32))
        totals = [part + column_sum(term) for part, term in zip(totals, terms, strict=True)]
    sums[...] = jnp.zeros_like(sums)
    for place, part in enumerate(totals):
        sums[place : place + 1, :] = part
    weight_other[...] = by_rows(gated_other[...], low[...]).astype(BF16)
    weight_mine[...] = by_rows(gated_own[...], low[...]).astype(BF16)


def part_norm(grad_first, normed_one, spread_one, attn_out, vectors, gated, after=()):
    width = grad_first.shape[1]
    half = gated[0].shape[1]
    values = [grad_first, normed_one, spread_one, attn_out, vectors, *gated]
    made = [
        f32(ROWS, width),
        bf16(ROWS, width),
        bf16(half, width),
        bf16(half, width),
        f32(8, width),
    ]
    return call(
        "part_norm",
        part_body,
        (1,),
        6,
        [],
        [(value, whole(*value.shape)) for value in values],
        [(shape, whole(*shape.shape)) for shape in made],
        after=after,
        vmem=28,
    )


def part_heads_body(
    head_width, low, gated_own, gated_other, out_own, out_other, pack_own, pack_other, context_own, context_other, means_own, means_other, sums
):
    half = gated_own.shape[1]
    head = lax.broadcasted_iota(jnp.int32, (8, half), 1) // head_width
    pick = (head == lax.broadcasted_iota(jnp.int32, (8, half), 0)).astype(BF16)
    sums[...] = jnp.zeros_like(sums)
    for place, (gated, weight, pack, context, means) in enumerate(
        (
            (gated_own, out_own, pack_own, context_own, means_own),
            (gated_other, out_other, pack_other, context_other, means_other),
        )
    ):
        column = jnp.zeros((1, half), F32)
        for start, size in BUCKETS:
            rows = slice(start, start + size)
            grads = by_cols(low[rows, :], weight[...])
            context[rows, :] = (grads * pack[PACK_HEAD : PACK_HEAD + 1, 0:half]).astype(BF16)
            terms = grads * gated[rows, :].astype(F32)
            column += column_sum(terms)
            high = terms.astype(BF16)
            rest = (terms - high.astype(F32)).astype(BF16)
            means[:, rows] = by_cols(pick, high) + by_cols(pick, rest)
        sums[place : place + 1, :] = column


def part_heads(low, gated, outs, packs, head_width, after=()):
    half = gated[0].shape[1]
    values = [low, *gated, *outs, *packs]
    made = [
        bf16(ROWS, half),
        bf16(ROWS, half),
        f32(8, ROWS),
        f32(8, ROWS),
        f32(8, half),
    ]
    return call(
        "part_heads",
        partial(part_heads_body, head_width),
        (1,),
        5,
        [],
        [(value, whole(*value.shape)) for value in values],
        [(shape, whole(*shape.shape)) for shape in made],
        after=after,
        vmem=28,
    )


def add_back_body(start, *refs):
    grads, weights, out = refs[:6], refs[6:12], refs[12]
    total = start[...]
    for side in (0, 3):
        left = jnp.concatenate([part[...] for part in grads[side : side + 3]], 1)
        right = jnp.concatenate([part[...] for part in weights[side : side + 3]], 1)
        total += by_cols(left, right)
    out[...] = total


def add_back(start, grads, weights, after=()):
    width = start.shape[1]
    half = grads[0].shape[1]
    step = ROWS // 4
    return call(
        "add_back",
        add_back_body,
        (4,),
        6,
        [],
        [(start, pl.BlockSpec((step, width), lambda i: (i, 0)))]
        + [(part, pl.BlockSpec((step, half), lambda i: (i, 0))) for part in grads]
        + [(part, whole(width, half)) for part in weights],
        [(f32(ROWS, width), pl.BlockSpec((step, width), lambda i: (i, 0)))],
        after=after,
        vmem=24,
    )[0]


def swap_bit(values, dp_size, bit):
    return lax.ppermute(values, "dp", [(at, at ^ (1 << bit)) for at in range(dp_size)])


TAIL = 128


def load(ref, rows, tail):
    values = ref[rows, :].astype(F32)
    if not tail:
        return values, None
    cut = values.shape[1] - TAIL
    return values[:, :cut], values[:, cut : cut + TAIL // 2] + values[:, cut + TAIL // 2 :]


def store(ref, main, extra):
    if extra is None:
        ref[...] = main.astype(ref.dtype)
        return
    cut = main.shape[1]
    high = extra.astype(BF16)
    ref[:, :cut] = main.astype(BF16)
    ref[:, cut : cut + TAIL // 2] = high
    ref[:, cut + TAIL // 2 :] = (extra - high.astype(F32)).astype(BF16)


def split_by(side, totals, kept, sent):
    for part, total in enumerate(totals):

        @pl.when(side == part)
        def _(total=total):
            store(kept, *total)

        @pl.when(side != part)
        def _(total=total):
            store(sent, *total)


def add(left, right):
    return tuple(None if a is None else a + b for a, b in zip(left, right, strict=True))


class Stream:
    def __init__(self, ins, shape, first, order, tail=False):
        self.ins = ins
        self.rows, self.cols = shape
        self.first = first
        self.order = order
        self.tail = tail
        self.stage = 0
        self.kept = self.value = self.arrived = None

    def job(self):
        stages = len(self.order)
        stage, tail = self.stage, self.tail
        size = self.rows >> stage if stage <= stages else self.value.shape[0]
        if stage < stages:
            half = size // 2
            ins = list(self.ins) if stage == 0 else [self.kept, self.arrived]

            def body(sides, *refs):
                *given, kept, sent = refs
                totals = []
                for at in (0, half):
                    rows = slice(at, at + half)
                    if stage == 0:
                        totals.append(self.first(given, rows))
                    else:
                        totals.append(add(*[load(ref, rows, tail) for ref in given]))
                split_by(sides[self.order[stage]], totals, kept, sent)

            return ins, [bf16(half, self.cols)] * 2, body
        if stage == stages:

            def body(sides, kept, arrived, value):
                rows = slice(0, size)
                store(value, *add(load(kept, rows, tail), load(arrived, rows, tail)))

            return [self.kept, self.arrived], [bf16(size, self.cols)], body
        bit = self.order[2 * stages - stage]

        def body(sides, own, arrived, value):
            for first, halves in in_order(sides[bit], own, arrived):

                @pl.when(first)
                def _(halves=halves):
                    for place, half in enumerate(halves):
                        value[place * size : place * size + size, :] = half[...]

        return [self.value, self.arrived], [bf16(2 * size, self.cols)], body

    def take(self, outs, dp_size):
        stages = len(self.order)
        if self.stage < stages:
            self.kept, sent = outs
            self.arrived = swap_bit(sent, dp_size, self.order[self.stage])
        else:
            (self.value,) = outs
            bit = self.order[2 * stages - 1 - self.stage]
            self.arrived = swap_bit(self.value, dp_size, bit)
        self.stage += 1

    def last(self):
        return self.stage == 2 * len(self.order)


class Gather:
    def __init__(self, streams, order):
        self.streams = streams
        self.order = order
        self.stage = 0
        self.value = self.arrived = None

    def job(self):
        stage = self.stage
        if stage == 0:
            ins = [part for stream in self.streams for part in (stream.kept, stream.arrived)]
            size = self.streams[0].kept.shape[0]

            def body(sides, *refs):
                *given, value = refs
                at = 0
                for kept, arrived in zip(given[::2], given[1::2], strict=True):
                    rows, cols = slice(0, size), slice(at, at + kept.shape[1])
                    value[:, cols] = add(load(kept, rows, False), load(arrived, rows, False))[
                        0
                    ].astype(BF16)
                    at = cols.stop

            cols = sum(stream.cols for stream in self.streams)
            return ins, [bf16(size, cols)], body
        size, cols = self.value.shape

        def body(sides, own, arrived, value):
            for first, halves in in_order(sides[self.order[stage - 1]], own, arrived):

                @pl.when(first)
                def _(halves=halves):
                    for place, half in enumerate(halves):
                        value[place * size : place * size + size, :] = half[...]

        return [self.value, self.arrived], [bf16(2 * size, cols)], body

    def take(self, outs, dp_size):
        (self.value,) = outs
        self.arrived = swap_bit(self.value, dp_size, self.order[self.stage])
        self.stage += 1

    def last(self):
        return self.stage == len(self.order)


def in_order(side, own, arrived):
    return (side == 0, (own, arrived)), (side == 1, (arrived, own))


def small_call(name, body, ins, outs, sides, after=()):
    return call(
        name,
        body,
        (1,),
        2,
        [sides],
        [(value, whole(*value.shape)) for value in ins],
        [(shape, whole(*shape.shape)) for shape in outs],
        after=after,
        vmem=24,
    )


def advance(streams, dp_size, sides, after=()):
    jobs = [stream.job() for stream in streams]
    ins = [value for job in jobs for value in job[0]]
    outs = [shape for job in jobs for shape in job[1]]

    def body(sides, *refs):
        given, made = refs[: len(ins)], refs[len(ins) :]
        for inputs, shapes, work in jobs:
            work(sides, *given[: len(inputs)], *made[: len(shapes)])
            given, made = given[len(inputs) :], made[len(shapes) :]

    found = small_call("advance", body, ins, outs, sides, after)
    for stream, job in zip(streams, jobs, strict=True):
        stream.take(found[: len(job[1])], dp_size)
        found = found[len(job[1]) :]


def states(streams):
    return [stream.kept if stream.value is None else stream.value for stream in streams]


def blocks_in(gather):
    streams, order = gather.streams, gather.order
    bits = len(order)
    size = streams[0].rows >> bits
    for block in range(1 << bits):
        device = sum((block >> turn & 1) << bit for turn, bit in enumerate(order))
        half, inside = divmod(block, 1 << (bits - 1))
        places = [
            size
            * sum((device >> bit & 1) << (bits - 1 - turn) for turn, bit in enumerate(stream.order))
            for stream in streams
        ]
        yield half, slice(inside * size, (inside + 1) * size), places, size


def finish(gather, sides, after=()):
    rows, cols = gather.streams[0].rows, gather.streams[0].cols

    def body(sides, own, arrived, out):
        for first, halves in in_order(sides[gather.order[-1]], own, arrived):

            @pl.when(first)
            def _(halves=halves):
                for half, where, places, size in blocks_in(gather):
                    for at, place in enumerate(places):
                        row = at * rows + place
                        out[row : row + size, :] = halves[half][
                            where, at * cols : (at + 1) * cols
                        ].astype(F32)

    ins = [gather.value, gather.arrived]
    outs = [f32(rows * len(gather.streams), cols)]
    return small_call("finish", body, ins, outs, sides, after)[0]


def finish_in(gathers, sides, depth, after=()):
    streams = [gather.streams[0] for gather in gathers]
    rows, cols = streams[1].rows, streams[1].cols

    def body(sides, *refs):
        *given, in_out, out_out = refs
        for at, gather in enumerate(gathers):
            pair = given[2 * at : 2 * at + 2]
            for first, halves in in_order(sides[gather.order[-1]], *pair):

                @pl.when(first)
                def _(at=at, gather=gather, halves=halves):
                    for half, where, (row,), size in blocks_in(gather):
                        in_out[row : row + size, at * cols : (at + 1) * cols] = halves[half][
                            where, 0:cols
                        ].astype(F32)
                        if at == 0:
                            side = row // depth
                            line = row - side * depth
                            out_out[line : line + size, side * depth : (side + 1) * depth] = halves[
                                half
                            ][where, cols : cols + depth].astype(F32)

    ins = [value for gather in gathers for value in (gather.value, gather.arrived)]
    outs = [f32(rows, 2 * cols), f32(depth, rows)]
    return small_call("finish_in", body, ins, outs, sides, after)


def orders_of(dp_size):
    bits = dp_size.bit_length() - 1
    if bits == 4:
        plain = (0, 1, 2, 3), (1, 0, 2, 3)
        return *plain, (2, 0, 1, 3), (0, 2, 3, 1), (0, 1, 2, 3), (1, 0, 2, 3), (1, 3, 2, 0), (3, 1, 0, 2), (1, 3, 2, 0)
    return tuple(tuple((at + turn) % bits for at in range(bits)) for turn in range(9))


def late_streams(qkv, small, orders):
    rows, cols = qkv[0].shape
    cut = -(-(cols + TAIL) // 256) * 128
    places = small[0].shape[1] // (TAIL // 2)
    depth = small[0].shape[0]

    def front(given, where):
        return sum(ref[where, 0:cut].astype(F32) for ref in given), None

    def back(given, where):
        first, size = where.start, where.stop - where.start
        main = sum(ref[where, cut:cols].astype(F32) for ref in given[0:2])
        extra = []
        for place in range(first // depth, (first + size) // depth):
            if place < places:
                at = slice(place * TAIL // 2, (place + 1) * TAIL // 2)
                extra.append(sum(ref[:, at] for ref in given[2:4]))
        used = depth * len(extra)
        if used < size:
            extra.append(jnp.zeros((size - used, TAIL // 2), F32))
        return main, jnp.concatenate(extra, 0)

    return [
        Stream(qkv, (rows, cut), front, orders[0]),
        Stream((*qkv, *small), (rows, cols - cut + TAIL), back, orders[1], True),
    ]


def finish_late(streams, sides, lanes, small_shape, after=()):
    front, back = streams
    rows = front.rows
    size = rows // 2
    depth, width = small_shape
    cut = front.cols
    half = (cut + back.cols - TAIL) // 3
    places = width // (TAIL // 2)

    def body(sides, own0, arrived0, own1, arrived1, qkv_out, small_out):
        def qkv_part(values, which, first, cols):
            for at in range(0, cols, lanes):
                pair, kind = divmod((first + at) // lanes, 3)
                columns = slice(pair * lanes, (pair + 1) * lanes)
                qkv_out[which * size : (which + 1) * size, kind, columns] = values[
                    :, at : at + lanes
                ].astype(F32)

        for first, halves in in_order(sides[front.order[0]], own0, arrived0):

            @pl.when(first)
            def _(halves=halves):
                for which, values in enumerate(halves):
                    qkv_part(values, which, 0, cut)

        for first, halves in in_order(sides[back.order[0]], own1, arrived1):

            @pl.when(first)
            def _(halves=halves):
                for which, values in enumerate(halves):
                    qkv_part(values, which, cut, back.cols - TAIL)
                    for place in range(which * size // depth, (which + 1) * size // depth):
                        if place < places:
                            at = place * depth - which * size
                            _, extra = load(values, slice(at, at + depth), True)
                            small_out[:, place * TAIL // 2 : (place + 1) * TAIL // 2] = extra

    ins = [front.value, front.arrived, back.value, back.arrived]
    outs = [f32(rows, 3, half), f32(depth, width)]
    return small_call("finish_late", body, ins, outs, sides, after)


def pack_sums(part_sums, turn_sums, head_sums, bias_sums, unit_sums):
    width = part_sums.shape[1]
    half = bias_sums[0].shape[1]
    unit_rows = unit_sums[0].shape[1] // width

    def body(part, turned, heads, bias_own, bias_other, unit_own, unit_other, mine, theirs):
        sides = ((mine, bias_own, unit_own), (theirs, bias_other, unit_other))
        for side, (out, bias, unit) in enumerate(sides):
            out[...] = jnp.zeros_like(out)
            out[0:4, :] = part[0:4, :]
            out[4:8, :] = turned[0:4, :]
            out[8:9, 0:half] = bias[0:1, :]
            out[8:9, half : 2 * half] = bias[1:2, :]
            out[9:10, 0:half] = heads[side : side + 1, :]
            for kind in (0, 1):
                for row in range(unit_rows):
                    place = 10 + kind * unit_rows + row
                    out[place : place + 1, :] = unit[
                        kind : kind + 1, row * width : (row + 1) * width
                    ]

    values = [part_sums, turn_sums, head_sums, *bias_sums, *unit_sums]
    rows = -(-(10 + 2 * unit_rows) // 8) * 8
    return call(
        "pack_sums",
        body,
        (1,),
        1,
        [],
        [(value, whole(*value.shape)) for value in values],
        [(f32(rows, width), whole(rows, width))] * 2,
        vmem=24,
    )


def per_device(
    dp_size,
    hidden,
    cotangent,
    counts,
    lengths,
    qkv_weight,
    qv_bias,
    out_weight,
    out_bias,
    ln1_gain,
    ln1_bias,
    in_weight,
    in_bias,
    ffn_out_weight,
    ffn_out_bias,
    ln2_gain,
    ln2_bias,
    head_gate,
    head_mask,
    ffn_gate,
    ffn_mask,
    hidden_gate,
    hidden_mask,
):
    width = hidden.shape[1]
    own_heads = head_gate.shape[0]
    half = qkv_weight.shape[2]
    units = in_weight.shape[1]
    head_width = half // own_heads
    head_at = lax.axis_index("head")

    def other(values):
        return lax.ppermute(values, "head", [(0, 1), (1, 0)])

    def pad_to(values, size):
        return jnp.pad(values, (0, size - values.shape[0]))

    meta = jnp.concatenate(
        [
            lax.dynamic_index_in_dim(
                jnp.where(counts[0] > 0, lengths[0], 0), head_at, 0, keepdims=False
            ),
            head_at[None],
        ]
    )
    head_flags = head_mask.astype(F32)
    ffn_flags = ffn_mask.astype(F32)
    hidden_flags = hidden_mask.astype(F32)
    pack = jnp.stack(
        [
            in_bias,
            ffn_gate * ffn_flags,
            pad_to(qv_bias.reshape(-1), units),
            pad_to(jnp.repeat(head_gate * head_flags, head_width), units),
        ]
    )
    vectors = jnp.stack(
        [
            out_bias,
            ln1_gain,
            ln1_bias,
            ffn_out_bias,
            ln2_gain,
            ln2_bias,
            hidden_gate * hidden_flags,
        ]
    )
    qkv_own = [qkv_weight[:, at] for at in range(3)]
    qkv_other = [other(part) for part in qkv_own]
    packs = (pack, other(pack))
    outs = (out_weight, other(out_weight))
    ins = (in_weight, other(in_weight))
    ffns = (ffn_out_weight, other(ffn_out_weight))
    sides = jnp.stack([(lax.axis_index("dp") >> bit) & 1 for bit in range(dp_size.bit_length() - 1)])
    orders = orders_of(dp_size)
    step = partial(advance, dp_size=dp_size, sides=sides)

    def halves(size, at):
        return slice(at * size // 2, (at + 1) * size // 2)

    def sum_stream(left, right, order, rows=None, cols=None):
        rows = rows or slice(0, left.shape[0])
        cols = cols or slice(0, left.shape[1])

        def first(given, at):
            at = slice(rows.start + at.start, rows.start + at.stop)
            return sum(ref[at, cols].astype(F32) for ref in given), None

        shape = (rows.stop - rows.start, cols.stop - cols.start)
        return Stream((left, right), shape, first, order)

    *qkv0, gated0, logs0 = attend(meta, hidden, qkv_own, packs[0], head_width)
    *qkv1, gated1, logs1 = attend(meta, hidden, qkv_other, packs[1], head_width, [gated0])
    gated = (gated0, gated1)
    (
        layer_out,
        first_low,
        normed_one,
        attn_out,
        grad_low,
        grad_two,
        spread_one,
        inner,
        slope,
        ffn_grad_other,
        turn_sums,
    ) = feed_forward(meta, hidden, cotangent, gated, outs, vectors, packs, ins, ffns)
    ffn_grad_theirs = other(ffn_grad_other)
    ffn_grad_mine = outer(inner, grad_low, slice(0, units))
    streams = [
        sum_stream(ffn_grad_mine, ffn_grad_theirs, orders[at], rows=halves(units, at))
        for at in (0, 1)
    ]
    step(streams)
    in_grad_other, grad_first, unit_sums1 = shrink(
        1, grad_low, first_low, grad_two, inner, slope, ins[1], ffns[1], after=states(streams)
    )
    in_grad_theirs = other(in_grad_other)
    step(streams, after=[grad_first])
    in_grad_mine, grad_first, unit_sums0 = shrink(
        0, grad_low, first_low, grad_first, inner, slope, ins[0], ffns[0], after=states(streams)
    )
    step(streams, after=[grad_first])
    grad_one, attn_low, out_grad_mine, out_grad_other, part_sums = part_norm(
        grad_first,
        normed_one,
        spread_one,
        attn_out,
        vectors,
        gated,
        after=states(streams),
    )
    out_grad_theirs = other(out_grad_other)
    grad_context0, grad_context1, means0, means1, head_sums = part_heads(
        attn_low, gated, outs, packs, head_width
    )

    def in_and_out(given, at):
        side = at.start // half
        lines = slice(at.start - side * half, at.stop - side * half)
        left = sum(ref[at, 0 : units // 2].astype(F32) for ref in given[0:2])
        right = sum(
            ref[lines, side * half : (side + 1) * half].astype(F32) for ref in given[2:4]
        )
        return jnp.concatenate([left, right], 1), None

    in_streams = [
        Stream(
            (in_grad_mine, in_grad_theirs, out_grad_mine, out_grad_theirs),
            (width, units // 2 + half),
            in_and_out,
            orders[2],
        ),
        sum_stream(in_grad_mine, in_grad_theirs, orders[3], cols=halves(units, 1)),
    ]
    streams += in_streams
    step(streams, after=[grad_context0])
    *mixed1, qkv_grad_other, bias_sums1 = attend_back(
        meta,
        hidden,
        qkv1,
        grad_context1,
        logs1,
        means1,
        packs[1],
        head_width,
        after=states(streams),
    )
    qkv_grad_theirs = other(qkv_grad_other)
    ffn_gather = Gather(streams[:2], orders[6])
    streams = [ffn_gather, *streams[2:]]
    step(streams, after=[mixed1[0]])
    *mixed0, qkv_grad_mine, bias_sums0 = attend_back(
        meta,
        hidden,
        qkv0,
        grad_context0,
        logs0,
        means0,
        packs[0],
        head_width,
        after=states(streams) + [mixed1[0]],
    )
    small = pack_sums(
        part_sums, turn_sums, head_sums, (bias_sums0, bias_sums1), (unit_sums0, unit_sums1))
    late = late_streams(
        (qkv_grad_mine, qkv_grad_theirs), (small[0], other(small[1])), orders[4:6]
    )
    step([*streams, *late], after=[mixed0[0]])
    grad_hidden = add_back(
        grad_one, mixed0 + mixed1, qkv_own + qkv_other, after=states(streams + late)
    )
    step([ffn_gather, *in_streams, *late], after=[grad_hidden])
    gathers = [Gather(in_streams[at : at + 1], orders[7 + at]) for at in (0, 1)]

    step([ffn_gather, *gathers, *late])
    step([*gathers, *late])
    step([*gathers, *late])
    grad_ffn_out_weight = finish(ffn_gather, sides)
    step([*gathers, *late], after=[grad_ffn_out_weight])
    step(late)
    while not late[0].last():
        step(late)
    grad_in_weight, grad_out_weight = finish_in(gathers, sides, half)
    grad_qkv_weight, small = finish_late(late, sides, 2 * head_width, small[0].shape)
    (
        grad_out_bias,
        grad_ln1_gain,
        grad_ln1_bias,
        gate_one,
        grad_ffn_out_bias,
        grad_ln2_gain,
        grad_ln2_bias,
        gate_two,
    ) = small[:8]
    unit_rows = units // width
    return (
        layer_out,
        grad_hidden,
        grad_qkv_weight,
        small[8].reshape(2, half),
        grad_out_weight,
        grad_out_bias,
        grad_ln1_gain,
        grad_ln1_bias,
        grad_in_weight,
        small[10 : 10 + unit_rows].reshape(-1),
        grad_ffn_out_weight,
        grad_ffn_out_bias,
        grad_ln2_gain,
        grad_ln2_bias,
        jnp.sum(small[9, :half].reshape(own_heads, head_width), 1) * head_flags / head_gate,
        small[10 + unit_rows : 10 + 2 * unit_rows].reshape(-1) * ffn_flags / ffn_gate,
        (gate_one + gate_two) * hidden_flags,
    )


def solution(mesh):
    placed = (
        P("dp", None),
        P("dp", None),
        P("dp", None, None),
        P("dp", None, None),
        P(None, None, "head"),
        P(None, "head"),
        P("head", None),
        P(),
        P(),
        P(),
        P(None, "head"),
        P("head"),
        P("head", None),
        P(),
        P(),
        P(),
        P("head"),
        P("head"),
        P("head"),
        P("head"),
        P(),
        P(),
    )
    return jax.shard_map(
        partial(per_device, mesh.shape["dp"]),
        mesh=mesh,
        in_specs=placed,
        out_specs=(
            P(("dp", "head"), None),
            P(("dp", "head"), None),
            P(None, None, "head"),
            P(None, "head"),
            P("head", None),
            P(),
            P(),
            P(),
            P(None, "head"),
            P("head"),
            P("head", None),
            P(),
            P(),
            P(),
            P("head"),
            P("head"),
            P(),
        ),
        check_vma=False,
    )
```

```python
from functools import partial

import jax
import jax.numpy as jnp
from jax import lax
from jax.experimental import pallas as pl
from jax.experimental.pallas import tpu as pltpu
from jax.sharding import PartitionSpec as P

BASE = 64
ROWS = 15 * BASE
EPSILON = 1e-12
MASKED = -1e9
LOG2E = 1.4426950408889634
BUCKETS = ((0, 8 * BASE), (8 * BASE, 4 * BASE), (12 * BASE, 2 * BASE), (14 * BASE, BASE))
F32 = jnp.float32
BF16 = jnp.bfloat16
MEBI = 1 << 20
HBM = pl.BlockSpec(memory_space=pl.ANY)


def dot(left, right):
    return jnp.dot(left, right, preferred_element_type=F32)


def by_rows(left, right):
    return lax.dot_general(left, right, (((0,), (0,)), ((), ())), preferred_element_type=F32)


def by_cols(left, right):
    return lax.dot_general(left, right, (((1,), (1,)), ((), ())), preferred_element_type=F32)


def f32(*shape):
    return jax.ShapeDtypeStruct(shape, F32)


def bf16(*shape):
    return jax.ShapeDtypeStruct(shape, BF16)


def whole(*shape):
    return pl.BlockSpec(shape, lambda *_: (0,) * len(shape))


def call(name, body, grid, micros, scalars, ins, outs, scratch=(), after=(), vmem=58):
    first = len(scalars) + len(ins)

    def run(*refs):
        body(*refs[:first], *refs[first + len(after) :])

    return pl.pallas_call(
        run,
        grid_spec=pltpu.PrefetchScalarGridSpec(
            num_scalar_prefetch=len(scalars),
            grid=grid,
            in_specs=[spec for _, spec in ins] + [HBM] * len(after),
            out_specs=[spec for _, spec in outs],
            scratch_shapes=list(scratch),
        ),
        out_shape=[shape for shape, _ in outs],
        compiler_params=pltpu.CompilerParams(
            dimension_semantics=("arbitrary",) * len(grid), vmem_limit_bytes=vmem * MEBI
        ),
        cost_estimate=pl.CostEstimate(
            flops=int(micros * 5e9), bytes_accessed=1 << 20, transcendentals=0
        ),
        name=name,
    )(*scalars, *[value for value, _ in ins], *after)


def row_of(vectors, at):
    return vectors[at : at + 1, :]


def column_sum(values):
    return jnp.sum(values, 0, keepdims=True)


def own_rows(width):
    return pl.BlockSpec((ROWS, width), lambda i, meta: (meta[4], 0))


PACK_IN_BIAS, PACK_FFN, PACK_QV, PACK_HEAD = range(4)


def side_masks(lanes):
    low = lax.broadcasted_iota(jnp.int32, (1, lanes), 1) < lanes // 2
    return low, low.astype(BF16), 1 - low.astype(BF16)


def kept_head(gate, side):
    half = gate.shape[1] // 2
    return jnp.max(gate[PACK_HEAD : PACK_HEAD + 1, side * half : (side + 1) * half]) > 0


def for_kept(gate, run):
    flags = [kept_head(gate, side) for side in (0, 1)]
    for sides in ((0, 1), (0,), (1,), ()):
        case = [flags[side] if side in sides else jnp.logical_not(flags[side]) for side in (0, 1)]
        pl.when(case[0] & case[1])(partial(run, sides))


def attend_body(
    pairs, lanes, meta, hidden, weight_q, weight_k, weight_v, bias_q, bias_v, gate, query, key, value, gated, logs, columns, context
):
    pair = pl.program_id(0)
    weight = jnp.concatenate([weight_q[...], weight_k[...], weight_v[...]], 1)
    mixed = dot(hidden[...], weight)
    query[...] = (mixed[:, :lanes] + bias_q[PACK_QV : PACK_QV + 1, :]).astype(BF16)
    key[...] = mixed[:, lanes : 2 * lanes].astype(BF16)
    value[...] = (mixed[:, 2 * lanes :] + bias_v[PACK_QV : PACK_QV + 1, :]).astype(BF16)
    scale = LOG2E * (lanes // 2) ** -0.5
    low_side, *masks = side_masks(lanes)
    lane = lax.broadcasted_iota(jnp.int32, (1, 128), 1)

    def run(sides):
        for place, (start, size) in enumerate(BUCKETS):
            rows = slice(start, start + size)
            seen = lax.broadcasted_iota(jnp.int32, (1, size), 1) < meta[place]
            shut = jnp.where(seen, 0.0, MASKED).astype(F32)
            queries, keys, values = query[rows, :], key[rows, :], value[rows, :]
            total_context = jnp.zeros((size, lanes), F32)
            column = columns[rows, :]
            for side in sides:
                scores = by_cols(queries * masks[side], keys) + shut
                top = jnp.max(scores, -1, keepdims=True)
                power = jnp.exp2((scores - top) * scale)
                total = jnp.sum(power, -1, keepdims=True)
                found = dot(power.astype(BF16), values) * (1.0 / total)
                log = top * scale + jnp.log2(total)
                column = jnp.where(lane == 2 * pair + side, log, column)
                total_context = jnp.where(low_side == (side == 0), found, total_context)
            columns[rows, :] = column
            context[rows, :] = total_context

    for_kept(gate, run)
    gated[...] = (context[...] * gate[PACK_HEAD : PACK_HEAD + 1, :]).astype(BF16)

    @pl.when(pair == pairs - 1)
    def _():
        for start, size in BUCKETS:
            rows = slice(start, start + size)
            logs[:, rows] = columns[rows, :].T[0:8, :]


def attend(meta, hidden, weights, pack, head_width, after=()):
    width, half = weights[0].shape
    lanes = 2 * head_width
    pairs = half // lanes
    column = pl.BlockSpec((ROWS, lanes), lambda i, meta: (0, i))
    weight = pl.BlockSpec((width, lanes), lambda i, meta: (0, i))

    def vector(shift):
        return pl.BlockSpec((pack.shape[0], lanes), lambda i, meta: (0, i + shift))

    return call(
        "attend",
        partial(attend_body, pairs, lanes),
        (pairs,),
        9,
        [meta],
        [(hidden, own_rows(width))]
        + [(part, weight) for part in weights]
        + [(pack, vector(0)), (pack, vector(pairs)), (pack, vector(0))],
        [(bf16(ROWS, half), column)] * 4 + [(f32(8, ROWS), whole(8, ROWS))],
        scratch=[pltpu.VMEM((ROWS, 128), F32), pltpu.VMEM((ROWS, lanes), F32)],
        after=after,
        vmem=58,
    )


def pick_row(values, at):
    place = lax.broadcasted_iota(jnp.int32, values.shape, 0)
    return column_sum(jnp.where(place == at, values, 0.0))


def attend_back_body(
    lanes, meta, hidden, query, key, value, grad_context, logs, means, gate, grad_q, grad_k, grad_v, weight_grad, bias_sums, *totals
):
    pair = pl.program_id(0)
    scale = LOG2E * (lanes // 2) ** -0.5
    final = (lanes // 2) ** -0.5
    _, *masks = side_masks(lanes)

    def run(sides):
        for place, (start, size) in enumerate(BUCKETS):
            rows = slice(start, start + size)
            seen = lax.broadcasted_iota(jnp.int32, (size, 1), 0) < meta[place]
            shut = jnp.where(seen, 0.0, MASKED).astype(F32)
            queries, keys, values = query[rows, :], key[rows, :], value[rows, :]
            grads = grad_context[rows, :]
            sums = [jnp.zeros((size, lanes), F32)] * 3
            for side in sides:
                log = pick_row(logs[:, rows], 2 * pair + side)
                mean = pick_row(means[:, rows], 2 * pair + side)
                side_queries = queries * masks[side]
                side_grads = grads * masks[side]
                scores = by_cols(keys, side_queries) + shut
                weights = jnp.exp2(scores * scale - log)
                change = (weights * (by_cols(values, side_grads) - mean)).astype(BF16)
                terms = (
                    by_rows(change, keys * masks[side]),
                    dot(change, side_queries),
                    dot(weights.astype(BF16), side_grads),
                )
                sums = [part + term for part, term in zip(sums, terms, strict=True)]
            for total, part in zip(totals, sums, strict=True):
                total[rows, :] = part

    for_kept(gate, run)
    grad_query = totals[0][...] * final
    grad_q[...] = grad_query.astype(BF16)
    grad_k[...] = (totals[1][...] * final).astype(BF16)
    grad_v[...] = totals[2][...].astype(BF16)
    query_sum = column_sum(grad_query)
    value_sum = column_sum(totals[2][...])
    grads = jnp.concatenate([grad_q[...], grad_k[...], grad_v[...]], 1)
    weight_grad[...] = by_rows(hidden[...], grads).astype(BF16)
    bias_sums[...] = jnp.zeros_like(bias_sums)
    bias_sums[0:1, :] = query_sum
    bias_sums[1:2, :] = value_sum


def attend_back(meta, hidden, parts, grad_context, logs, means, pack, head_width, after=()):
    half = grad_context.shape[1]
    width = hidden.shape[1]
    lanes = 2 * head_width
    pairs = half // lanes
    column = pl.BlockSpec((ROWS, lanes), lambda i, meta: (0, i))
    return call(
        "attend_back",
        partial(attend_back_body, lanes),
        (pairs,),
        11,
        [meta],
        [(hidden, own_rows(width))]
        + [(part, column) for part in (*parts, grad_context)]
        + [(logs, whole(8, ROWS)), (means, whole(8, ROWS))]
        + [(pack, pl.BlockSpec((pack.shape[0], lanes), lambda i, meta: (0, i)))],
        [(bf16(ROWS, half), column)] * 3
        + [
            (
                bf16(width, 3 * half),
                pl.BlockSpec((width, 3 * lanes), lambda i, meta: (0, i)),
            ),
            (f32(8, half), pl.BlockSpec((8, lanes), lambda i, meta: (0, i))),
        ],
        scratch=[pltpu.VMEM((ROWS, lanes), F32)] * 3,
        after=after,
        vmem=24,
    )


(OUT_BIAS, LN1_GAIN, LN1_BIAS, FFN_OUT_BIAS, LN2_GAIN, LN2_BIAS, HID_EFF) = range(7)


def valid_column(meta):
    at = lax.broadcasted_iota(jnp.int32, (ROWS, 1), 0)
    found = jnp.zeros((ROWS, 1), F32)
    for place, (start, size) in enumerate(BUCKETS):
        found = jnp.where((at >= start) & (at < start + meta[place]), 1.0, found)
    return found


def norm_stats(resid):
    centred = resid - jnp.mean(resid, -1, keepdims=True)
    spread = lax.rsqrt(jnp.mean(centred * centred, -1, keepdims=True) + EPSILON)
    return (centred * spread, spread)


def norm_back(grad_out, normed, spread, gain):
    grad_normed = grad_out * gain
    first_mean = jnp.mean(grad_normed, -1, keepdims=True)
    second_mean = jnp.mean(grad_normed * normed, -1, keepdims=True)
    return spread * (grad_normed - first_mean - normed * second_mean)


def blocks_of(step):
    return [slice(at, at + step) for at in range(0, ROWS, step)]


def gelu_and_slope(z):
    below = 0.5 + 0.5 * lax.erf(z * 0.5**0.5)
    density = jnp.exp2((-0.5 * LOG2E) * (z * z)) * (0.5 / 3.141592653589793) ** 0.5
    return (z * below, below + z * density)


def ffn_body(
    chunks,
    row_step,
    meta,
    hidden,
    cotangent_all,
    gated_own,
    gated_other,
    out_own,
    out_other,
    vectors,
    pack_own,
    pack_other,
    in_own,
    in_other,
    ffn_own,
    ffn_other,
    layer_out_hbm,
    first_low_hbm,
    normed_hbm,
    attn_hbm,
    grad_low_hbm,
    grad_two_hbm,
    spread_one,
    inner_out,
    slope_out,
    weight_other,
    sums,
    first,
    total,
    inner,
    cotangent,
    layer_out,
    first_low,
    normed_one,
    attn_out,
    grad_low,
    grad_two,
    done,
):
    step = pl.program_id(0)
    cols = inner_out.shape[1]
    early = ((first_low, first_low_hbm), (normed_one, normed_hbm), (attn_out, attn_hbm))
    late = ((layer_out, layer_out_hbm), (grad_low, grad_low_hbm), (grad_two, grad_two_hbm))
    early = [pltpu.make_async_copy(*pair, done.at[at]) for at, pair in enumerate(early)]
    late = [pltpu.make_async_copy(*pair, done.at[3 + at]) for at, pair in enumerate(late)]
    mine = pl.ds(pl.multiple_of(meta[4] * ROWS, ROWS), ROWS)
    fetch = pltpu.make_async_copy(cotangent_all.at[mine, :], cotangent, done.at[6])

    @pl.when(step == 0)
    def _():
        fetch.start()
        for block in blocks_of(240):
            attn = (
                dot(gated_own[block, :], out_own[...])
                + dot(gated_other[block, :], out_other[...])
                + row_of(vectors, OUT_BIAS)
            )
            attn_out[block, :] = attn.astype(BF16)
            normed, spread = norm_stats(
                hidden[block, :].astype(F32) + attn * row_of(vectors, HID_EFF)
            )
            normed_one[block, :] = normed.astype(BF16)
            spread_one[block, :] = jnp.broadcast_to(spread, (240, 128))
            value = normed * row_of(vectors, LN1_GAIN) + row_of(vectors, LN1_BIAS)
            first[block, :] = value
            first_low[block, :] = value.astype(BF16)
            total[block, :] = jnp.broadcast_to(row_of(vectors, FFN_OUT_BIAS), value.shape)
        for copy in early:
            copy.start()

    def forward(pack, weight_in, weight_out):
        bias = pack[PACK_IN_BIAS : PACK_IN_BIAS + 1, :]
        eff = pack[PACK_FFN : PACK_FFN + 1, :]
        at = pl.multiple_of(step * cols, cols)
        for block in blocks_of(row_step):
            pre = dot(first_low[block, :], weight_in[...]) + bias
            value, slope = gelu_and_slope(pre)
            low = (value * eff).astype(BF16)
            inner_out[block, :] = low
            inner[block, pl.ds(at, cols)] = low
            slope_out[block, :] = (slope * eff).astype(BF16)
            total[block, :] += dot(low, weight_out[...])

    pl.when(step < chunks)(lambda: forward(pack_own, in_own, ffn_own))
    pl.when((step >= chunks) & (step < 2 * chunks))(
        lambda: forward(pack_other, in_other, ffn_other)
    )

    @pl.when(step == 2 * chunks)
    def _():
        for copy in early:
            copy.wait()
        fetch.wait()
        gain = row_of(vectors, LN2_GAIN)
        valid = valid_column(meta)
        hid_eff = row_of(vectors, HID_EFF)
        totals = [jnp.zeros((1, first.shape[1]), F32)] * 4
        for block in blocks_of(120):
            ffn_out = total[block, :]
            normed, spread = norm_stats(first[block, :] + ffn_out * hid_eff)
            layer_out[block, :] = (
                (normed * gain + row_of(vectors, LN2_BIAS)) * valid[block]
            ).astype(BF16)
            grad_final = cotangent[block, :].astype(F32) * valid[block]
            grad = norm_back(grad_final, normed, spread, gain)
            grad_ffn = grad * hid_eff
            grad_two[block, :] = grad
            grad_low[block, :] = grad_ffn.astype(BF16)
            terms = (grad_ffn, grad_final * normed, grad_final, grad * ffn_out)
            totals = [part + column_sum(term) for part, term in zip(totals, terms, strict=True)]
        sums[...] = jnp.zeros_like(sums)
        for place, part in enumerate(totals):
            sums[place : place + 1, :] = part
        for copy in late:
            copy.start()

    def backward(chunk, out):
        at = pl.multiple_of(chunk * cols, cols)
        out[...] = by_rows(inner[:, pl.ds(at, cols)], grad_low[...]).astype(BF16)

    pl.when(step >= 2 * chunks)(lambda: backward(step - chunks, weight_other))

    @pl.when(step == 3 * chunks - 1)
    def _():
        for copy in late:
            copy.wait()


def feed_forward(
    meta, hidden, cotangent, gated, outs, vectors, packs, ins, ffns, cols=768, row_step=480, after=()
):
    width = hidden.shape[1]
    half = gated[0].shape[1]
    units = ins[0].shape[1]
    chunks = units // cols
    column = pl.BlockSpec((ROWS, cols), lambda i, meta: (0, jnp.minimum(i, 2 * chunks - 1)))

    def part(first, i):
        return jnp.clip(i - first, 0, chunks - 1)

    def across(first, rows):
        return pl.BlockSpec((rows, cols), lambda i, meta: (0, part(first, i)))

    def down(first):
        return pl.BlockSpec((cols, width), lambda i, meta: (part(first, i), 0))

    low = bf16(ROWS, width)
    held = pltpu.VMEM((ROWS, width), BF16)
    wide = pltpu.VMEM((ROWS, width), F32)
    return call(
        "feed_forward",
        partial(ffn_body, chunks, row_step),
        (3 * chunks,),
        32,
        [meta],
        [
            (hidden, own_rows(width)),
            (cotangent, HBM),
            (gated[0], whole(ROWS, half)),
            (gated[1], whole(ROWS, half)),
            (outs[0], whole(half, width)),
            (outs[1], whole(half, width)),
            (vectors, whole(*vectors.shape)),
            (packs[0], across(0, packs[0].shape[0])),
            (packs[1], across(chunks, packs[1].shape[0])),
            (ins[0], across(0, width)),
            (ins[1], across(chunks, width)),
            (ffns[0], down(0)),
            (ffns[1], down(chunks)),
        ],
        [(low, HBM)] * 5
        + [
            (f32(ROWS, width), HBM),
            (f32(ROWS, 128), whole(ROWS, 128)),
            (bf16(ROWS, 2 * units), column),
            (bf16(ROWS, 2 * units), column),
            (bf16(units, width), down(2 * chunks)),
            (f32(8, width), whole(8, width)),
        ],
        scratch=[
            wide,
            wide,
            pltpu.VMEM((ROWS, 2 * units), BF16),
            held,
            held,
            held,
            held,
            held,
            held,
            wide,
            pltpu.SemaphoreType.DMA((7,)),
        ],
        after=after,
    )


def outer_body(left, right, out):
    out[...] = by_rows(left[...], right[...]).astype(BF16)


def outer(left, right, cols, after=(), step=512):
    width = right.shape[1]
    first = cols.start // step
    size = cols.stop - cols.start
    return call(
        "outer",
        outer_body,
        (size // step,),
        5,
        [],
        [
            (left, pl.BlockSpec((ROWS, step), lambda i: (0, i + first))),
            (right, whole(ROWS, width)),
        ],
        [(bf16(size, width), pl.BlockSpec((step, width), lambda i: (i, 0)))],
        after=after,
        vmem=16,
    )[0]


def shrink_body(
    chunks,
    row_step,
    grad_low,
    first_low_hbm,
    before_hbm,
    inner,
    slope,
    weight_in,
    weight_out,
    weight_grad,
    grad_first,
    unit_sums,
    kept,
    total,
    first_low,
    before,
    done,
):
    step = pl.program_id(0)
    fetch_low = pltpu.make_async_copy(first_low_hbm, first_low, done.at[0])
    fetch_before = pltpu.make_async_copy(before_hbm, before, done.at[1])

    @pl.when(step == 0)
    def _():
        fetch_low.start()
        fetch_before.start()

    bias_sum = jnp.zeros((1, inner.shape[1]), F32)
    gate_sum = jnp.zeros((1, inner.shape[1]), F32)
    for block in blocks_of(row_step):
        grad_inner = by_cols(grad_low[block, :], weight_out[...])
        grad_pre = grad_inner * slope[block, :].astype(F32)
        bias_sum += column_sum(grad_pre)
        gate_sum += column_sum(inner[block, :].astype(F32) * grad_inner)
        low = grad_pre.astype(BF16)
        kept[block, :] = low
        back = by_cols(low, weight_in[...])

        @pl.when(step == 0)
        def _(block=block, back=back):
            total[block, :] = back

        @pl.when((step > 0) & (step < chunks - 1))
        def _(block=block, back=back):
            total[block, :] += back

        @pl.when(step == chunks - 1)
        def _(block=block, back=back):
            if block.start == 0:
                fetch_before.wait()
            grad_first[block, :] = total[block, :] + back + before[block, :]

    unit_sums[...] = jnp.zeros_like(unit_sums)
    unit_sums[0:1, :] = bias_sum
    unit_sums[1:2, :] = gate_sum
    pl.when(step == 0)(fetch_low.wait)
    weight_grad[...] = by_rows(first_low[...], kept[...]).astype(BF16)


def shrink(
    side, grad_low, first_low, before, inner, slope, weight_in, weight_out, cols=512, row_step=960, after=()
):
    width, units = weight_in.shape
    chunks = units // cols
    full = whole(ROWS, width)
    across = pl.BlockSpec((width, cols), lambda i: (0, i))
    column = pl.BlockSpec((ROWS, cols), lambda i: (0, i + side * chunks))
    return call(
        "shrink",
        partial(shrink_body, chunks, row_step),
        (chunks,),
        12,
        [],
        [
            (grad_low, full),
            (first_low, HBM),
            (before, HBM),
            (inner, column),
            (slope, column),
            (weight_in, across),
            (weight_out, pl.BlockSpec((cols, width), lambda i: (i, 0))),
        ],
        [
            (bf16(width, units), across),
            (f32(ROWS, width), full),
            (f32(8, units), pl.BlockSpec((8, cols), lambda i: (0, i))),
        ],
        scratch=[
            pltpu.VMEM((ROWS, cols), BF16),
            pltpu.VMEM((ROWS, width), F32),
            pltpu.VMEM((ROWS, width), BF16),
            pltpu.VMEM((ROWS, width), F32),
            pltpu.SemaphoreType.DMA((2,)),
        ],
        after=after,
        vmem=36,
    )


def part_body(
    grad_first, normed_one, spread_one, attn_out, vectors, gated_own, gated_other, grad_one, low, weight_mine, weight_other, sums
):
    gain = row_of(vectors, LN1_GAIN)
    hid_eff = row_of(vectors, HID_EFF)
    totals = [jnp.zeros((1, grad_first.shape[1]), F32)] * 4
    for block in blocks_of(120):
        grad = grad_first[block, :]
        normed = normed_one[block, :].astype(F32)
        one = norm_back(grad, normed, spread_one[block, 0:1], gain)
        grad_one[block, :] = one
        attn = one * hid_eff
        low[block, :] = attn.astype(BF16)
        terms = (attn, grad * normed, grad, one * attn_out[block, :].astype(F32))
        totals = [part + column_sum(term) for part, term in zip(totals, terms, strict=True)]
    sums[...] = jnp.zeros_like(sums)
    for place, part in enumerate(totals):
        sums[place : place + 1, :] = part
    weight_other[...] = by_rows(gated_other[...], low[...]).astype(BF16)
    weight_mine[...] = by_rows(gated_own[...], low[...]).astype(BF16)


def part_norm(grad_first, normed_one, spread_one, attn_out, vectors, gated, after=()):
    width = grad_first.shape[1]
    half = gated[0].shape[1]
    values = [grad_first, normed_one, spread_one, attn_out, vectors, *gated]
    made = [
        f32(ROWS, width),
        bf16(ROWS, width),
        bf16(half, width),
        bf16(half, width),
        f32(8, width),
    ]
    return call(
        "part_norm",
        part_body,
        (1,),
        6,
        [],
        [(value, whole(*value.shape)) for value in values],
        [(shape, whole(*shape.shape)) for shape in made],
        after=after,
        vmem=28,
    )


def part_heads_body(
    head_width, low, gated_own, gated_other, out_own, out_other, pack_own, pack_other, context_own, context_other, means_own, means_other, sums
):
    half = gated_own.shape[1]
    head = lax.broadcasted_iota(jnp.int32, (8, half), 1) // head_width
    pick = (head == lax.broadcasted_iota(jnp.int32, (8, half), 0)).astype(BF16)
    sums[...] = jnp.zeros_like(sums)
    for place, (gated, weight, pack, context, means) in enumerate(
        (
            (gated_own, out_own, pack_own, context_own, means_own),
            (gated_other, out_other, pack_other, context_other, means_other),
        )
    ):
        column = jnp.zeros((1, half), F32)
        for start, size in BUCKETS:
            rows = slice(start, start + size)
            grads = by_cols(low[rows, :], weight[...])
            context[rows, :] = (grads * pack[PACK_HEAD : PACK_HEAD + 1, 0:half]).astype(BF16)
            terms = grads * gated[rows, :].astype(F32)
            column += column_sum(terms)
            high = terms.astype(BF16)
            rest = (terms - high.astype(F32)).astype(BF16)
            means[:, rows] = by_cols(pick, high) + by_cols(pick, rest)
        sums[place : place + 1, :] = column


def part_heads(low, gated, outs, packs, head_width, after=()):
    half = gated[0].shape[1]
    values = [low, *gated, *outs, *packs]
    made = [
        bf16(ROWS, half),
        bf16(ROWS, half),
        f32(8, ROWS),
        f32(8, ROWS),
        f32(8, half),
    ]
    return call(
        "part_heads",
        partial(part_heads_body, head_width),
        (1,),
        5,
        [],
        [(value, whole(*value.shape)) for value in values],
        [(shape, whole(*shape.shape)) for shape in made],
        after=after,
        vmem=28,
    )


def add_back_body(start, *refs):
    grads, weights, out = refs[:6], refs[6:12], refs[12]
    total = start[...]
    for side in (0, 3):
        left = jnp.concatenate([part[...] for part in grads[side : side + 3]], 1)
        right = jnp.concatenate([part[...] for part in weights[side : side + 3]], 1)
        total += by_cols(left, right)
    out[...] = total


def add_back(start, grads, weights, after=()):
    width = start.shape[1]
    half = grads[0].shape[1]
    step = ROWS // 4
    return call(
        "add_back",
        add_back_body,
        (4,),
        6,
        [],
        [(start, pl.BlockSpec((step, width), lambda i: (i, 0)))]
        + [(part, pl.BlockSpec((step, half), lambda i: (i, 0))) for part in grads]
        + [(part, whole(width, half)) for part in weights],
        [(f32(ROWS, width), pl.BlockSpec((step, width), lambda i: (i, 0)))],
        after=after,
        vmem=24,
    )[0]


def swap_bit(values, dp_size, bit):
    return lax.ppermute(values, "dp", [(at, at ^ (1 << bit)) for at in range(dp_size)])


TAIL = 128


def load(ref, rows, tail):
    values = ref[rows, :].astype(F32)
    if not tail:
        return values, None
    cut = values.shape[1] - TAIL
    return values[:, :cut], values[:, cut : cut + TAIL // 2] + values[:, cut + TAIL // 2 :]


def store(ref, main, extra):
    if extra is None:
        ref[...] = main.astype(ref.dtype)
        return
    cut = main.shape[1]
    high = extra.astype(BF16)
    ref[:, :cut] = main.astype(BF16)
    ref[:, cut : cut + TAIL // 2] = high
    ref[:, cut + TAIL // 2 :] = (extra - high.astype(F32)).astype(BF16)


def split_by(side, totals, kept, sent):
    for part, total in enumerate(totals):

        @pl.when(side == part)
        def _(total=total):
            store(kept, *total)

        @pl.when(side != part)
        def _(total=total):
            store(sent, *total)


def add(left, right):
    return tuple(None if a is None else a + b for a, b in zip(left, right, strict=True))


class Stream:
    def __init__(self, ins, shape, first, order, tail=False):
        self.ins = ins
        self.rows, self.cols = shape
        self.first = first
        self.order = order
        self.tail = tail
        self.stage = 0
        self.kept = self.value = self.arrived = None

    def job(self):
        stages = len(self.order)
        stage, tail = self.stage, self.tail
        size = self.rows >> stage if stage <= stages else self.value.shape[0]
        if stage < stages:
            half = size // 2
            ins = list(self.ins) if stage == 0 else [self.kept, self.arrived]

            def body(sides, *refs):
                *given, kept, sent = refs
                totals = []
                for at in (0, half):
                    rows = slice(at, at + half)
                    if stage == 0:
                        totals.append(self.first(given, rows))
                    else:
                        totals.append(add(*[load(ref, rows, tail) for ref in given]))
                split_by(sides[self.order[stage]], totals, kept, sent)

            return ins, [bf16(half, self.cols)] * 2, body
        if stage == stages:

            def body(sides, kept, arrived, value):
                rows = slice(0, size)
                store(value, *add(load(kept, rows, tail), load(arrived, rows, tail)))

            return [self.kept, self.arrived], [bf16(size, self.cols)], body
        bit = self.order[2 * stages - stage]

        def body(sides, own, arrived, value):
            for first, halves in in_order(sides[bit], own, arrived):

                @pl.when(first)
                def _(halves=halves):
                    for place, half in enumerate(halves):
                        value[place * size : place * size + size, :] = half[...]

        return [self.value, self.arrived], [bf16(2 * size, self.cols)], body

    def take(self, outs, dp_size):
        stages = len(self.order)
        if self.stage < stages:
            self.kept, sent = outs
            self.arrived = swap_bit(sent, dp_size, self.order[self.stage])
        else:
            (self.value,) = outs
            bit = self.order[2 * stages - 1 - self.stage]
            self.arrived = swap_bit(self.value, dp_size, bit)
        self.stage += 1

    def last(self):
        return self.stage == 2 * len(self.order)


class Gather:
    def __init__(self, streams, order):
        self.streams = streams
        self.order = order
        self.stage = 0
        self.value = self.arrived = None

    def job(self):
        stage = self.stage
        if stage == 0:
            ins = [part for stream in self.streams for part in (stream.kept, stream.arrived)]
            size = self.streams[0].kept.shape[0]

            def body(sides, *refs):
                *given, value = refs
                at = 0
                for stream, kept, arrived in zip(
                    self.streams, given[::2], given[1::2], strict=True
                ):
                    rows, tail = slice(0, size), stream.tail
                    total = add(load(kept, rows, tail), load(arrived, rows, tail))
                    store(value.at[:, at : at + stream.cols], *total)
                    at += stream.cols

            cols = sum(stream.cols for stream in self.streams)
            return ins, [bf16(size, cols)], body
        size, cols = self.value.shape

        def body(sides, own, arrived, value):
            for first, halves in in_order(sides[self.order[stage - 1]], own, arrived):

                @pl.when(first)
                def _(halves=halves):
                    for place, half in enumerate(halves):
                        value[place * size : place * size + size, :] = half[...]

        return [self.value, self.arrived], [bf16(2 * size, cols)], body

    def take(self, outs, dp_size):
        (self.value,) = outs
        self.arrived = swap_bit(self.value, dp_size, self.order[self.stage])
        self.stage += 1

    def last(self):
        return self.stage == len(self.order)


class Quad:
    def __init__(self, front, beside, back, orders):
        self.front, self.beside, self.back = front, beside, back
        self.orders = orders
        self.stage = 0
        self.values = self.arrived = self.kept = None
        self.first, self.second = front.order[2:]

    def to_partners(self, values, dp_size):
        found = []
        for number, value in enumerate(values, 1):
            flip = (number >> 1) << self.first | (number & 1) << self.second
            pairs = [(at, at ^ flip) for at in range(dp_size)]
            found.append(lax.ppermute(value, "dp", pairs))
        return found

    def place(self, sides):
        return 2 * sides[self.first] + sides[self.second]

    def job(self):
        front, beside, back = self.front, self.beside, self.back
        width = front.cols + back.cols
        if self.stage == 0:
            size = front.rows // 16
            ins = [front.kept, front.arrived, back.kept, back.arrived]

            def body(sides, *refs):
                given, outs = refs[:4], refs[4:]
                totals = []
                for at in range(4):
                    rows = slice(at * size, (at + 1) * size)
                    one, _ = add(*[load(ref, rows, False) for ref in given[:2]])
                    two, extra = add(*[load(ref, rows, True) for ref in given[2:]])
                    totals.append((jnp.concatenate([one, two], 1), extra))
                for mine in range(4):

                    @pl.when(self.place(sides) == mine)
                    def _(mine=mine):
                        for number, out in enumerate(outs):
                            store(out, *totals[mine ^ number])

            return ins, [bf16(size, width)] * 4, body
        if self.stage == 1:
            size = self.kept.shape[0]
            ins = [self.kept, *self.arrived, beside.kept, beside.arrived]

            def body(sides, *refs):
                *given, out = refs
                rows = slice(0, size)
                total = load(given[0], rows, True)
                for ref in given[1:4]:
                    total = add(total, load(ref, rows, True))
                extra = add(*[load(ref, rows, False) for ref in given[4:]])[0]
                main = [total[0][:, : front.cols], extra, total[0][:, front.cols :]]
                store(out, jnp.concatenate(main, 1), total[1])

            return ins, [bf16(size, width + beside.cols)], body
        cut = front.cols + beside.cols
        if self.stage == 2:
            size = self.values[0].shape[0]

            def body(sides, *refs):
                given, outs = refs[:4], refs[4:]
                for mine in range(4):

                    @pl.when(self.place(sides) == mine)
                    def _(mine=mine):
                        for number, ref in enumerate(given):
                            at = mine ^ number
                            at = (at >> 1) + 2 * (at & 1) if self.swapped() else at
                            rows = slice(at * size, (at + 1) * size)
                            outs[0][rows, :] = ref[:, :cut]
                            outs[1][rows, :] = ref[:, cut:]

            made = [bf16(4 * size, cut), bf16(4 * size, back.cols)]
            return [self.values[0], *self.arrived], made, body
        size = self.values[0].shape[0]
        bits = [order[2] for order in self.orders]

        def body(sides, *refs):
            for at, bit in enumerate(bits):
                own, arrived, out = refs[2 * at], refs[2 * at + 1], refs[4 + at]
                for first, halves in in_order(sides[bit], own, arrived):

                    @pl.when(first)
                    def _(halves=halves, out=out):
                        for place, half in enumerate(halves):
                            out[place * size : place * size + size, :] = half[...]

        ins = [value for pair in zip(self.values, self.arrived, strict=True) for value in pair]
        return ins, [bf16(2 * size, cut), bf16(2 * size, back.cols)], body

    def swapped(self):
        return self.orders[0][0] == self.first

    def take(self, outs, dp_size):
        if self.stage == 0:
            self.kept = outs[0]
            self.arrived = self.to_partners(outs[1:], dp_size)
        elif self.stage == 1:
            self.values = list(outs)
            self.arrived = self.to_partners([outs[0]] * 3, dp_size)
        else:
            self.values = list(outs)
            self.arrived = [
                swap_bit(value, dp_size, order[self.stage])
                for value, order in zip(outs, self.orders, strict=True)
            ]
        self.stage += 1

    def gathers(self):
        found = []
        for at, streams in enumerate(([self.front, self.beside], [self.back])):
            gather = Gather(streams, self.orders[at])
            gather.value, gather.arrived = self.values[at], self.arrived[at]
            found.append(gather)
        return found


def in_order(side, own, arrived):
    return (side == 0, (own, arrived)), (side == 1, (arrived, own))


def small_call(name, body, ins, outs, sides, after=()):
    return call(
        name,
        body,
        (1,),
        2,
        [sides],
        [(value, whole(*value.shape)) for value in ins],
        [(shape, whole(*shape.shape)) for shape in outs],
        after=after,
        vmem=24,
    )


def advance(streams, dp_size, sides, after=()):
    jobs = [stream.job() for stream in streams]
    ins = [value for job in jobs for value in job[0]]
    outs = [shape for job in jobs for shape in job[1]]

    def body(sides, *refs):
        given, made = refs[: len(ins)], refs[len(ins) :]
        for inputs, shapes, work in jobs:
            work(sides, *given[: len(inputs)], *made[: len(shapes)])
            given, made = given[len(inputs) :], made[len(shapes) :]

    found = small_call("advance", body, ins, outs, sides, after)
    for stream, job in zip(streams, jobs, strict=True):
        stream.take(found[: len(job[1])], dp_size)
        found = found[len(job[1]) :]


def states(streams):
    return [stream.kept if stream.value is None else stream.value for stream in streams]


def blocks_in(gather):
    streams, order = gather.streams, gather.order
    bits = len(order)
    size = streams[0].rows >> bits
    for block in range(1 << bits):
        device = sum((block >> turn & 1) << bit for turn, bit in enumerate(order))
        half, inside = divmod(block, 1 << (bits - 1))
        places = [
            size
            * sum((device >> bit & 1) << (bits - 1 - turn) for turn, bit in enumerate(stream.order))
            for stream in streams
        ]
        yield half, slice(inside * size, (inside + 1) * size), places, size


def finish(gathers, sides, by_cols, after=()):
    rows, cols = gathers[0].streams[0].rows, gathers[0].streams[0].cols

    def body(sides, *refs):
        *given, out = refs
        for at, gather in enumerate(gathers):
            pair = given[2 * at : 2 * at + 2]
            top, left = (0, at * cols) if by_cols else (at * rows, 0)
            for first, halves in in_order(sides[gather.order[-1]], *pair):

                @pl.when(first)
                def _(gather=gather, halves=halves, top=top, left=left):
                    for half, where, (row,), size in blocks_in(gather):
                        out[top + row : top + row + size, left : left + cols] = halves[half][
                            where, :
                        ].astype(F32)

    ins = [value for gather in gathers for value in (gather.value, gather.arrived)]
    shape = (rows, 2 * cols) if by_cols else (2 * rows, cols)
    return small_call("finish", body, ins, [f32(*shape)], sides, after)[0]


def orders_of(dp_size):
    bits = dp_size.bit_length() - 1
    if bits == 4:
        halved = (0, 1, 2, 3), (1, 0, 2, 3), (2, 0, 1, 3), (0, 2, 3, 1), (0, 1, 2, 3), (1, 0, 2, 3)
        doubled = (1, 3, 2, 0), (3, 1, 0, 2), (3, 0, 1, 2), (3, 2, 1, 0), (3, 2, 0, 1), (0, 3, 2, 1)
        return halved + doubled
    return tuple(tuple((at + turn) % bits for at in range(bits)) for turn in range(12))


def late_streams(qkv, small, orders):
    rows, cols = qkv[0].shape
    cut = -(-(cols + TAIL) // 256) * 128
    places = small[0].shape[1] // (TAIL // 2)
    depth = small[0].shape[0]

    def front(given, where):
        return sum(ref[where, 0:cut].astype(F32) for ref in given), None

    def back(given, where):
        first, size = where.start, where.stop - where.start
        main = sum(ref[where, cut:cols].astype(F32) for ref in given[0:2])
        extra = []
        for place in range(first // depth, (first + size) // depth):
            if place < places:
                at = slice(place * TAIL // 2, (place + 1) * TAIL // 2)
                extra.append(sum(ref[:, at] for ref in given[2:4]))
        used = depth * len(extra)
        if used < size:
            extra.append(jnp.zeros((size - used, TAIL // 2), F32))
        return main, jnp.concatenate(extra, 0)

    return [
        Stream(qkv, (rows, cut), front, orders[0]),
        Stream((*qkv, *small), (rows, cols - cut + TAIL), back, orders[1], True),
    ]


def finish_late(gathers, sides, lanes, small_shape, after=()):
    (front, out_stream), (back,) = [gather.streams for gather in gathers]
    rows, half = front.rows, out_stream.cols
    depth, width = small_shape
    cut = front.cols
    places = width // (TAIL // 2)

    def body(sides, own0, arrived0, own1, arrived1, qkv_out, out_out, small_out):
        def qkv_part(values, row, where, first, cols):
            for at in range(0, cols, lanes):
                pair, kind = divmod((first + at) // lanes, 3)
                columns = slice(pair * lanes, (pair + 1) * lanes)
                lines = slice(row, row + where.stop - where.start)
                qkv_out[lines, kind, columns] = values[where, at : at + lanes].astype(F32)

        for first, halves in in_order(sides[gathers[0].order[-1]], own0, arrived0):

            @pl.when(first)
            def _(halves=halves):
                for number, where, (row, other_row), size in blocks_in(gathers[0]):
                    qkv_part(halves[number], row, where, 0, cut)
                    side = other_row // half
                    line = other_row - side * half
                    out_out[line : line + size, side * half : (side + 1) * half] = halves[number][
                        where, cut : cut + half
                    ].astype(F32)

        for first, halves in in_order(sides[gathers[1].order[-1]], own1, arrived1):

            @pl.when(first)
            def _(halves=halves):
                for number, where, (row,), size in blocks_in(gathers[1]):
                    qkv_part(halves[number], row, where, cut, back.cols - TAIL)
                    cuts = sorted({row, row + size, *range(-(-row // depth) * depth, row + size, depth)})
                    for at, end in zip(cuts, cuts[1:]):
                        place, line = divmod(at, depth)
                        count = end - at
                        if place < places:
                            top = where.start + at - row
                            _, extra = load(halves[number], slice(top, top + count), True)
                            columns = slice(place * TAIL // 2, (place + 1) * TAIL // 2)
                            small_out[line : line + count, columns] = extra

    ins = [value for gather in gathers for value in (gather.value, gather.arrived)]
    outs = [f32(rows, 3, half), f32(half, rows), f32(depth, width)]
    return small_call("finish_late", body, ins, outs, sides, after)


def pack_sums(part_sums, turn_sums, head_sums, bias_sums, unit_sums, after=()):
    width = part_sums.shape[1]
    half = bias_sums[0].shape[1]
    unit_rows = unit_sums[0].shape[1] // width

    def body(part, turned, heads, bias_own, bias_other, unit_own, unit_other, mine, theirs):
        sides = ((mine, bias_own, unit_own), (theirs, bias_other, unit_other))
        for side, (out, bias, unit) in enumerate(sides):
            out[...] = jnp.zeros_like(out)
            out[0:4, :] = part[0:4, :]
            out[4:8, :] = turned[0:4, :]
            out[8:9, 0:half] = bias[0:1, :]
            out[8:9, half : 2 * half] = bias[1:2, :]
            out[9:10, 0:half] = heads[side : side + 1, :]
            for kind in (0, 1):
                for row in range(unit_rows):
                    place = 10 + kind * unit_rows + row
                    out[place : place + 1, :] = unit[
                        kind : kind + 1, row * width : (row + 1) * width
                    ]

    values = [part_sums, turn_sums, head_sums, *bias_sums, *unit_sums]
    rows = -(-(10 + 2 * unit_rows) // 8) * 8
    return call(
        "pack_sums",
        body,
        (1,),
        1,
        [],
        [(value, whole(*value.shape)) for value in values],
        [(f32(rows, width), whole(rows, width))] * 2,
        after=after,
        vmem=24,
    )


def per_device(
    dp_size,
    hidden,
    cotangent,
    counts,
    lengths,
    qkv_weight,
    qv_bias,
    out_weight,
    out_bias,
    ln1_gain,
    ln1_bias,
    in_weight,
    in_bias,
    ffn_out_weight,
    ffn_out_bias,
    ln2_gain,
    ln2_bias,
    head_gate,
    head_mask,
    ffn_gate,
    ffn_mask,
    hidden_gate,
    hidden_mask,
):
    width = hidden.shape[1]
    own_heads = head_gate.shape[0]
    half = qkv_weight.shape[2]
    units = in_weight.shape[1]
    head_width = half // own_heads
    head_at = lax.axis_index("head")

    def other(values):
        return lax.ppermute(values, "head", [(0, 1), (1, 0)])

    def pad_to(values, size):
        return jnp.pad(values, (0, size - values.shape[0]))

    meta = jnp.concatenate(
        [
            lax.dynamic_index_in_dim(
                jnp.where(counts[0] > 0, lengths[0], 0), head_at, 0, keepdims=False
            ),
            head_at[None],
        ]
    )
    head_flags = head_mask.astype(F32)
    ffn_flags = ffn_mask.astype(F32)
    hidden_flags = hidden_mask.astype(F32)
    pack = jnp.stack(
        [
            in_bias,
            ffn_gate * ffn_flags,
            pad_to(qv_bias.reshape(-1), units),
            pad_to(jnp.repeat(head_gate * head_flags, head_width), units),
        ]
    )
    vectors = jnp.stack(
        [
            out_bias,
            ln1_gain,
            ln1_bias,
            ffn_out_bias,
            ln2_gain,
            ln2_bias,
            hidden_gate * hidden_flags,
        ]
    )
    qkv_own = [qkv_weight[:, at] for at in range(3)]
    qkv_other = [other(part) for part in qkv_own]
    packs = (pack, other(pack))
    outs = (out_weight, other(out_weight))
    ins = (in_weight, other(in_weight))
    ffns = (ffn_out_weight, other(ffn_out_weight))
    sides = jnp.stack([(lax.axis_index("dp") >> bit) & 1 for bit in range(dp_size.bit_length() - 1)])
    orders = orders_of(dp_size)
    step = partial(advance, dp_size=dp_size, sides=sides)

    def halves(size, at):
        return slice(at * size // 2, (at + 1) * size // 2)

    def sum_stream(left, right, order, rows=None, cols=None):
        rows = rows or slice(0, left.shape[0])
        cols = cols or slice(0, left.shape[1])

        def first(given, at):
            at = slice(rows.start + at.start, rows.start + at.stop)
            return sum(ref[at, cols].astype(F32) for ref in given), None

        shape = (rows.stop - rows.start, cols.stop - cols.start)
        return Stream((left, right), shape, first, order)

    *qkv0, gated0, logs0 = attend(meta, hidden, qkv_own, packs[0], head_width)
    *qkv1, gated1, logs1 = attend(meta, hidden, qkv_other, packs[1], head_width, [gated0])
    gated = (gated0, gated1)
    (
        layer_out,
        first_low,
        normed_one,
        attn_out,
        grad_low,
        grad_two,
        spread_one,
        inner,
        slope,
        ffn_grad_other,
        turn_sums,
    ) = feed_forward(meta, hidden, cotangent, gated, outs, vectors, packs, ins, ffns)
    ffn_grad_theirs = other(ffn_grad_other)
    ffn_grad_mine = outer(inner, grad_low, slice(0, units))
    streams = [
        sum_stream(ffn_grad_mine, ffn_grad_theirs, orders[at], rows=halves(units, at))
        for at in (0, 1)
    ]
    step(streams)
    in_grad_other, grad_first, unit_sums1 = shrink(
        1, grad_low, first_low, grad_two, inner, slope, ins[1], ffns[1], after=states(streams)
    )
    in_grad_theirs = other(in_grad_other)
    step(streams, after=[grad_first])
    in_grad_mine, grad_first, unit_sums0 = shrink(
        0, grad_low, first_low, grad_first, inner, slope, ins[0], ffns[0], after=states(streams)
    )
    in_streams = [
        sum_stream(in_grad_mine, in_grad_theirs, orders[2 + at], cols=halves(units, at))
        for at in (0, 1)
    ]
    streams += in_streams
    step(streams, after=[grad_first])
    grad_one, attn_low, out_grad_mine, out_grad_other, part_sums = part_norm(
        grad_first,
        normed_one,
        spread_one,
        attn_out,
        vectors,
        gated,
        after=states(streams),
    )
    out_grad_theirs = other(out_grad_other)
    grad_context0, grad_context1, means0, means1, head_sums = part_heads(
        attn_low, gated, outs, packs, head_width
    )

    def out_part(given, at):
        side = at.start // half
        rows = slice(at.start - side * half, at.stop - side * half)
        cols = slice(side * half, (side + 1) * half)
        return sum(ref[rows, cols].astype(F32) for ref in given), None

    out_stream = Stream((out_grad_mine, out_grad_theirs), (width, half), out_part, orders[4])
    streams = [*streams[:2], out_stream]
    step(streams, after=[grad_context0])
    *mixed1, qkv_grad_other, bias_sums1 = attend_back(
        meta,
        hidden,
        qkv1,
        grad_context1,
        logs1,
        means1,
        packs[1],
        head_width,
        after=states(streams),
    )
    qkv_grad_theirs = other(qkv_grad_other)
    ffn_gathers = [Gather(streams[at : at + 1], orders[(6, 11)[at]]) for at in (0, 1)]
    streams = [*ffn_gathers, *in_streams, out_stream]
    step(streams, after=[mixed1[0]])
    *mixed0, qkv_grad_mine, bias_sums0 = attend_back(
        meta,
        hidden,
        qkv0,
        grad_context0,
        logs0,
        means0,
        packs[0],
        head_width,
        after=states(streams) + [mixed1[0]],
    )
    step(streams, after=[mixed0[0]])
    small = pack_sums(
        part_sums,
        turn_sums,
        head_sums,
        (bias_sums0, bias_sums1),
        (unit_sums0, unit_sums1),
        after=states(streams),
    )
    late = late_streams(
        (qkv_grad_mine, qkv_grad_theirs), (small[0], other(small[1])), orders[4:6]
    )
    step(late)
    grad_hidden = add_back(
        grad_one, mixed0 + mixed1, qkv_own + qkv_other, after=states(streams + late)
    )
    step([*ffn_gathers, *in_streams, out_stream, *late], after=[grad_hidden])
    gathers = [Gather(in_streams[at : at + 1], orders[7 + at]) for at in (0, 1)]
    if dp_size == 16:
        quad = Quad(late[0], out_stream, late[1], orders[9:11])
        step([*ffn_gathers, *gathers, quad])
        step([*gathers, quad])
        step([*gathers, quad], after=[gather.arrived for gather in ffn_gathers])
        step([*gathers, quad])
        late = quad.gathers()
    else:
        while late[0].stage < len(late[0].order):
            step(late)
        while out_stream.stage < len(out_stream.order):
            step([out_stream])
        late = [Gather([late[0], out_stream], orders[9]), Gather([late[1]], orders[10])]
        for gather in gathers:
            while not gather.last():
                step([gather])
        for gather in ffn_gathers:
            while not gather.last():
                step([gather])
        while not late[0].last():
            step(late)
    grad_ffn_out_weight = finish(ffn_gathers, sides, by_cols=False)
    grad_in_weight = finish(gathers, sides, by_cols=True)
    grad_qkv_weight, grad_out_weight, small = finish_late(
        late, sides, 2 * head_width, small[0].shape
    )
    (
        grad_out_bias,
        grad_ln1_gain,
        grad_ln1_bias,
        gate_one,
        grad_ffn_out_bias,
        grad_ln2_gain,
        grad_ln2_bias,
        gate_two,
    ) = small[:8]
    unit_rows = units // width
    return (
        layer_out,
        grad_hidden,
        grad_qkv_weight,
        small[8].reshape(2, half),
        grad_out_weight,
        grad_out_bias,
        grad_ln1_gain,
        grad_ln1_bias,
        grad_in_weight,
        small[10 : 10 + unit_rows].reshape(-1),
        grad_ffn_out_weight,
        grad_ffn_out_bias,
        grad_ln2_gain,
        grad_ln2_bias,
        jnp.sum(small[9, :half].reshape(own_heads, head_width), 1) * head_flags / head_gate,
        small[10 + unit_rows : 10 + 2 * unit_rows].reshape(-1) * ffn_flags / ffn_gate,
        (gate_one + gate_two) * hidden_flags,
    )


def solution(mesh):
    placed = (
        P("dp", None),
        P("dp", None),
        P("dp", None, None),
        P("dp", None, None),
        P(None, None, "head"),
        P(None, "head"),
        P("head", None),
        P(),
        P(),
        P(),
        P(None, "head"),
        P("head"),
        P("head", None),
        P(),
        P(),
        P(),
        P("head"),
        P("head"),
        P("head"),
        P("head"),
        P(),
        P(),
    )
    return jax.shard_map(
        partial(per_device, mesh.shape["dp"]),
        mesh=mesh,
        in_specs=placed,
        out_specs=(
            P(("dp", "head"), None),
            P(("dp", "head"), None),
            P(None, None, "head"),
            P(None, "head"),
            P("head", None),
            P(),
            P(),
            P(),
            P(None, "head"),
            P("head"),
            P("head", None),
            P(),
            P(),
            P(),
            P("head"),
            P("head"),
            P(),
        ),
        check_vma=False,
    )
```

```python
from functools import partial

import jax
import jax.numpy as jnp
from jax import lax
from jax.experimental import pallas as pl
from jax.experimental.pallas import tpu as pltpu
from jax.sharding import PartitionSpec as P

BASE = 64
ROWS = 15 * BASE
EPSILON = 1e-12
MASKED = -1e9
LOG2E = 1.4426950408889634
BUCKETS = ((0, 8 * BASE), (8 * BASE, 4 * BASE), (12 * BASE, 2 * BASE), (14 * BASE, BASE))
F32 = jnp.float32
BF16 = jnp.bfloat16
MEBI = 1 << 20
HBM = pl.BlockSpec(memory_space=pl.ANY)


def dot(left, right):
    return jnp.dot(left, right, preferred_element_type=F32)


def by_rows(left, right):
    return lax.dot_general(left, right, (((0,), (0,)), ((), ())), preferred_element_type=F32)


def by_cols(left, right):
    return lax.dot_general(left, right, (((1,), (1,)), ((), ())), preferred_element_type=F32)


def f32(*shape):
    return jax.ShapeDtypeStruct(shape, F32)


def bf16(*shape):
    return jax.ShapeDtypeStruct(shape, BF16)


def whole(*shape):
    return pl.BlockSpec(shape, lambda *_: (0,) * len(shape))


def call(name, body, grid, micros, scalars, ins, outs, scratch=(), after=(), vmem=58):
    first = len(scalars) + len(ins)

    def run(*refs):
        body(*refs[:first], *refs[first + len(after) :])

    return pl.pallas_call(
        run,
        grid_spec=pltpu.PrefetchScalarGridSpec(
            num_scalar_prefetch=len(scalars),
            grid=grid,
            in_specs=[spec for _, spec in ins] + [HBM] * len(after),
            out_specs=[spec for _, spec in outs],
            scratch_shapes=list(scratch),
        ),
        out_shape=[shape for shape, _ in outs],
        compiler_params=pltpu.CompilerParams(
            dimension_semantics=("arbitrary",) * len(grid), vmem_limit_bytes=vmem * MEBI
        ),
        cost_estimate=pl.CostEstimate(
            flops=int(micros * 5e9), bytes_accessed=1 << 20, transcendentals=0
        ),
        name=name,
    )(*scalars, *[value for value, _ in ins], *after)


def row_of(vectors, at):
    return vectors[at : at + 1, :]


def column_sum(values):
    return jnp.sum(values, 0, keepdims=True)


def own_rows(width):
    return pl.BlockSpec((ROWS, width), lambda i, meta: (meta[4], 0))


PACK_IN_BIAS, PACK_FFN, PACK_QV, PACK_HEAD = range(4)


def side_masks(lanes):
    low = lax.broadcasted_iota(jnp.int32, (1, lanes), 1) < lanes // 2
    return low, low.astype(BF16), 1 - low.astype(BF16)


def kept_head(gate, side):
    half = gate.shape[1] // 2
    return jnp.max(gate[PACK_HEAD : PACK_HEAD + 1, side * half : (side + 1) * half]) > 0


def for_kept(gate, run):
    flags = [kept_head(gate, side) for side in (0, 1)]
    for sides in ((0, 1), (0,), (1,), ()):
        case = [flags[side] if side in sides else jnp.logical_not(flags[side]) for side in (0, 1)]
        pl.when(case[0] & case[1])(partial(run, sides))


def attend_body(
    pairs, lanes, meta, hidden, weight_q, weight_k, weight_v, bias_q, bias_v, gate, query, key, value, gated, logs, columns, context
):
    pair = pl.program_id(0)
    weight = jnp.concatenate([weight_q[...], weight_k[...], weight_v[...]], 1)
    mixed = dot(hidden[...], weight)
    query[...] = (mixed[:, :lanes] + bias_q[PACK_QV : PACK_QV + 1, :]).astype(BF16)
    key[...] = mixed[:, lanes : 2 * lanes].astype(BF16)
    value[...] = (mixed[:, 2 * lanes :] + bias_v[PACK_QV : PACK_QV + 1, :]).astype(BF16)
    scale = LOG2E * (lanes // 2) ** -0.5
    low_side, *masks = side_masks(lanes)
    lane = lax.broadcasted_iota(jnp.int32, (1, 128), 1)

    def run(sides):
        for place, (start, size) in enumerate(BUCKETS):
            rows = slice(start, start + size)
            seen = lax.broadcasted_iota(jnp.int32, (1, size), 1) < meta[place]
            shut = jnp.where(seen, 0.0, MASKED).astype(F32)
            queries, keys, values = query[rows, :], key[rows, :], value[rows, :]
            total_context = jnp.zeros((size, lanes), F32)
            column = columns[rows, :]
            for side in sides:
                scores = by_cols(queries * masks[side], keys) + shut
                top = jnp.max(scores, -1, keepdims=True)
                power = jnp.exp2((scores - top) * scale)
                total = jnp.sum(power, -1, keepdims=True)
                found = dot(power.astype(BF16), values) * (1.0 / total)
                log = top * scale + jnp.log2(total)
                column = jnp.where(lane == 2 * pair + side, log, column)
                total_context = jnp.where(low_side == (side == 0), found, total_context)
            columns[rows, :] = column
            context[rows, :] = total_context

    for_kept(gate, run)
    gated[...] = (context[...] * gate[PACK_HEAD : PACK_HEAD + 1, :]).astype(BF16)

    @pl.when(pair == pairs - 1)
    def _():
        for start, size in BUCKETS:
            rows = slice(start, start + size)
            logs[:, rows] = columns[rows, :].T[0:8, :]


def attend(meta, hidden, weights, pack, head_width, after=()):
    width, half = weights[0].shape
    lanes = 2 * head_width
    pairs = half // lanes
    column = pl.BlockSpec((ROWS, lanes), lambda i, meta: (0, i))
    weight = pl.BlockSpec((width, lanes), lambda i, meta: (0, i))

    def vector(shift):
        return pl.BlockSpec((pack.shape[0], lanes), lambda i, meta: (0, i + shift))

    return call(
        "attend",
        partial(attend_body, pairs, lanes),
        (pairs,),
        9,
        [meta],
        [(hidden, own_rows(width))]
        + [(part, weight) for part in weights]
        + [(pack, vector(0)), (pack, vector(pairs)), (pack, vector(0))],
        [(bf16(ROWS, half), column)] * 4 + [(f32(8, ROWS), whole(8, ROWS))],
        scratch=[pltpu.VMEM((ROWS, 128), F32), pltpu.VMEM((ROWS, lanes), F32)],
        after=after,
        vmem=58,
    )


def pick_row(values, at):
    place = lax.broadcasted_iota(jnp.int32, values.shape, 0)
    return column_sum(jnp.where(place == at, values, 0.0))


def attend_back_body(
    lanes, meta, hidden, query, key, value, grad_context, logs, means, gate, grad_q, grad_k, grad_v, weight_grad, bias_sums, *totals
):
    pair = pl.program_id(0)
    scale = LOG2E * (lanes // 2) ** -0.5
    final = (lanes // 2) ** -0.5
    _, *masks = side_masks(lanes)

    def run(sides):
        for place, (start, size) in enumerate(BUCKETS):
            rows = slice(start, start + size)
            seen = lax.broadcasted_iota(jnp.int32, (size, 1), 0) < meta[place]
            shut = jnp.where(seen, 0.0, MASKED).astype(F32)
            queries, keys, values = query[rows, :], key[rows, :], value[rows, :]
            grads = grad_context[rows, :]
            sums = [jnp.zeros((size, lanes), F32)] * 3
            for side in sides:
                log = pick_row(logs[:, rows], 2 * pair + side)
                mean = pick_row(means[:, rows], 2 * pair + side)
                side_queries = queries * masks[side]
                side_grads = grads * masks[side]
                scores = by_cols(keys, side_queries) + shut
                weights = jnp.exp2(scores * scale - log)
                change = (weights * (by_cols(values, side_grads) - mean)).astype(BF16)
                terms = (
                    by_rows(change, keys * masks[side]),
                    dot(change, side_queries),
                    dot(weights.astype(BF16), side_grads),
                )
                sums = [part + term for part, term in zip(sums, terms, strict=True)]
            for total, part in zip(totals, sums, strict=True):
                total[rows, :] = part

    for_kept(gate, run)
    grad_query = totals[0][...] * final
    grad_q[...] = grad_query.astype(BF16)
    grad_k[...] = (totals[1][...] * final).astype(BF16)
    grad_v[...] = totals[2][...].astype(BF16)
    query_sum = column_sum(grad_query)
    value_sum = column_sum(totals[2][...])
    grads = jnp.concatenate([grad_q[...], grad_k[...], grad_v[...]], 1)
    weight_grad[...] = by_rows(hidden[...], grads).astype(BF16)
    bias_sums[...] = jnp.zeros_like(bias_sums)
    bias_sums[0:1, :] = query_sum
    bias_sums[1:2, :] = value_sum


def attend_back(meta, hidden, parts, grad_context, logs, means, pack, head_width, after=()):
    half = grad_context.shape[1]
    width = hidden.shape[1]
    lanes = 2 * head_width
    pairs = half // lanes
    column = pl.BlockSpec((ROWS, lanes), lambda i, meta: (0, i))
    return call(
        "attend_back",
        partial(attend_back_body, lanes),
        (pairs,),
        11,
        [meta],
        [(hidden, own_rows(width))]
        + [(part, column) for part in (*parts, grad_context)]
        + [(logs, whole(8, ROWS)), (means, whole(8, ROWS))]
        + [(pack, pl.BlockSpec((pack.shape[0], lanes), lambda i, meta: (0, i)))],
        [(bf16(ROWS, half), column)] * 3
        + [
            (
                bf16(width, 3 * half),
                pl.BlockSpec((width, 3 * lanes), lambda i, meta: (0, i)),
            ),
            (f32(8, half), pl.BlockSpec((8, lanes), lambda i, meta: (0, i))),
        ],
        scratch=[pltpu.VMEM((ROWS, lanes), F32)] * 3,
        after=after,
        vmem=24,
    )


(OUT_BIAS, LN1_GAIN, LN1_BIAS, FFN_OUT_BIAS, LN2_GAIN, LN2_BIAS, HID_EFF) = range(7)


def valid_column(meta):
    at = lax.broadcasted_iota(jnp.int32, (ROWS, 1), 0)
    found = jnp.zeros((ROWS, 1), F32)
    for place, (start, size) in enumerate(BUCKETS):
        found = jnp.where((at >= start) & (at < start + meta[place]), 1.0, found)
    return found


def norm_stats(resid):
    centred = resid - jnp.mean(resid, -1, keepdims=True)
    spread = lax.rsqrt(jnp.mean(centred * centred, -1, keepdims=True) + EPSILON)
    return (centred * spread, spread)


def norm_back(grad_out, normed, spread, gain):
    grad_normed = grad_out * gain
    first_mean = jnp.mean(grad_normed, -1, keepdims=True)
    second_mean = jnp.mean(grad_normed * normed, -1, keepdims=True)
    return spread * (grad_normed - first_mean - normed * second_mean)


def blocks_of(step):
    return [slice(at, at + step) for at in range(0, ROWS, step)]


def gelu_and_slope(z):
    below = 0.5 + 0.5 * lax.erf(z * 0.5**0.5)
    density = jnp.exp2((-0.5 * LOG2E) * (z * z)) * (0.5 / 3.141592653589793) ** 0.5
    return (z * below, below + z * density)


def ffn_body(
    chunks,
    row_step,
    meta,
    hidden,
    cotangent_all,
    gated_own,
    gated_other,
    out_own,
    out_other,
    vectors,
    pack_own,
    pack_other,
    in_own,
    in_other,
    ffn_own,
    ffn_other,
    layer_out_hbm,
    first_low_hbm,
    normed_hbm,
    attn_hbm,
    grad_low_hbm,
    grad_two_hbm,
    spread_one,
    inner_out,
    slope_out,
    weight_other,
    sums,
    first,
    total,
    inner,
    cotangent,
    layer_out,
    first_low,
    normed_one,
    attn_out,
    grad_low,
    grad_two,
    done,
):
    step = pl.program_id(0)
    cols = inner_out.shape[1]
    early = ((first_low, first_low_hbm), (normed_one, normed_hbm), (attn_out, attn_hbm))
    late = ((layer_out, layer_out_hbm), (grad_low, grad_low_hbm), (grad_two, grad_two_hbm))
    early = [pltpu.make_async_copy(*pair, done.at[at]) for at, pair in enumerate(early)]
    late = [pltpu.make_async_copy(*pair, done.at[3 + at]) for at, pair in enumerate(late)]
    mine = pl.ds(pl.multiple_of(meta[4] * ROWS, ROWS), ROWS)
    fetch = pltpu.make_async_copy(cotangent_all.at[mine, :], cotangent, done.at[6])

    @pl.when(step == 0)
    def _():
        fetch.start()
        for block in blocks_of(240):
            attn = (
                dot(gated_own[block, :], out_own[...])
                + dot(gated_other[block, :], out_other[...])
                + row_of(vectors, OUT_BIAS)
            )
            attn_out[block, :] = attn.astype(BF16)
            normed, spread = norm_stats(
                hidden[block, :].astype(F32) + attn * row_of(vectors, HID_EFF)
            )
            normed_one[block, :] = normed.astype(BF16)
            spread_one[block, :] = jnp.broadcast_to(spread, (240, 128))
            value = normed * row_of(vectors, LN1_GAIN) + row_of(vectors, LN1_BIAS)
            first[block, :] = value
            first_low[block, :] = value.astype(BF16)
            total[block, :] = jnp.broadcast_to(row_of(vectors, FFN_OUT_BIAS), value.shape)
        for copy in early:
            copy.start()

    def forward(pack, weight_in, weight_out):
        bias = pack[PACK_IN_BIAS : PACK_IN_BIAS + 1, :]
        eff = pack[PACK_FFN : PACK_FFN + 1, :]
        at = pl.multiple_of(step * cols, cols)
        for block in blocks_of(row_step):
            pre = dot(first_low[block, :], weight_in[...]) + bias
            value, slope = gelu_and_slope(pre)
            low = (value * eff).astype(BF16)
            inner_out[block, :] = low
            inner[block, pl.ds(at, cols)] = low
            slope_out[block, :] = (slope * eff).astype(BF16)
            total[block, :] += dot(low, weight_out[...])

    pl.when(step < chunks)(lambda: forward(pack_own, in_own, ffn_own))
    pl.when((step >= chunks) & (step < 2 * chunks))(
        lambda: forward(pack_other, in_other, ffn_other)
    )

    @pl.when(step == 2 * chunks)
    def _():
        for copy in early:
            copy.wait()
        fetch.wait()
        gain = row_of(vectors, LN2_GAIN)
        valid = valid_column(meta)
        hid_eff = row_of(vectors, HID_EFF)
        totals = [jnp.zeros((1, first.shape[1]), F32)] * 4
        for block in blocks_of(120):
            ffn_out = total[block, :]
            normed, spread = norm_stats(first[block, :] + ffn_out * hid_eff)
            layer_out[block, :] = (
                (normed * gain + row_of(vectors, LN2_BIAS)) * valid[block]
            ).astype(BF16)
            grad_final = cotangent[block, :].astype(F32) * valid[block]
            grad = norm_back(grad_final, normed, spread, gain)
            grad_ffn = grad * hid_eff
            grad_two[block, :] = grad
            grad_low[block, :] = grad_ffn.astype(BF16)
            terms = (grad_ffn, grad_final * normed, grad_final, grad * ffn_out)
            totals = [part + column_sum(term) for part, term in zip(totals, terms, strict=True)]
        sums[...] = jnp.zeros_like(sums)
        for place, part in enumerate(totals):
            sums[place : place + 1, :] = part
        for copy in late:
            copy.start()

    def backward(chunk, out):
        at = pl.multiple_of(chunk * cols, cols)
        out[...] = by_rows(inner[:, pl.ds(at, cols)], grad_low[...]).astype(BF16)

    pl.when(step >= 2 * chunks)(lambda: backward(step - chunks, weight_other))

    @pl.when(step == 3 * chunks - 1)
    def _():
        for copy in late:
            copy.wait()


def feed_forward(
    meta, hidden, cotangent, gated, outs, vectors, packs, ins, ffns, cols=768, row_step=480, after=()
):
    width = hidden.shape[1]
    half = gated[0].shape[1]
    units = ins[0].shape[1]
    chunks = units // cols
    column = pl.BlockSpec((ROWS, cols), lambda i, meta: (0, jnp.minimum(i, 2 * chunks - 1)))

    def part(first, i):
        return jnp.clip(i - first, 0, chunks - 1)

    def across(first, rows):
        return pl.BlockSpec((rows, cols), lambda i, meta: (0, part(first, i)))

    def down(first):
        return pl.BlockSpec((cols, width), lambda i, meta: (part(first, i), 0))

    low = bf16(ROWS, width)
    held = pltpu.VMEM((ROWS, width), BF16)
    wide = pltpu.VMEM((ROWS, width), F32)
    return call(
        "feed_forward",
        partial(ffn_body, chunks, row_step),
        (3 * chunks,),
        32,
        [meta],
        [
            (hidden, own_rows(width)),
            (cotangent, HBM),
            (gated[0], whole(ROWS, half)),
            (gated[1], whole(ROWS, half)),
            (outs[0], whole(half, width)),
            (outs[1], whole(half, width)),
            (vectors, whole(*vectors.shape)),
            (packs[0], across(0, packs[0].shape[0])),
            (packs[1], across(chunks, packs[1].shape[0])),
            (ins[0], across(0, width)),
            (ins[1], across(chunks, width)),
            (ffns[0], down(0)),
            (ffns[1], down(chunks)),
        ],
        [(low, HBM)] * 5
        + [
            (f32(ROWS, width), HBM),
            (f32(ROWS, 128), whole(ROWS, 128)),
            (bf16(ROWS, 2 * units), column),
            (bf16(ROWS, 2 * units), column),
            (bf16(units, width), down(2 * chunks)),
            (f32(8, width), whole(8, width)),
        ],
        scratch=[
            wide,
            wide,
            pltpu.VMEM((ROWS, 2 * units), BF16),
            held,
            held,
            held,
            held,
            held,
            held,
            wide,
            pltpu.SemaphoreType.DMA((7,)),
        ],
        after=after,
    )


def outer_body(left, right, out):
    out[...] = by_rows(left[...], right[...]).astype(BF16)


def outer(left, right, cols, after=(), step=512):
    width = right.shape[1]
    first = cols.start // step
    size = cols.stop - cols.start
    return call(
        "outer",
        outer_body,
        (size // step,),
        5,
        [],
        [
            (left, pl.BlockSpec((ROWS, step), lambda i: (0, i + first))),
            (right, whole(ROWS, width)),
        ],
        [(bf16(size, width), pl.BlockSpec((step, width), lambda i: (i, 0)))],
        after=after,
        vmem=16,
    )[0]


def shrink_body(
    chunks,
    row_step,
    grad_low,
    first_low_hbm,
    before_hbm,
    inner,
    slope,
    weight_in,
    weight_out,
    weight_grad,
    grad_first,
    unit_sums,
    kept,
    total,
    first_low,
    before,
    done,
):
    step = pl.program_id(0)
    fetch_low = pltpu.make_async_copy(first_low_hbm, first_low, done.at[0])
    fetch_before = pltpu.make_async_copy(before_hbm, before, done.at[1])

    @pl.when(step == 0)
    def _():
        fetch_low.start()
        fetch_before.start()

    bias_sum = jnp.zeros((1, inner.shape[1]), F32)
    gate_sum = jnp.zeros((1, inner.shape[1]), F32)
    for block in blocks_of(row_step):
        grad_inner = by_cols(grad_low[block, :], weight_out[...])
        grad_pre = grad_inner * slope[block, :].astype(F32)
        bias_sum += column_sum(grad_pre)
        gate_sum += column_sum(inner[block, :].astype(F32) * grad_inner)
        low = grad_pre.astype(BF16)
        kept[block, :] = low
        back = by_cols(low, weight_in[...])

        @pl.when(step == 0)
        def _(block=block, back=back):
            total[block, :] = back

        @pl.when((step > 0) & (step < chunks - 1))
        def _(block=block, back=back):
            total[block, :] += back

        @pl.when(step == chunks - 1)
        def _(block=block, back=back):
            if block.start == 0:
                fetch_before.wait()
            grad_first[block, :] = total[block, :] + back + before[block, :]

    unit_sums[...] = jnp.zeros_like(unit_sums)
    unit_sums[0:1, :] = bias_sum
    unit_sums[1:2, :] = gate_sum
    pl.when(step == 0)(fetch_low.wait)
    weight_grad[...] = by_rows(first_low[...], kept[...]).astype(BF16)


def shrink(
    side, grad_low, first_low, before, inner, slope, weight_in, weight_out, cols=512, row_step=960, after=()
):
    width, units = weight_in.shape
    chunks = units // cols
    full = whole(ROWS, width)
    across = pl.BlockSpec((width, cols), lambda i: (0, i))
    column = pl.BlockSpec((ROWS, cols), lambda i: (0, i + side * chunks))
    return call(
        "shrink",
        partial(shrink_body, chunks, row_step),
        (chunks,),
        12,
        [],
        [
            (grad_low, full),
            (first_low, HBM),
            (before, HBM),
            (inner, column),
            (slope, column),
            (weight_in, across),
            (weight_out, pl.BlockSpec((cols, width), lambda i: (i, 0))),
        ],
        [
            (bf16(width, units), across),
            (f32(ROWS, width), full),
            (f32(8, units), pl.BlockSpec((8, cols), lambda i: (0, i))),
        ],
        scratch=[
            pltpu.VMEM((ROWS, cols), BF16),
            pltpu.VMEM((ROWS, width), F32),
            pltpu.VMEM((ROWS, width), BF16),
            pltpu.VMEM((ROWS, width), F32),
            pltpu.SemaphoreType.DMA((2,)),
        ],
        after=after,
        vmem=36,
    )


def part_body(
    grad_first, normed_one, spread_one, attn_out, vectors, gated_own, gated_other, grad_one, low, weight_mine, weight_other, sums
):
    gain = row_of(vectors, LN1_GAIN)
    hid_eff = row_of(vectors, HID_EFF)
    totals = [jnp.zeros((1, grad_first.shape[1]), F32)] * 4
    for block in blocks_of(120):
        grad = grad_first[block, :]
        normed = normed_one[block, :].astype(F32)
        one = norm_back(grad, normed, spread_one[block, 0:1], gain)
        grad_one[block, :] = one
        attn = one * hid_eff
        low[block, :] = attn.astype(BF16)
        terms = (attn, grad * normed, grad, one * attn_out[block, :].astype(F32))
        totals = [part + column_sum(term) for part, term in zip(totals, terms, strict=True)]
    sums[...] = jnp.zeros_like(sums)
    for place, part in enumerate(totals):
        sums[place : place + 1, :] = part
    weight_other[...] = by_rows(gated_other[...], low[...]).astype(BF16)
    weight_mine[...] = by_rows(gated_own[...], low[...]).astype(BF16)


def part_norm(grad_first, normed_one, spread_one, attn_out, vectors, gated, after=()):
    width = grad_first.shape[1]
    half = gated[0].shape[1]
    values = [grad_first, normed_one, spread_one, attn_out, vectors, *gated]
    made = [
        f32(ROWS, width),
        bf16(ROWS, width),
        bf16(half, width),
        bf16(half, width),
        f32(8, width),
    ]
    return call(
        "part_norm",
        part_body,
        (1,),
        6,
        [],
        [(value, whole(*value.shape)) for value in values],
        [(shape, whole(*shape.shape)) for shape in made],
        after=after,
        vmem=28,
    )


def part_heads_body(
    head_width, low, gated_own, gated_other, out_own, out_other, pack_own, pack_other, context_own, context_other, means_own, means_other, sums
):
    half = gated_own.shape[1]
    head = lax.broadcasted_iota(jnp.int32, (8, half), 1) // head_width
    pick = (head == lax.broadcasted_iota(jnp.int32, (8, half), 0)).astype(BF16)
    sums[...] = jnp.zeros_like(sums)
    for place, (gated, weight, pack, context, means) in enumerate(
        (
            (gated_own, out_own, pack_own, context_own, means_own),
            (gated_other, out_other, pack_other, context_other, means_other),
        )
    ):
        column = jnp.zeros((1, half), F32)
        for start, size in BUCKETS:
            rows = slice(start, start + size)
            grads = by_cols(low[rows, :], weight[...])
            context[rows, :] = (grads * pack[PACK_HEAD : PACK_HEAD + 1, 0:half]).astype(BF16)
            terms = grads * gated[rows, :].astype(F32)
            column += column_sum(terms)
            high = terms.astype(BF16)
            rest = (terms - high.astype(F32)).astype(BF16)
            means[:, rows] = by_cols(pick, high) + by_cols(pick, rest)
        sums[place : place + 1, :] = column


def part_heads(low, gated, outs, packs, head_width, after=()):
    half = gated[0].shape[1]
    values = [low, *gated, *outs, *packs]
    made = [
        bf16(ROWS, half),
        bf16(ROWS, half),
        f32(8, ROWS),
        f32(8, ROWS),
        f32(8, half),
    ]
    return call(
        "part_heads",
        partial(part_heads_body, head_width),
        (1,),
        5,
        [],
        [(value, whole(*value.shape)) for value in values],
        [(shape, whole(*shape.shape)) for shape in made],
        after=after,
        vmem=28,
    )


def add_back_body(start, *refs):
    grads, weights, out = refs[:6], refs[6:12], refs[12]
    total = start[...]
    for side in (0, 3):
        left = jnp.concatenate([part[...] for part in grads[side : side + 3]], 1)
        right = jnp.concatenate([part[...] for part in weights[side : side + 3]], 1)
        total += by_cols(left, right)
    out[...] = total


def add_back(start, grads, weights, after=()):
    width = start.shape[1]
    half = grads[0].shape[1]
    step = ROWS // 4
    return call(
        "add_back",
        add_back_body,
        (4,),
        6,
        [],
        [(start, pl.BlockSpec((step, width), lambda i: (i, 0)))]
        + [(part, pl.BlockSpec((step, half), lambda i: (i, 0))) for part in grads]
        + [(part, whole(width, half)) for part in weights],
        [(f32(ROWS, width), pl.BlockSpec((step, width), lambda i: (i, 0)))],
        after=after,
        vmem=24,
    )[0]


def swap_bit(values, dp_size, bit):
    return lax.ppermute(values, "dp", [(at, at ^ (1 << bit)) for at in range(dp_size)])


TAIL = 128


def load(ref, rows, tail):
    values = ref[rows, :].astype(F32)
    if not tail:
        return values, None
    cut = values.shape[1] - TAIL
    return values[:, :cut], values[:, cut : cut + TAIL // 2] + values[:, cut + TAIL // 2 :]


def store(ref, main, extra):
    if extra is None:
        ref[...] = main.astype(ref.dtype)
        return
    cut = main.shape[1]
    high = extra.astype(BF16)
    ref[:, :cut] = main.astype(BF16)
    ref[:, cut : cut + TAIL // 2] = high
    ref[:, cut + TAIL // 2 :] = (extra - high.astype(F32)).astype(BF16)


def split_by(side, totals, kept, sent):
    for part, total in enumerate(totals):

        @pl.when(side == part)
        def _(total=total):
            store(kept, *total)

        @pl.when(side != part)
        def _(total=total):
            store(sent, *total)


def add(left, right):
    return tuple(None if a is None else a + b for a, b in zip(left, right, strict=True))


class Stream:
    def __init__(self, ins, shape, first, order, tail=False):
        self.ins = ins
        self.rows, self.cols = shape
        self.first = first
        self.order = order
        self.tail = tail
        self.stage = 0
        self.kept = self.value = self.arrived = None

    def job(self):
        stages = len(self.order)
        stage, tail = self.stage, self.tail
        size = self.rows >> stage if stage <= stages else self.value.shape[0]
        if stage < stages:
            half = size // 2
            ins = list(self.ins) if stage == 0 else [self.kept, self.arrived]

            def body(sides, *refs):
                *given, kept, sent = refs
                totals = []
                for at in (0, half):
                    rows = slice(at, at + half)
                    if stage == 0:
                        totals.append(self.first(given, rows))
                    else:
                        totals.append(add(*[load(ref, rows, tail) for ref in given]))
                split_by(sides[self.order[stage]], totals, kept, sent)

            return ins, [bf16(half, self.cols)] * 2, body
        if stage == stages:

            def body(sides, kept, arrived, value):
                rows = slice(0, size)
                store(value, *add(load(kept, rows, tail), load(arrived, rows, tail)))

            return [self.kept, self.arrived], [bf16(size, self.cols)], body
        bit = self.order[2 * stages - stage]

        def body(sides, own, arrived, value):
            for first, halves in in_order(sides[bit], own, arrived):

                @pl.when(first)
                def _(halves=halves):
                    for place, half in enumerate(halves):
                        value[place * size : place * size + size, :] = half[...]

        return [self.value, self.arrived], [bf16(2 * size, self.cols)], body

    def take(self, outs, dp_size):
        stages = len(self.order)
        if self.stage < stages:
            self.kept, sent = outs
            self.arrived = swap_bit(sent, dp_size, self.order[self.stage])
        else:
            (self.value,) = outs
            bit = self.order[2 * stages - 1 - self.stage]
            self.arrived = swap_bit(self.value, dp_size, bit)
        self.stage += 1

    def last(self):
        return self.stage == 2 * len(self.order)


class Gather:
    def __init__(self, streams, order):
        self.streams = streams
        self.order = order
        self.stage = 0
        self.value = self.arrived = None

    def job(self):
        stage = self.stage
        if stage == 0:
            ins = [part for stream in self.streams for part in (stream.kept, stream.arrived)]
            size = self.streams[0].kept.shape[0]

            def body(sides, *refs):
                *given, value = refs
                at = 0
                for stream, kept, arrived in zip(
                    self.streams, given[::2], given[1::2], strict=True
                ):
                    rows, tail = slice(0, size), stream.tail
                    total = add(load(kept, rows, tail), load(arrived, rows, tail))
                    store(value.at[:, at : at + stream.cols], *total)
                    at += stream.cols

            cols = sum(stream.cols for stream in self.streams)
            return ins, [bf16(size, cols)], body
        size, cols = self.value.shape

        def body(sides, own, arrived, value):
            for first, halves in in_order(sides[self.order[stage - 1]], own, arrived):

                @pl.when(first)
                def _(halves=halves):
                    for place, half in enumerate(halves):
                        value[place * size : place * size + size, :] = half[...]

        return [self.value, self.arrived], [bf16(2 * size, cols)], body

    def take(self, outs, dp_size):
        (self.value,) = outs
        self.arrived = swap_bit(self.value, dp_size, self.order[self.stage])
        self.stage += 1

    def last(self):
        return self.stage == len(self.order)


class Quad:
    def __init__(self, front, beside, back, orders):
        self.front, self.beside, self.back = front, beside, back
        self.orders = orders
        self.stage = 0
        self.values = self.arrived = self.kept = None
        self.first, self.second = front.order[2:]

    def to_partners(self, values, dp_size):
        found = []
        for number, value in enumerate(values, 1):
            flip = (number >> 1) << self.first | (number & 1) << self.second
            pairs = [(at, at ^ flip) for at in range(dp_size)]
            found.append(lax.ppermute(value, "dp", pairs))
        return found

    def place(self, sides):
        return 2 * sides[self.first] + sides[self.second]

    def job(self):
        front, beside, back = self.front, self.beside, self.back
        width = front.cols + back.cols
        if self.stage == 0:
            size = front.rows // 16
            ins = [front.kept, front.arrived, back.kept, back.arrived]

            def body(sides, *refs):
                given, outs = refs[:4], refs[4:]
                totals = []
                for at in range(4):
                    rows = slice(at * size, (at + 1) * size)
                    one, _ = add(*[load(ref, rows, False) for ref in given[:2]])
                    two, extra = add(*[load(ref, rows, True) for ref in given[2:]])
                    totals.append((jnp.concatenate([one, two], 1), extra))
                for mine in range(4):

                    @pl.when(self.place(sides) == mine)
                    def _(mine=mine):
                        for number, out in enumerate(outs):
                            store(out, *totals[mine ^ number])

            return ins, [bf16(size, width)] * 4, body
        if self.stage == 1:
            size = self.kept.shape[0]
            ins = [self.kept, *self.arrived, beside.kept, beside.arrived]

            def body(sides, *refs):
                *given, out = refs
                rows = slice(0, size)
                total = load(given[0], rows, True)
                for ref in given[1:4]:
                    total = add(total, load(ref, rows, True))
                extra = add(*[load(ref, rows, False) for ref in given[4:]])[0]
                main = [total[0][:, : front.cols], extra, total[0][:, front.cols :]]
                store(out, jnp.concatenate(main, 1), total[1])

            return ins, [bf16(size, width + beside.cols)], body
        cut = front.cols + beside.cols
        if self.stage == 2:
            size = self.values[0].shape[0]

            def body(sides, *refs):
                given, outs = refs[:4], refs[4:]
                for mine in range(4):

                    @pl.when(self.place(sides) == mine)
                    def _(mine=mine):
                        for number, ref in enumerate(given):
                            at = mine ^ number
                            at = (at >> 1) + 2 * (at & 1) if self.swapped() else at
                            rows = slice(at * size, (at + 1) * size)
                            outs[0][rows, :] = ref[:, :cut]
                            outs[1][rows, :] = ref[:, cut:]

            made = [bf16(4 * size, cut), bf16(4 * size, back.cols)]
            return [self.values[0], *self.arrived], made, body
        size = self.values[0].shape[0]
        bits = [order[2] for order in self.orders]

        def body(sides, *refs):
            for at, bit in enumerate(bits):
                own, arrived, out = refs[2 * at], refs[2 * at + 1], refs[4 + at]
                for first, halves in in_order(sides[bit], own, arrived):

                    @pl.when(first)
                    def _(halves=halves, out=out):
                        for place, half in enumerate(halves):
                            out[place * size : place * size + size, :] = half[...]

        ins = [value for pair in zip(self.values, self.arrived, strict=True) for value in pair]
        return ins, [bf16(2 * size, cut), bf16(2 * size, back.cols)], body

    def swapped(self):
        return self.orders[0][0] == self.first

    def take(self, outs, dp_size):
        if self.stage == 0:
            self.kept = outs[0]
            self.arrived = self.to_partners(outs[1:], dp_size)
        elif self.stage == 1:
            self.values = list(outs)
            self.arrived = self.to_partners([outs[0]] * 3, dp_size)
        else:
            self.values = list(outs)
            self.arrived = [
                swap_bit(value, dp_size, order[self.stage])
                for value, order in zip(outs, self.orders, strict=True)
            ]
        self.stage += 1

    def gathers(self):
        found = []
        for at, streams in enumerate(([self.front, self.beside], [self.back])):
            gather = Gather(streams, self.orders[at])
            gather.value, gather.arrived = self.values[at], self.arrived[at]
            found.append(gather)
        return found


def in_order(side, own, arrived):
    return (side == 0, (own, arrived)), (side == 1, (arrived, own))


def small_call(name, body, ins, outs, sides, after=()):
    return call(
        name,
        body,
        (1,),
        2,
        [sides],
        [(value, whole(*value.shape)) for value in ins],
        [(shape, whole(*shape.shape)) for shape in outs],
        after=after,
        vmem=24,
    )


def advance(streams, dp_size, sides, after=()):
    jobs = [stream.job() for stream in streams]
    ins = [value for job in jobs for value in job[0]]
    outs = [shape for job in jobs for shape in job[1]]

    def body(sides, *refs):
        given, made = refs[: len(ins)], refs[len(ins) :]
        for inputs, shapes, work in jobs:
            work(sides, *given[: len(inputs)], *made[: len(shapes)])
            given, made = given[len(inputs) :], made[len(shapes) :]

    found = small_call("advance", body, ins, outs, sides, after)
    for stream, job in zip(streams, jobs, strict=True):
        stream.take(found[: len(job[1])], dp_size)
        found = found[len(job[1]) :]


def states(streams):
    return [stream.kept if stream.value is None else stream.value for stream in streams]


def blocks_in(gather):
    streams, order = gather.streams, gather.order
    bits = len(order)
    size = streams[0].rows >> bits
    for block in range(1 << bits):
        device = sum((block >> turn & 1) << bit for turn, bit in enumerate(order))
        half, inside = divmod(block, 1 << (bits - 1))
        places = [
            size
            * sum((device >> bit & 1) << (bits - 1 - turn) for turn, bit in enumerate(stream.order))
            for stream in streams
        ]
        yield half, slice(inside * size, (inside + 1) * size), places, size


def finish(gathers, sides, by_cols, after=()):
    rows, cols = gathers[0].streams[0].rows, gathers[0].streams[0].cols

    def body(sides, *refs):
        *given, out = refs
        for at, gather in enumerate(gathers):
            pair = given[2 * at : 2 * at + 2]
            top, left = (0, at * cols) if by_cols else (at * rows, 0)
            for first, halves in in_order(sides[gather.order[-1]], *pair):

                @pl.when(first)
                def _(gather=gather, halves=halves, top=top, left=left):
                    for half, where, (row,), size in blocks_in(gather):
                        out[top + row : top + row + size, left : left + cols] = halves[half][
                            where, :
                        ].astype(F32)

    ins = [value for gather in gathers for value in (gather.value, gather.arrived)]
    shape = (rows, 2 * cols) if by_cols else (2 * rows, cols)
    return small_call("finish", body, ins, [f32(*shape)], sides, after)[0]


def orders_of(dp_size):
    bits = dp_size.bit_length() - 1
    if bits == 4:
        halved = (0, 1, 2, 3), (1, 0, 2, 3), (2, 0, 1, 3), (0, 2, 3, 1), (0, 1, 2, 3), (1, 0, 2, 3)
        doubled = (1, 3, 2, 0), (3, 1, 0, 2), (3, 0, 1, 2), (3, 2, 1, 0), (3, 2, 0, 1), (0, 3, 2, 1)
        return halved + doubled
    return tuple(tuple((at + turn) % bits for at in range(bits)) for turn in range(12))


def late_streams(qkv, small, orders):
    rows, cols = qkv[0].shape
    cut = -(-(cols + TAIL) // 256) * 128
    places = small[0].shape[1] // (TAIL // 2)
    depth = small[0].shape[0]

    def front(given, where):
        return sum(ref[where, 0:cut].astype(F32) for ref in given), None

    def back(given, where):
        first, size = where.start, where.stop - where.start
        main = sum(ref[where, cut:cols].astype(F32) for ref in given[0:2])
        extra = []
        for place in range(first // depth, (first + size) // depth):
            if place < places:
                at = slice(place * TAIL // 2, (place + 1) * TAIL // 2)
                extra.append(sum(ref[:, at] for ref in given[2:4]))
        used = depth * len(extra)
        if used < size:
            extra.append(jnp.zeros((size - used, TAIL // 2), F32))
        return main, jnp.concatenate(extra, 0)

    return [
        Stream(qkv, (rows, cut), front, orders[0]),
        Stream((*qkv, *small), (rows, cols - cut + TAIL), back, orders[1], True),
    ]


def finish_late(gathers, sides, lanes, small_shape, after=()):
    (front, out_stream), (back,) = [gather.streams for gather in gathers]
    rows, half = front.rows, out_stream.cols
    depth, width = small_shape
    cut = front.cols
    places = width // (TAIL // 2)

    def body(sides, own0, arrived0, own1, arrived1, qkv_out, out_out, small_out):
        def qkv_part(values, row, where, first, cols):
            for at in range(0, cols, lanes):
                pair, kind = divmod((first + at) // lanes, 3)
                columns = slice(pair * lanes, (pair + 1) * lanes)
                lines = slice(row, row + where.stop - where.start)
                qkv_out[lines, kind, columns] = values[where, at : at + lanes].astype(F32)

        for first, halves in in_order(sides[gathers[0].order[-1]], own0, arrived0):

            @pl.when(first)
            def _(halves=halves):
                for number, where, (row, other_row), size in blocks_in(gathers[0]):
                    qkv_part(halves[number], row, where, 0, cut)
                    side = other_row // half
                    line = other_row - side * half
                    out_out[line : line + size, side * half : (side + 1) * half] = halves[number][
                        where, cut : cut + half
                    ].astype(F32)

        for first, halves in in_order(sides[gathers[1].order[-1]], own1, arrived1):

            @pl.when(first)
            def _(halves=halves):
                for number, where, (row,), size in blocks_in(gathers[1]):
                    qkv_part(halves[number], row, where, cut, back.cols - TAIL)
                    cuts = sorted({row, row + size, *range(-(-row // depth) * depth, row + size, depth)})
                    for at, end in zip(cuts, cuts[1:]):
                        place, line = divmod(at, depth)
                        count = end - at
                        if place < places:
                            top = where.start + at - row
                            _, extra = load(halves[number], slice(top, top + count), True)
                            columns = slice(place * TAIL // 2, (place + 1) * TAIL // 2)
                            small_out[line : line + count, columns] = extra

    ins = [value for gather in gathers for value in (gather.value, gather.arrived)]
    outs = [f32(rows, 3, half), f32(half, rows), f32(depth, width)]
    return small_call("finish_late", body, ins, outs, sides, after)


def pack_sums(part_sums, turn_sums, head_sums, bias_sums, unit_sums, after=()):
    width = part_sums.shape[1]
    half = bias_sums[0].shape[1]
    unit_rows = unit_sums[0].shape[1] // width

    def body(part, turned, heads, bias_own, bias_other, unit_own, unit_other, mine, theirs):
        sides = ((mine, bias_own, unit_own), (theirs, bias_other, unit_other))
        for side, (out, bias, unit) in enumerate(sides):
            out[...] = jnp.zeros_like(out)
            out[0:4, :] = part[0:4, :]
            out[4:8, :] = turned[0:4, :]
            out[8:9, 0:half] = bias[0:1, :]
            out[8:9, half : 2 * half] = bias[1:2, :]
            out[9:10, 0:half] = heads[side : side + 1, :]
            for kind in (0, 1):
                for row in range(unit_rows):
                    place = 10 + kind * unit_rows + row
                    out[place : place + 1, :] = unit[
                        kind : kind + 1, row * width : (row + 1) * width
                    ]

    values = [part_sums, turn_sums, head_sums, *bias_sums, *unit_sums]
    rows = -(-(10 + 2 * unit_rows) // 8) * 8
    return call(
        "pack_sums",
        body,
        (1,),
        1,
        [],
        [(value, whole(*value.shape)) for value in values],
        [(f32(rows, width), whole(rows, width))] * 2,
        after=after,
        vmem=24,
    )


def per_device(
    dp_size,
    hidden,
    cotangent,
    counts,
    lengths,
    qkv_weight,
    qv_bias,
    out_weight,
    out_bias,
    ln1_gain,
    ln1_bias,
    in_weight,
    in_bias,
    ffn_out_weight,
    ffn_out_bias,
    ln2_gain,
    ln2_bias,
    head_gate,
    head_mask,
    ffn_gate,
    ffn_mask,
    hidden_gate,
    hidden_mask,
):
    width = hidden.shape[1]
    own_heads = head_gate.shape[0]
    half = qkv_weight.shape[2]
    units = in_weight.shape[1]
    head_width = half // own_heads
    head_at = lax.axis_index("head")

    def other(values):
        return lax.ppermute(values, "head", [(0, 1), (1, 0)])

    def pad_to(values, size):
        return jnp.pad(values, (0, size - values.shape[0]))

    meta = jnp.concatenate(
        [
            lax.dynamic_index_in_dim(
                jnp.where(counts[0] > 0, lengths[0], 0), head_at, 0, keepdims=False
            ),
            head_at[None],
        ]
    )
    head_flags = head_mask.astype(F32)
    ffn_flags = ffn_mask.astype(F32)
    hidden_flags = hidden_mask.astype(F32)
    pack = jnp.stack(
        [
            in_bias,
            ffn_gate * ffn_flags,
            pad_to(qv_bias.reshape(-1), units),
            pad_to(jnp.repeat(head_gate * head_flags, head_width), units),
        ]
    )
    vectors = jnp.stack(
        [
            out_bias,
            ln1_gain,
            ln1_bias,
            ffn_out_bias,
            ln2_gain,
            ln2_bias,
            hidden_gate * hidden_flags,
        ]
    )
    qkv_own = [qkv_weight[:, at] for at in range(3)]
    qkv_other = [other(part) for part in qkv_own]
    packs = (pack, other(pack))
    outs = (out_weight, other(out_weight))
    ins = (in_weight, other(in_weight))
    ffns = (ffn_out_weight, other(ffn_out_weight))
    sides = jnp.stack([(lax.axis_index("dp") >> bit) & 1 for bit in range(dp_size.bit_length() - 1)])
    orders = orders_of(dp_size)
    step = partial(advance, dp_size=dp_size, sides=sides)

    def halves(size, at):
        return slice(at * size // 2, (at + 1) * size // 2)

    def sum_stream(left, right, order, rows=None, cols=None):
        rows = rows or slice(0, left.shape[0])
        cols = cols or slice(0, left.shape[1])

        def first(given, at):
            at = slice(rows.start + at.start, rows.start + at.stop)
            return sum(ref[at, cols].astype(F32) for ref in given), None

        shape = (rows.stop - rows.start, cols.stop - cols.start)
        return Stream((left, right), shape, first, order)

    *qkv0, gated0, logs0 = attend(meta, hidden, qkv_own, packs[0], head_width)
    *qkv1, gated1, logs1 = attend(meta, hidden, qkv_other, packs[1], head_width, [gated0])
    gated = (gated0, gated1)
    (
        layer_out,
        first_low,
        normed_one,
        attn_out,
        grad_low,
        grad_two,
        spread_one,
        inner,
        slope,
        ffn_grad_other,
        turn_sums,
    ) = feed_forward(meta, hidden, cotangent, gated, outs, vectors, packs, ins, ffns)
    ffn_grad_theirs = other(ffn_grad_other)
    ffn_grad_mine = outer(inner, grad_low, slice(0, units))
    streams = [
        sum_stream(ffn_grad_mine, ffn_grad_theirs, orders[at], rows=halves(units, at))
        for at in (0, 1)
    ]
    step(streams)
    in_grad_other, grad_first, unit_sums1 = shrink(
        1, grad_low, first_low, grad_two, inner, slope, ins[1], ffns[1], after=states(streams)
    )
    in_grad_theirs = other(in_grad_other)
    step(streams, after=[grad_first])
    in_grad_mine, grad_first, unit_sums0 = shrink(
        0, grad_low, first_low, grad_first, inner, slope, ins[0], ffns[0], after=states(streams)
    )
    in_streams = [
        sum_stream(in_grad_mine, in_grad_theirs, orders[2 + at], cols=halves(units, at))
        for at in (0, 1)
    ]
    streams += in_streams
    step(streams, after=[grad_first])
    grad_one, attn_low, out_grad_mine, out_grad_other, part_sums = part_norm(
        grad_first,
        normed_one,
        spread_one,
        attn_out,
        vectors,
        gated,
        after=states(streams),
    )
    out_grad_theirs = other(out_grad_other)
    grad_context0, grad_context1, means0, means1, head_sums = part_heads(
        attn_low, gated, outs, packs, head_width
    )

    def out_part(given, at):
        side = at.start // half
        rows = slice(at.start - side * half, at.stop - side * half)
        cols = slice(side * half, (side + 1) * half)
        return sum(ref[rows, cols].astype(F32) for ref in given), None

    out_stream = Stream((out_grad_mine, out_grad_theirs), (width, half), out_part, orders[4])
    streams = [*streams[:2], out_stream]
    step(streams, after=[grad_context0])
    *mixed1, qkv_grad_other, bias_sums1 = attend_back(
        meta,
        hidden,
        qkv1,
        grad_context1,
        logs1,
        means1,
        packs[1],
        head_width,
        after=states(streams),
    )
    qkv_grad_theirs = other(qkv_grad_other)
    ffn_gathers = [Gather(streams[at : at + 1], orders[(6, 11)[at]]) for at in (0, 1)]
    streams = [*ffn_gathers, *in_streams, out_stream]
    step(streams, after=[mixed1[0]])
    *mixed0, qkv_grad_mine, bias_sums0 = attend_back(
        meta,
        hidden,
        qkv0,
        grad_context0,
        logs0,
        means0,
        packs[0],
        head_width,
        after=states(streams) + [mixed1[0]],
    )
    step(streams, after=[mixed0[0]])
    small = pack_sums(
        part_sums,
        turn_sums,
        head_sums,
        (bias_sums0, bias_sums1),
        (unit_sums0, unit_sums1),
        after=states(streams),
    )
    late = late_streams(
        (qkv_grad_mine, qkv_grad_theirs), (small[0], other(small[1])), orders[4:6]
    )
    step(late)
    grad_hidden = add_back(
        grad_one, mixed0 + mixed1, qkv_own + qkv_other, after=states(streams + late)
    )
    step([*ffn_gathers, *in_streams, out_stream, *late], after=[grad_hidden])
    gathers = [Gather(in_streams[at : at + 1], orders[7 + at]) for at in (0, 1)]
    if dp_size == 16:
        quad = Quad(late[0], out_stream, late[1], orders[9:11])
        step([*ffn_gathers, *gathers, quad])
        step([*gathers, quad], after=[gather.arrived for gather in ffn_gathers])
        step([*gathers, quad])
        step([*gathers, quad])
        late = quad.gathers()
    else:
        while late[0].stage < len(late[0].order):
            step(late)
        while out_stream.stage < len(out_stream.order):
            step([out_stream])
        late = [Gather([late[0], out_stream], orders[9]), Gather([late[1]], orders[10])]
        for gather in gathers:
            while not gather.last():
                step([gather])
        for gather in ffn_gathers:
            while not gather.last():
                step([gather])
        while not late[0].last():
            step(late)
    grad_ffn_out_weight = finish(ffn_gathers, sides, by_cols=False)
    grad_in_weight = finish(gathers, sides, by_cols=True)
    grad_qkv_weight, grad_out_weight, small = finish_late(
        late, sides, 2 * head_width, small[0].shape
    )
    (
        grad_out_bias,
        grad_ln1_gain,
        grad_ln1_bias,
        gate_one,
        grad_ffn_out_bias,
        grad_ln2_gain,
        grad_ln2_bias,
        gate_two,
    ) = small[:8]
    unit_rows = units // width
    return (
        layer_out,
        grad_hidden,
        grad_qkv_weight,
        small[8].reshape(2, half),
        grad_out_weight,
        grad_out_bias,
        grad_ln1_gain,
        grad_ln1_bias,
        grad_in_weight,
        small[10 : 10 + unit_rows].reshape(-1),
        grad_ffn_out_weight,
        grad_ffn_out_bias,
        grad_ln2_gain,
        grad_ln2_bias,
        jnp.sum(small[9, :half].reshape(own_heads, head_width), 1) * head_flags / head_gate,
        small[10 + unit_rows : 10 + 2 * unit_rows].reshape(-1) * ffn_flags / ffn_gate,
        (gate_one + gate_two) * hidden_flags,
    )


def solution(mesh):
    placed = (
        P("dp", None),
        P("dp", None),
        P("dp", None, None),
        P("dp", None, None),
        P(None, None, "head"),
        P(None, "head"),
        P("head", None),
        P(),
        P(),
        P(),
        P(None, "head"),
        P("head"),
        P("head", None),
        P(),
        P(),
        P(),
        P("head"),
        P("head"),
        P("head"),
        P("head"),
        P(),
        P(),
    )
    return jax.shard_map(
        partial(per_device, mesh.shape["dp"]),
        mesh=mesh,
        in_specs=placed,
        out_specs=(
            P(("dp", "head"), None),
            P(("dp", "head"), None),
            P(None, None, "head"),
            P(None, "head"),
            P("head", None),
            P(),
            P(),
            P(),
            P(None, "head"),
            P("head"),
            P("head", None),
            P(),
            P(),
            P(),
            P("head"),
            P("head"),
            P(),
        ),
        check_vma=False,
    )
```

```python
from functools import partial

import jax
import jax.numpy as jnp
from jax import lax
from jax.experimental import pallas as pl
from jax.experimental.pallas import tpu as pltpu
from jax.sharding import PartitionSpec as P

BASE = 64
ROWS = 15 * BASE
EPSILON = 1e-12
MASKED = -1e9
LOG2E = 1.4426950408889634
BUCKETS = ((0, 8 * BASE), (8 * BASE, 4 * BASE), (12 * BASE, 2 * BASE), (14 * BASE, BASE))
F32 = jnp.float32
BF16 = jnp.bfloat16
MEBI = 1 << 20
HBM = pl.BlockSpec(memory_space=pl.ANY)


def dot(left, right):
    return jnp.dot(left, right, preferred_element_type=F32)


def by_rows(left, right):
    return lax.dot_general(left, right, (((0,), (0,)), ((), ())), preferred_element_type=F32)


def by_cols(left, right):
    return lax.dot_general(left, right, (((1,), (1,)), ((), ())), preferred_element_type=F32)


def f32(*shape):
    return jax.ShapeDtypeStruct(shape, F32)


def bf16(*shape):
    return jax.ShapeDtypeStruct(shape, BF16)


def whole(*shape):
    return pl.BlockSpec(shape, lambda *_: (0,) * len(shape))


def call(name, body, grid, micros, scalars, ins, outs, scratch=(), after=(), vmem=58):
    first = len(scalars) + len(ins)

    def run(*refs):
        body(*refs[:first], *refs[first + len(after) :])

    return pl.pallas_call(
        run,
        grid_spec=pltpu.PrefetchScalarGridSpec(
            num_scalar_prefetch=len(scalars),
            grid=grid,
            in_specs=[spec for _, spec in ins] + [HBM] * len(after),
            out_specs=[spec for _, spec in outs],
            scratch_shapes=list(scratch),
        ),
        out_shape=[shape for shape, _ in outs],
        compiler_params=pltpu.CompilerParams(
            dimension_semantics=("arbitrary",) * len(grid), vmem_limit_bytes=vmem * MEBI
        ),
        cost_estimate=pl.CostEstimate(
            flops=int(micros * 5e9), bytes_accessed=1 << 20, transcendentals=0
        ),
        name=name,
    )(*scalars, *[value for value, _ in ins], *after)


def row_of(vectors, at):
    return vectors[at : at + 1, :]


def column_sum(values):
    return jnp.sum(values, 0, keepdims=True)


def own_rows(width):
    return pl.BlockSpec((ROWS, width), lambda i, meta: (meta[4], 0))


PACK_IN_BIAS, PACK_FFN, PACK_QV, PACK_HEAD = range(4)


def side_masks(lanes):
    low = lax.broadcasted_iota(jnp.int32, (1, lanes), 1) < lanes // 2
    return low, low.astype(BF16), 1 - low.astype(BF16)


def kept_head(gate, side):
    half = gate.shape[1] // 2
    return jnp.max(gate[PACK_HEAD : PACK_HEAD + 1, side * half : (side + 1) * half]) > 0


def for_kept(gate, run):
    flags = [kept_head(gate, side) for side in (0, 1)]
    for sides in ((0, 1), (0,), (1,), ()):
        case = [flags[side] if side in sides else jnp.logical_not(flags[side]) for side in (0, 1)]
        pl.when(case[0] & case[1])(partial(run, sides))


def attend_body(
    pairs, lanes, meta, hidden, weight_q, weight_k, weight_v, bias_q, bias_v, gate, query, key, value, gated, logs, columns, context
):
    pair = pl.program_id(0)
    weight = jnp.concatenate([weight_q[...], weight_k[...], weight_v[...]], 1)
    mixed = dot(hidden[...], weight)
    query[...] = (mixed[:, :lanes] + bias_q[PACK_QV : PACK_QV + 1, :]).astype(BF16)
    key[...] = mixed[:, lanes : 2 * lanes].astype(BF16)
    value[...] = (mixed[:, 2 * lanes :] + bias_v[PACK_QV : PACK_QV + 1, :]).astype(BF16)
    scale = LOG2E * (lanes // 2) ** -0.5
    low_side, *masks = side_masks(lanes)
    lane = lax.broadcasted_iota(jnp.int32, (1, 128), 1)

    def run(sides):
        for place, (start, size) in enumerate(BUCKETS):
            rows = slice(start, start + size)
            seen = lax.broadcasted_iota(jnp.int32, (1, size), 1) < meta[place]
            shut = jnp.where(seen, 0.0, MASKED).astype(F32)
            queries, keys, values = query[rows, :], key[rows, :], value[rows, :]
            total_context = jnp.zeros((size, lanes), F32)
            column = columns[rows, :]
            for side in sides:
                scores = by_cols(queries * masks[side], keys) + shut
                top = jnp.max(scores, -1, keepdims=True)
                power = jnp.exp2((scores - top) * scale)
                total = jnp.sum(power, -1, keepdims=True)
                found = dot(power.astype(BF16), values) * (1.0 / total)
                log = top * scale + jnp.log2(total)
                column = jnp.where(lane == 2 * pair + side, log, column)
                total_context = jnp.where(low_side == (side == 0), found, total_context)
            columns[rows, :] = column
            context[rows, :] = total_context

    for_kept(gate, run)
    gated[...] = (context[...] * gate[PACK_HEAD : PACK_HEAD + 1, :]).astype(BF16)

    @pl.when(pair == pairs - 1)
    def _():
        for start, size in BUCKETS:
            rows = slice(start, start + size)
            logs[:, rows] = columns[rows, :].T[0:8, :]


def attend(meta, hidden, weights, pack, head_width, after=()):
    width, half = weights[0].shape
    lanes = 2 * head_width
    pairs = half // lanes
    column = pl.BlockSpec((ROWS, lanes), lambda i, meta: (0, i))
    weight = pl.BlockSpec((width, lanes), lambda i, meta: (0, i))

    def vector(shift):
        return pl.BlockSpec((pack.shape[0], lanes), lambda i, meta: (0, i + shift))

    return call(
        "attend",
        partial(attend_body, pairs, lanes),
        (pairs,),
        9,
        [meta],
        [(hidden, own_rows(width))]
        + [(part, weight) for part in weights]
        + [(pack, vector(0)), (pack, vector(pairs)), (pack, vector(0))],
        [(bf16(ROWS, half), column)] * 4 + [(f32(8, ROWS), whole(8, ROWS))],
        scratch=[pltpu.VMEM((ROWS, 128), F32), pltpu.VMEM((ROWS, lanes), F32)],
        after=after,
        vmem=58,
    )


def pick_row(values, at):
    place = lax.broadcasted_iota(jnp.int32, values.shape, 0)
    return column_sum(jnp.where(place == at, values, 0.0))


def attend_back_body(
    lanes, meta, hidden, query, key, value, grad_context, logs, means, gate, grad_q, grad_k, grad_v, weight_grad, bias_sums, *totals
):
    pair = pl.program_id(0)
    scale = LOG2E * (lanes // 2) ** -0.5
    final = (lanes // 2) ** -0.5
    _, *masks = side_masks(lanes)

    def run(sides):
        for place, (start, size) in enumerate(BUCKETS):
            rows = slice(start, start + size)
            seen = lax.broadcasted_iota(jnp.int32, (size, 1), 0) < meta[place]
            shut = jnp.where(seen, 0.0, MASKED).astype(F32)
            queries, keys, values = query[rows, :], key[rows, :], value[rows, :]
            grads = grad_context[rows, :]
            sums = [jnp.zeros((size, lanes), F32)] * 3
            for side in sides:
                log = pick_row(logs[:, rows], 2 * pair + side)
                mean = pick_row(means[:, rows], 2 * pair + side)
                side_queries = queries * masks[side]
                side_grads = grads * masks[side]
                scores = by_cols(keys, side_queries) + shut
                weights = jnp.exp2(scores * scale - log)
                change = (weights * (by_cols(values, side_grads) - mean)).astype(BF16)
                terms = (
                    by_rows(change, keys * masks[side]),
                    dot(change, side_queries),
                    dot(weights.astype(BF16), side_grads),
                )
                sums = [part + term for part, term in zip(sums, terms, strict=True)]
            for total, part in zip(totals, sums, strict=True):
                total[rows, :] = part

    for_kept(gate, run)
    grad_query = totals[0][...] * final
    grad_q[...] = grad_query.astype(BF16)
    grad_k[...] = (totals[1][...] * final).astype(BF16)
    grad_v[...] = totals[2][...].astype(BF16)
    query_sum = column_sum(grad_query)
    value_sum = column_sum(totals[2][...])
    grads = jnp.concatenate([grad_q[...], grad_k[...], grad_v[...]], 1)
    weight_grad[...] = by_rows(hidden[...], grads).astype(BF16)
    bias_sums[...] = jnp.zeros_like(bias_sums)
    bias_sums[0:1, :] = query_sum
    bias_sums[1:2, :] = value_sum


def attend_back(meta, hidden, parts, grad_context, logs, means, pack, head_width, after=()):
    half = grad_context.shape[1]
    width = hidden.shape[1]
    lanes = 2 * head_width
    pairs = half // lanes
    column = pl.BlockSpec((ROWS, lanes), lambda i, meta: (0, i))
    return call(
        "attend_back",
        partial(attend_back_body, lanes),
        (pairs,),
        11,
        [meta],
        [(hidden, own_rows(width))]
        + [(part, column) for part in (*parts, grad_context)]
        + [(logs, whole(8, ROWS)), (means, whole(8, ROWS))]
        + [(pack, pl.BlockSpec((pack.shape[0], lanes), lambda i, meta: (0, i)))],
        [(bf16(ROWS, half), column)] * 3
        + [
            (
                bf16(width, 3 * half),
                pl.BlockSpec((width, 3 * lanes), lambda i, meta: (0, i)),
            ),
            (f32(8, half), pl.BlockSpec((8, lanes), lambda i, meta: (0, i))),
        ],
        scratch=[pltpu.VMEM((ROWS, lanes), F32)] * 3,
        after=after,
        vmem=24,
    )


(OUT_BIAS, LN1_GAIN, LN1_BIAS, FFN_OUT_BIAS, LN2_GAIN, LN2_BIAS, HID_EFF) = range(7)


def valid_column(meta):
    at = lax.broadcasted_iota(jnp.int32, (ROWS, 1), 0)
    found = jnp.zeros((ROWS, 1), F32)
    for place, (start, size) in enumerate(BUCKETS):
        found = jnp.where((at >= start) & (at < start + meta[place]), 1.0, found)
    return found


def norm_stats(resid):
    centred = resid - jnp.mean(resid, -1, keepdims=True)
    spread = lax.rsqrt(jnp.mean(centred * centred, -1, keepdims=True) + EPSILON)
    return (centred * spread, spread)


def norm_back(grad_out, normed, spread, gain):
    grad_normed = grad_out * gain
    first_mean = jnp.mean(grad_normed, -1, keepdims=True)
    second_mean = jnp.mean(grad_normed * normed, -1, keepdims=True)
    return spread * (grad_normed - first_mean - normed * second_mean)


def blocks_of(step):
    return [slice(at, at + step) for at in range(0, ROWS, step)]


def gelu_and_slope(z):
    below = 0.5 + 0.5 * lax.erf(z * 0.5**0.5)
    density = jnp.exp2((-0.5 * LOG2E) * (z * z)) * (0.5 / 3.141592653589793) ** 0.5
    return (z * below, below + z * density)


def ffn_body(
    chunks,
    row_step,
    meta,
    hidden,
    cotangent_all,
    gated_own,
    gated_other,
    out_own,
    out_other,
    vectors,
    pack_own,
    pack_other,
    in_own,
    in_other,
    ffn_own,
    ffn_other,
    layer_out_hbm,
    first_low_hbm,
    normed_hbm,
    attn_hbm,
    grad_low_hbm,
    grad_two_hbm,
    spread_one,
    inner_out,
    slope_out,
    weight_other,
    sums,
    first,
    total,
    inner,
    cotangent,
    layer_out,
    first_low,
    normed_one,
    attn_out,
    grad_low,
    grad_two,
    done,
):
    step = pl.program_id(0)
    cols = inner_out.shape[1]
    early = ((first_low, first_low_hbm), (normed_one, normed_hbm), (attn_out, attn_hbm))
    late = ((layer_out, layer_out_hbm), (grad_low, grad_low_hbm), (grad_two, grad_two_hbm))
    early = [pltpu.make_async_copy(*pair, done.at[at]) for at, pair in enumerate(early)]
    late = [pltpu.make_async_copy(*pair, done.at[3 + at]) for at, pair in enumerate(late)]
    mine = pl.ds(pl.multiple_of(meta[4] * ROWS, ROWS), ROWS)
    fetch = pltpu.make_async_copy(cotangent_all.at[mine, :], cotangent, done.at[6])

    @pl.when(step == 0)
    def _():
        fetch.start()
        for block in blocks_of(240):
            attn = (
                dot(gated_own[block, :], out_own[...])
                + dot(gated_other[block, :], out_other[...])
                + row_of(vectors, OUT_BIAS)
            )
            attn_out[block, :] = attn.astype(BF16)
            normed, spread = norm_stats(
                hidden[block, :].astype(F32) + attn * row_of(vectors, HID_EFF)
            )
            normed_one[block, :] = normed.astype(BF16)
            spread_one[block, :] = jnp.broadcast_to(spread, (240, 128))
            value = normed * row_of(vectors, LN1_GAIN) + row_of(vectors, LN1_BIAS)
            first[block, :] = value
            first_low[block, :] = value.astype(BF16)
            total[block, :] = jnp.broadcast_to(row_of(vectors, FFN_OUT_BIAS), value.shape)
        for copy in early:
            copy.start()

    def forward(pack, weight_in, weight_out):
        bias = pack[PACK_IN_BIAS : PACK_IN_BIAS + 1, :]
        eff = pack[PACK_FFN : PACK_FFN + 1, :]
        at = pl.multiple_of(step * cols, cols)
        for block in blocks_of(row_step):
            pre = dot(first_low[block, :], weight_in[...]) + bias
            value, slope = gelu_and_slope(pre)
            low = (value * eff).astype(BF16)
            inner_out[block, :] = low
            inner[block, pl.ds(at, cols)] = low
            slope_out[block, :] = (slope * eff).astype(BF16)
            total[block, :] += dot(low, weight_out[...])

    pl.when(step < chunks)(lambda: forward(pack_own, in_own, ffn_own))
    pl.when((step >= chunks) & (step < 2 * chunks))(
        lambda: forward(pack_other, in_other, ffn_other)
    )

    @pl.when(step == 2 * chunks)
    def _():
        for copy in early:
            copy.wait()
        fetch.wait()
        gain = row_of(vectors, LN2_GAIN)
        valid = valid_column(meta)
        hid_eff = row_of(vectors, HID_EFF)
        totals = [jnp.zeros((1, first.shape[1]), F32)] * 4
        for block in blocks_of(120):
            ffn_out = total[block, :]
            normed, spread = norm_stats(first[block, :] + ffn_out * hid_eff)
            layer_out[block, :] = (
                (normed * gain + row_of(vectors, LN2_BIAS)) * valid[block]
            ).astype(BF16)
            grad_final = cotangent[block, :].astype(F32) * valid[block]
            grad = norm_back(grad_final, normed, spread, gain)
            grad_ffn = grad * hid_eff
            grad_two[block, :] = grad
            grad_low[block, :] = grad_ffn.astype(BF16)
            terms = (grad_ffn, grad_final * normed, grad_final, grad * ffn_out)
            totals = [part + column_sum(term) for part, term in zip(totals, terms, strict=True)]
        sums[...] = jnp.zeros_like(sums)
        for place, part in enumerate(totals):
            sums[place : place + 1, :] = part
        for copy in late:
            copy.start()

    def backward(chunk, out):
        at = pl.multiple_of(chunk * cols, cols)
        out[...] = by_rows(inner[:, pl.ds(at, cols)], grad_low[...]).astype(BF16)

    pl.when(step >= 2 * chunks)(lambda: backward(step - chunks, weight_other))

    @pl.when(step == 3 * chunks - 1)
    def _():
        for copy in late:
            copy.wait()


def feed_forward(
    meta, hidden, cotangent, gated, outs, vectors, packs, ins, ffns, cols=768, row_step=480, after=()
):
    width = hidden.shape[1]
    half = gated[0].shape[1]
    units = ins[0].shape[1]
    chunks = units // cols
    column = pl.BlockSpec((ROWS, cols), lambda i, meta: (0, jnp.minimum(i, 2 * chunks - 1)))

    def part(first, i):
        return jnp.clip(i - first, 0, chunks - 1)

    def across(first, rows):
        return pl.BlockSpec((rows, cols), lambda i, meta: (0, part(first, i)))

    def down(first):
        return pl.BlockSpec((cols, width), lambda i, meta: (part(first, i), 0))

    low = bf16(ROWS, width)
    held = pltpu.VMEM((ROWS, width), BF16)
    wide = pltpu.VMEM((ROWS, width), F32)
    return call(
        "feed_forward",
        partial(ffn_body, chunks, row_step),
        (3 * chunks,),
        32,
        [meta],
        [
            (hidden, own_rows(width)),
            (cotangent, HBM),
            (gated[0], whole(ROWS, half)),
            (gated[1], whole(ROWS, half)),
            (outs[0], whole(half, width)),
            (outs[1], whole(half, width)),
            (vectors, whole(*vectors.shape)),
            (packs[0], across(0, packs[0].shape[0])),
            (packs[1], across(chunks, packs[1].shape[0])),
            (ins[0], across(0, width)),
            (ins[1], across(chunks, width)),
            (ffns[0], down(0)),
            (ffns[1], down(chunks)),
        ],
        [(low, HBM)] * 5
        + [
            (f32(ROWS, width), HBM),
            (f32(ROWS, 128), whole(ROWS, 128)),
            (bf16(ROWS, 2 * units), column),
            (bf16(ROWS, 2 * units), column),
            (bf16(units, width), down(2 * chunks)),
            (f32(8, width), whole(8, width)),
        ],
        scratch=[
            wide,
            wide,
            pltpu.VMEM((ROWS, 2 * units), BF16),
            held,
            held,
            held,
            held,
            held,
            held,
            wide,
            pltpu.SemaphoreType.DMA((7,)),
        ],
        after=after,
    )


def outer_body(left, right, out):
    out[...] = by_rows(left[...], right[...]).astype(BF16)


def outer(left, right, cols, after=(), step=512):
    width = right.shape[1]
    first = cols.start // step
    size = cols.stop - cols.start
    return call(
        "outer",
        outer_body,
        (size // step,),
        5,
        [],
        [
            (left, pl.BlockSpec((ROWS, step), lambda i: (0, i + first))),
            (right, whole(ROWS, width)),
        ],
        [(bf16(size, width), pl.BlockSpec((step, width), lambda i: (i, 0)))],
        after=after,
        vmem=16,
    )[0]


def shrink_body(
    chunks,
    row_step,
    grad_low,
    first_low_hbm,
    before_hbm,
    inner,
    slope,
    weight_in,
    weight_out,
    weight_grad,
    grad_first,
    unit_sums,
    kept,
    total,
    first_low,
    before,
    done,
):
    step = pl.program_id(0)
    fetch_low = pltpu.make_async_copy(first_low_hbm, first_low, done.at[0])
    fetch_before = pltpu.make_async_copy(before_hbm, before, done.at[1])

    @pl.when(step == 0)
    def _():
        fetch_low.start()
        fetch_before.start()

    bias_sum = jnp.zeros((1, inner.shape[1]), F32)
    gate_sum = jnp.zeros((1, inner.shape[1]), F32)
    for block in blocks_of(row_step):
        grad_inner = by_cols(grad_low[block, :], weight_out[...])
        grad_pre = grad_inner * slope[block, :].astype(F32)
        bias_sum += column_sum(grad_pre)
        gate_sum += column_sum(inner[block, :].astype(F32) * grad_inner)
        low = grad_pre.astype(BF16)
        kept[block, :] = low
        back = by_cols(low, weight_in[...])

        @pl.when(step == 0)
        def _(block=block, back=back):
            total[block, :] = back

        @pl.when((step > 0) & (step < chunks - 1))
        def _(block=block, back=back):
            total[block, :] += back

        @pl.when(step == chunks - 1)
        def _(block=block, back=back):
            if block.start == 0:
                fetch_before.wait()
            grad_first[block, :] = total[block, :] + back + before[block, :]

    unit_sums[...] = jnp.zeros_like(unit_sums)
    unit_sums[0:1, :] = bias_sum
    unit_sums[1:2, :] = gate_sum
    pl.when(step == 0)(fetch_low.wait)
    weight_grad[...] = by_rows(first_low[...], kept[...]).astype(BF16)


def shrink(
    side, grad_low, first_low, before, inner, slope, weight_in, weight_out, cols=512, row_step=960, after=()
):
    width, units = weight_in.shape
    chunks = units // cols
    full = whole(ROWS, width)
    across = pl.BlockSpec((width, cols), lambda i: (0, i))
    column = pl.BlockSpec((ROWS, cols), lambda i: (0, i + side * chunks))
    return call(
        "shrink",
        partial(shrink_body, chunks, row_step),
        (chunks,),
        12,
        [],
        [
            (grad_low, full),
            (first_low, HBM),
            (before, HBM),
            (inner, column),
            (slope, column),
            (weight_in, across),
            (weight_out, pl.BlockSpec((cols, width), lambda i: (i, 0))),
        ],
        [
            (bf16(width, units), across),
            (f32(ROWS, width), full),
            (f32(8, units), pl.BlockSpec((8, cols), lambda i: (0, i))),
        ],
        scratch=[
            pltpu.VMEM((ROWS, cols), BF16),
            pltpu.VMEM((ROWS, width), F32),
            pltpu.VMEM((ROWS, width), BF16),
            pltpu.VMEM((ROWS, width), F32),
            pltpu.SemaphoreType.DMA((2,)),
        ],
        after=after,
        vmem=36,
    )


def part_body(
    grad_first, normed_one, spread_one, attn_out, vectors, gated_own, gated_other, grad_one, low, weight_mine, weight_other, sums
):
    gain = row_of(vectors, LN1_GAIN)
    hid_eff = row_of(vectors, HID_EFF)
    totals = [jnp.zeros((1, grad_first.shape[1]), F32)] * 4
    for block in blocks_of(120):
        grad = grad_first[block, :]
        normed = normed_one[block, :].astype(F32)
        one = norm_back(grad, normed, spread_one[block, 0:1], gain)
        grad_one[block, :] = one
        attn = one * hid_eff
        low[block, :] = attn.astype(BF16)
        terms = (attn, grad * normed, grad, one * attn_out[block, :].astype(F32))
        totals = [part + column_sum(term) for part, term in zip(totals, terms, strict=True)]
    sums[...] = jnp.zeros_like(sums)
    for place, part in enumerate(totals):
        sums[place : place + 1, :] = part
    weight_other[...] = by_rows(gated_other[...], low[...]).astype(BF16)
    weight_mine[...] = by_rows(gated_own[...], low[...]).astype(BF16)


def part_norm(grad_first, normed_one, spread_one, attn_out, vectors, gated, after=()):
    width = grad_first.shape[1]
    half = gated[0].shape[1]
    values = [grad_first, normed_one, spread_one, attn_out, vectors, *gated]
    made = [
        f32(ROWS, width),
        bf16(ROWS, width),
        bf16(half, width),
        bf16(half, width),
        f32(8, width),
    ]
    return call(
        "part_norm",
        part_body,
        (1,),
        6,
        [],
        [(value, whole(*value.shape)) for value in values],
        [(shape, whole(*shape.shape)) for shape in made],
        after=after,
        vmem=28,
    )


def part_heads_body(
    head_width, low, gated_own, gated_other, out_own, out_other, pack_own, pack_other, context_own, context_other, means_own, means_other, sums
):
    half = gated_own.shape[1]
    head = lax.broadcasted_iota(jnp.int32, (8, half), 1) // head_width
    pick = (head == lax.broadcasted_iota(jnp.int32, (8, half), 0)).astype(BF16)
    sums[...] = jnp.zeros_like(sums)
    for place, (gated, weight, pack, context, means) in enumerate(
        (
            (gated_own, out_own, pack_own, context_own, means_own),
            (gated_other, out_other, pack_other, context_other, means_other),
        )
    ):
        column = jnp.zeros((1, half), F32)
        for start, size in BUCKETS:
            rows = slice(start, start + size)
            grads = by_cols(low[rows, :], weight[...])
            context[rows, :] = (grads * pack[PACK_HEAD : PACK_HEAD + 1, 0:half]).astype(BF16)
            terms = grads * gated[rows, :].astype(F32)
            column += column_sum(terms)
            high = terms.astype(BF16)
            rest = (terms - high.astype(F32)).astype(BF16)
            means[:, rows] = by_cols(pick, high) + by_cols(pick, rest)
        sums[place : place + 1, :] = column


def part_heads(low, gated, outs, packs, head_width, after=()):
    half = gated[0].shape[1]
    values = [low, *gated, *outs, *packs]
    made = [
        bf16(ROWS, half),
        bf16(ROWS, half),
        f32(8, ROWS),
        f32(8, ROWS),
        f32(8, half),
    ]
    return call(
        "part_heads",
        partial(part_heads_body, head_width),
        (1,),
        5,
        [],
        [(value, whole(*value.shape)) for value in values],
        [(shape, whole(*shape.shape)) for shape in made],
        after=after,
        vmem=28,
    )


def add_back_body(start, *refs):
    grads, weights, out = refs[:6], refs[6:12], refs[12]
    total = start[...]
    for side in (0, 3):
        left = jnp.concatenate([part[...] for part in grads[side : side + 3]], 1)
        right = jnp.concatenate([part[...] for part in weights[side : side + 3]], 1)
        total += by_cols(left, right)
    out[...] = total


def add_back(start, grads, weights, after=()):
    width = start.shape[1]
    half = grads[0].shape[1]
    step = ROWS // 4
    return call(
        "add_back",
        add_back_body,
        (4,),
        6,
        [],
        [(start, pl.BlockSpec((step, width), lambda i: (i, 0)))]
        + [(part, pl.BlockSpec((step, half), lambda i: (i, 0))) for part in grads]
        + [(part, whole(width, half)) for part in weights],
        [(f32(ROWS, width), pl.BlockSpec((step, width), lambda i: (i, 0)))],
        after=after,
        vmem=24,
    )[0]


def swap_bit(values, dp_size, bit):
    return lax.ppermute(values, "dp", [(at, at ^ (1 << bit)) for at in range(dp_size)])


TAIL = 128


def load(ref, rows, tail):
    values = ref[rows, :].astype(F32)
    if not tail:
        return values, None
    cut = values.shape[1] - TAIL
    return values[:, :cut], values[:, cut : cut + TAIL // 2] + values[:, cut + TAIL // 2 :]


def store(ref, main, extra):
    if extra is None:
        ref[...] = main.astype(ref.dtype)
        return
    cut = main.shape[1]
    high = extra.astype(BF16)
    ref[:, :cut] = main.astype(BF16)
    ref[:, cut : cut + TAIL // 2] = high
    ref[:, cut + TAIL // 2 :] = (extra - high.astype(F32)).astype(BF16)


def split_by(side, totals, kept, sent):
    for part, total in enumerate(totals):

        @pl.when(side == part)
        def _(total=total):
            store(kept, *total)

        @pl.when(side != part)
        def _(total=total):
            store(sent, *total)


def add(left, right):
    return tuple(None if a is None else a + b for a, b in zip(left, right, strict=True))


class Stream:
    def __init__(self, ins, shape, first, order, tail=False):
        self.ins = ins
        self.rows, self.cols = shape
        self.first = first
        self.order = order
        self.tail = tail
        self.stage = 0
        self.kept = self.value = self.arrived = None

    def job(self):
        stages = len(self.order)
        stage, tail = self.stage, self.tail
        size = self.rows >> stage if stage <= stages else self.value.shape[0]
        if stage < stages:
            half = size // 2
            ins = list(self.ins) if stage == 0 else [self.kept, self.arrived]

            def body(sides, *refs):
                *given, kept, sent = refs
                totals = []
                for at in (0, half):
                    rows = slice(at, at + half)
                    if stage == 0:
                        totals.append(self.first(given, rows))
                    else:
                        totals.append(add(*[load(ref, rows, tail) for ref in given]))
                split_by(sides[self.order[stage]], totals, kept, sent)

            return ins, [bf16(half, self.cols)] * 2, body
        if stage == stages:

            def body(sides, kept, arrived, value):
                rows = slice(0, size)
                store(value, *add(load(kept, rows, tail), load(arrived, rows, tail)))

            return [self.kept, self.arrived], [bf16(size, self.cols)], body
        bit = self.order[2 * stages - stage]

        def body(sides, own, arrived, value):
            for first, halves in in_order(sides[bit], own, arrived):

                @pl.when(first)
                def _(halves=halves):
                    for place, half in enumerate(halves):
                        value[place * size : place * size + size, :] = half[...]

        return [self.value, self.arrived], [bf16(2 * size, self.cols)], body

    def take(self, outs, dp_size):
        stages = len(self.order)
        if self.stage < stages:
            self.kept, sent = outs
            self.arrived = swap_bit(sent, dp_size, self.order[self.stage])
        else:
            (self.value,) = outs
            bit = self.order[2 * stages - 1 - self.stage]
            self.arrived = swap_bit(self.value, dp_size, bit)
        self.stage += 1

    def last(self):
        return self.stage == 2 * len(self.order)


class Gather:
    def __init__(self, streams, order):
        self.streams = streams
        self.order = order
        self.stage = 0
        self.value = self.arrived = None

    def job(self):
        stage = self.stage
        if stage == 0:
            ins = [part for stream in self.streams for part in (stream.kept, stream.arrived)]
            size = self.streams[0].kept.shape[0]

            def body(sides, *refs):
                *given, value = refs
                at = 0
                for stream, kept, arrived in zip(
                    self.streams, given[::2], given[1::2], strict=True
                ):
                    rows, tail = slice(0, size), stream.tail
                    total = add(load(kept, rows, tail), load(arrived, rows, tail))
                    store(value.at[:, at : at + stream.cols], *total)
                    at += stream.cols

            cols = sum(stream.cols for stream in self.streams)
            return ins, [bf16(size, cols)], body
        size, cols = self.value.shape

        def body(sides, own, arrived, value):
            for first, halves in in_order(sides[self.order[stage - 1]], own, arrived):

                @pl.when(first)
                def _(halves=halves):
                    for place, half in enumerate(halves):
                        value[place * size : place * size + size, :] = half[...]

        return [self.value, self.arrived], [bf16(2 * size, cols)], body

    def take(self, outs, dp_size):
        (self.value,) = outs
        self.arrived = swap_bit(self.value, dp_size, self.order[self.stage])
        self.stage += 1

    def last(self):
        return self.stage == len(self.order)


class Quad:
    def __init__(self, front, beside, back, orders):
        self.front, self.beside, self.back = front, beside, back
        self.orders = orders
        self.stage = 0
        self.values = self.arrived = self.kept = None
        self.first, self.second = front.order[2:]

    def to_partners(self, values, dp_size):
        found = []
        for number, value in enumerate(values, 1):
            flip = (number >> 1) << self.first | (number & 1) << self.second
            pairs = [(at, at ^ flip) for at in range(dp_size)]
            found.append(lax.ppermute(value, "dp", pairs))
        return found

    def place(self, sides):
        return 2 * sides[self.first] + sides[self.second]

    def job(self):
        front, beside, back = self.front, self.beside, self.back
        width = front.cols + back.cols
        if self.stage == 0:
            size = front.rows // 16
            ins = [front.kept, front.arrived, back.kept, back.arrived]

            def body(sides, *refs):
                given, outs = refs[:4], refs[4:]
                totals = []
                for at in range(4):
                    rows = slice(at * size, (at + 1) * size)
                    one, _ = add(*[load(ref, rows, False) for ref in given[:2]])
                    two, extra = add(*[load(ref, rows, True) for ref in given[2:]])
                    totals.append((jnp.concatenate([one, two], 1), extra))
                for mine in range(4):

                    @pl.when(self.place(sides) == mine)
                    def _(mine=mine):
                        for number, out in enumerate(outs):
                            store(out, *totals[mine ^ number])

            return ins, [bf16(size, width)] * 4, body
        if self.stage == 1:
            size = self.kept.shape[0]
            ins = [self.kept, *self.arrived, beside.kept, beside.arrived]

            def body(sides, *refs):
                *given, out = refs
                rows = slice(0, size)
                total = load(given[0], rows, True)
                for ref in given[1:4]:
                    total = add(total, load(ref, rows, True))
                extra = add(*[load(ref, rows, False) for ref in given[4:]])[0]
                main = [total[0][:, : front.cols], extra, total[0][:, front.cols :]]
                store(out, jnp.concatenate(main, 1), total[1])

            return ins, [bf16(size, width + beside.cols)], body
        cut = front.cols + beside.cols
        if self.stage == 2:
            size = self.values[0].shape[0]

            def body(sides, *refs):
                given, outs = refs[:4], refs[4:]
                for mine in range(4):

                    @pl.when(self.place(sides) == mine)
                    def _(mine=mine):
                        for number, ref in enumerate(given):
                            at = mine ^ number
                            at = (at >> 1) + 2 * (at & 1) if self.swapped() else at
                            rows = slice(at * size, (at + 1) * size)
                            outs[0][rows, :] = ref[:, :cut]
                            outs[1][rows, :] = ref[:, cut:]

            made = [bf16(4 * size, cut), bf16(4 * size, back.cols)]
            return [self.values[0], *self.arrived], made, body
        size = self.values[0].shape[0]
        bits = [order[2] for order in self.orders]

        def body(sides, *refs):
            for at, bit in enumerate(bits):
                own, arrived, out = refs[2 * at], refs[2 * at + 1], refs[4 + at]
                for first, halves in in_order(sides[bit], own, arrived):

                    @pl.when(first)
                    def _(halves=halves, out=out):
                        for place, half in enumerate(halves):
                            out[place * size : place * size + size, :] = half[...]

        ins = [value for pair in zip(self.values, self.arrived, strict=True) for value in pair]
        return ins, [bf16(2 * size, cut), bf16(2 * size, back.cols)], body

    def swapped(self):
        return self.orders[0][0] == self.first

    def take(self, outs, dp_size):
        if self.stage == 0:
            self.kept = outs[0]
            self.arrived = self.to_partners(outs[1:], dp_size)
        elif self.stage == 1:
            self.values = list(outs)
            self.arrived = self.to_partners([outs[0]] * 3, dp_size)
        else:
            self.values = list(outs)
            self.arrived = [
                swap_bit(value, dp_size, order[self.stage])
                for value, order in zip(outs, self.orders, strict=True)
            ]
        self.stage += 1

    def gathers(self):
        found = []
        for at, streams in enumerate(([self.front, self.beside], [self.back])):
            gather = Gather(streams, self.orders[at])
            gather.value, gather.arrived = self.values[at], self.arrived[at]
            found.append(gather)
        return found


def in_order(side, own, arrived):
    return (side == 0, (own, arrived)), (side == 1, (arrived, own))


def small_call(name, body, ins, outs, sides, after=()):
    return call(
        name,
        body,
        (1,),
        2,
        [sides],
        [(value, whole(*value.shape)) for value in ins],
        [(shape, whole(*shape.shape)) for shape in outs],
        after=after,
        vmem=24,
    )


def advance(streams, dp_size, sides, after=()):
    jobs = [stream.job() for stream in streams]
    ins = [value for job in jobs for value in job[0]]
    outs = [shape for job in jobs for shape in job[1]]

    def body(sides, *refs):
        given, made = refs[: len(ins)], refs[len(ins) :]
        for inputs, shapes, work in jobs:
            work(sides, *given[: len(inputs)], *made[: len(shapes)])
            given, made = given[len(inputs) :], made[len(shapes) :]

    found = small_call("advance", body, ins, outs, sides, after)
    for stream, job in zip(streams, jobs, strict=True):
        stream.take(found[: len(job[1])], dp_size)
        found = found[len(job[1]) :]


def states(streams):
    return [stream.kept if stream.value is None else stream.value for stream in streams]


def blocks_in(gather):
    streams, order = gather.streams, gather.order
    bits = len(order)
    size = streams[0].rows >> bits
    for block in range(1 << bits):
        device = sum((block >> turn & 1) << bit for turn, bit in enumerate(order))
        half, inside = divmod(block, 1 << (bits - 1))
        places = [
            size
            * sum((device >> bit & 1) << (bits - 1 - turn) for turn, bit in enumerate(stream.order))
            for stream in streams
        ]
        yield half, slice(inside * size, (inside + 1) * size), places, size


def finish(gathers, sides, by_cols, after=()):
    rows, cols = gathers[0].streams[0].rows, gathers[0].streams[0].cols

    def body(sides, *refs):
        *given, out = refs
        for at, gather in enumerate(gathers):
            pair = given[2 * at : 2 * at + 2]
            top, left = (0, at * cols) if by_cols else (at * rows, 0)
            for first, halves in in_order(sides[gather.order[-1]], *pair):

                @pl.when(first)
                def _(gather=gather, halves=halves, top=top, left=left):
                    for half, where, (row,), size in blocks_in(gather):
                        out[top + row : top + row + size, left : left + cols] = halves[half][
                            where, :
                        ].astype(F32)

    ins = [value for gather in gathers for value in (gather.value, gather.arrived)]
    shape = (rows, 2 * cols) if by_cols else (2 * rows, cols)
    return small_call("finish", body, ins, [f32(*shape)], sides, after)[0]


def orders_of(dp_size):
    bits = dp_size.bit_length() - 1
    if bits == 4:
        halved = (0, 1, 2, 3), (1, 0, 2, 3), (2, 0, 1, 3), (0, 2, 3, 1), (0, 1, 2, 3), (1, 0, 2, 3)
        doubled = (1, 3, 2, 0), (3, 0, 1, 2), (3, 2, 0, 1), (3, 2, 1, 0), (3, 2, 0, 1), (0, 3, 2, 1)
        return halved + doubled
    return tuple(tuple((at + turn) % bits for at in range(bits)) for turn in range(12))


def late_streams(qkv, small, orders):
    rows, cols = qkv[0].shape
    cut = -(-(cols + TAIL) // 256) * 128
    places = small[0].shape[1] // (TAIL // 2)
    depth = small[0].shape[0]

    def front(given, where):
        return sum(ref[where, 0:cut].astype(F32) for ref in given), None

    def back(given, where):
        first, size = where.start, where.stop - where.start
        main = sum(ref[where, cut:cols].astype(F32) for ref in given[0:2])
        extra = []
        for place in range(first // depth, (first + size) // depth):
            if place < places:
                at = slice(place * TAIL // 2, (place + 1) * TAIL // 2)
                extra.append(sum(ref[:, at] for ref in given[2:4]))
        used = depth * len(extra)
        if used < size:
            extra.append(jnp.zeros((size - used, TAIL // 2), F32))
        return main, jnp.concatenate(extra, 0)

    return [
        Stream(qkv, (rows, cut), front, orders[0]),
        Stream((*qkv, *small), (rows, cols - cut + TAIL), back, orders[1], True),
    ]


def finish_late(gathers, sides, lanes, small_shape, after=()):
    (front, out_stream), (back,) = [gather.streams for gather in gathers]
    rows, half = front.rows, out_stream.cols
    depth, width = small_shape
    cut = front.cols
    places = width // (TAIL // 2)

    def body(sides, own0, arrived0, own1, arrived1, qkv_out, out_out, small_out):
        def qkv_part(values, row, where, first, cols):
            for at in range(0, cols, lanes):
                pair, kind = divmod((first + at) // lanes, 3)
                columns = slice(pair * lanes, (pair + 1) * lanes)
                lines = slice(row, row + where.stop - where.start)
                qkv_out[lines, kind, columns] = values[where, at : at + lanes].astype(F32)

        for first, halves in in_order(sides[gathers[0].order[-1]], own0, arrived0):

            @pl.when(first)
            def _(halves=halves):
                for number, where, (row, other_row), size in blocks_in(gathers[0]):
                    qkv_part(halves[number], row, where, 0, cut)
                    side = other_row // half
                    line = other_row - side * half
                    out_out[line : line + size, side * half : (side + 1) * half] = halves[number][
                        where, cut : cut + half
                    ].astype(F32)

        for first, halves in in_order(sides[gathers[1].order[-1]], own1, arrived1):

            @pl.when(first)
            def _(halves=halves):
                for number, where, (row,), size in blocks_in(gathers[1]):
                    qkv_part(halves[number], row, where, cut, back.cols - TAIL)
                    cuts = sorted({row, row + size, *range(-(-row // depth) * depth, row + size, depth)})
                    for at, end in zip(cuts, cuts[1:]):
                        place, line = divmod(at, depth)
                        count = end - at
                        if place < places:
                            top = where.start + at - row
                            _, extra = load(halves[number], slice(top, top + count), True)
                            columns = slice(place * TAIL // 2, (place + 1) * TAIL // 2)
                            small_out[line : line + count, columns] = extra

    ins = [value for gather in gathers for value in (gather.value, gather.arrived)]
    outs = [f32(rows, 3, half), f32(half, rows), f32(depth, width)]
    return small_call("finish_late", body, ins, outs, sides, after)


def pack_sums(part_sums, turn_sums, head_sums, bias_sums, unit_sums, after=()):
    width = part_sums.shape[1]
    half = bias_sums[0].shape[1]
    unit_rows = unit_sums[0].shape[1] // width

    def body(part, turned, heads, bias_own, bias_other, unit_own, unit_other, mine, theirs):
        sides = ((mine, bias_own, unit_own), (theirs, bias_other, unit_other))
        for side, (out, bias, unit) in enumerate(sides):
            out[...] = jnp.zeros_like(out)
            out[0:4, :] = part[0:4, :]
            out[4:8, :] = turned[0:4, :]
            out[8:9, 0:half] = bias[0:1, :]
            out[8:9, half : 2 * half] = bias[1:2, :]
            out[9:10, 0:half] = heads[side : side + 1, :]
            for kind in (0, 1):
                for row in range(unit_rows):
                    place = 10 + kind * unit_rows + row
                    out[place : place + 1, :] = unit[
                        kind : kind + 1, row * width : (row + 1) * width
                    ]

    values = [part_sums, turn_sums, head_sums, *bias_sums, *unit_sums]
    rows = -(-(10 + 2 * unit_rows) // 8) * 8
    return call(
        "pack_sums",
        body,
        (1,),
        1,
        [],
        [(value, whole(*value.shape)) for value in values],
        [(f32(rows, width), whole(rows, width))] * 2,
        after=after,
        vmem=24,
    )


def per_device(
    dp_size,
    hidden,
    cotangent,
    counts,
    lengths,
    qkv_weight,
    qv_bias,
    out_weight,
    out_bias,
    ln1_gain,
    ln1_bias,
    in_weight,
    in_bias,
    ffn_out_weight,
    ffn_out_bias,
    ln2_gain,
    ln2_bias,
    head_gate,
    head_mask,
    ffn_gate,
    ffn_mask,
    hidden_gate,
    hidden_mask,
):
    width = hidden.shape[1]
    own_heads = head_gate.shape[0]
    half = qkv_weight.shape[2]
    units = in_weight.shape[1]
    head_width = half // own_heads
    head_at = lax.axis_index("head")

    def other(values):
        return lax.ppermute(values, "head", [(0, 1), (1, 0)])

    def pad_to(values, size):
        return jnp.pad(values, (0, size - values.shape[0]))

    meta = jnp.concatenate(
        [
            lax.dynamic_index_in_dim(
                jnp.where(counts[0] > 0, lengths[0], 0), head_at, 0, keepdims=False
            ),
            head_at[None],
        ]
    )
    head_flags = head_mask.astype(F32)
    ffn_flags = ffn_mask.astype(F32)
    hidden_flags = hidden_mask.astype(F32)
    pack = jnp.stack(
        [
            in_bias,
            ffn_gate * ffn_flags,
            pad_to(qv_bias.reshape(-1), units),
            pad_to(jnp.repeat(head_gate * head_flags, head_width), units),
        ]
    )
    vectors = jnp.stack(
        [
            out_bias,
            ln1_gain,
            ln1_bias,
            ffn_out_bias,
            ln2_gain,
            ln2_bias,
            hidden_gate * hidden_flags,
        ]
    )
    qkv_own = [qkv_weight[:, at] for at in range(3)]
    qkv_other = [other(part) for part in qkv_own]
    packs = (pack, other(pack))
    outs = (out_weight, other(out_weight))
    ins = (in_weight, other(in_weight))
    ffns = (ffn_out_weight, other(ffn_out_weight))
    sides = jnp.stack([(lax.axis_index("dp") >> bit) & 1 for bit in range(dp_size.bit_length() - 1)])
    orders = orders_of(dp_size)
    step = partial(advance, dp_size=dp_size, sides=sides)

    def halves(size, at):
        return slice(at * size // 2, (at + 1) * size // 2)

    def sum_stream(left, right, order, rows=None, cols=None):
        rows = rows or slice(0, left.shape[0])
        cols = cols or slice(0, left.shape[1])

        def first(given, at):
            at = slice(rows.start + at.start, rows.start + at.stop)
            return sum(ref[at, cols].astype(F32) for ref in given), None

        shape = (rows.stop - rows.start, cols.stop - cols.start)
        return Stream((left, right), shape, first, order)

    *qkv0, gated0, logs0 = attend(meta, hidden, qkv_own, packs[0], head_width)
    *qkv1, gated1, logs1 = attend(meta, hidden, qkv_other, packs[1], head_width, [gated0])
    gated = (gated0, gated1)
    (
        layer_out,
        first_low,
        normed_one,
        attn_out,
        grad_low,
        grad_two,
        spread_one,
        inner,
        slope,
        ffn_grad_other,
        turn_sums,
    ) = feed_forward(meta, hidden, cotangent, gated, outs, vectors, packs, ins, ffns)
    ffn_grad_theirs = other(ffn_grad_other)
    ffn_grad_mine = outer(inner, grad_low, slice(0, units))
    streams = [
        sum_stream(ffn_grad_mine, ffn_grad_theirs, orders[at], rows=halves(units, at))
        for at in (0, 1)
    ]
    step(streams)
    in_grad_other, grad_first, unit_sums1 = shrink(
        1, grad_low, first_low, grad_two, inner, slope, ins[1], ffns[1], after=states(streams)
    )
    in_grad_theirs = other(in_grad_other)
    step(streams, after=[grad_first])
    in_grad_mine, grad_first, unit_sums0 = shrink(
        0, grad_low, first_low, grad_first, inner, slope, ins[0], ffns[0], after=states(streams)
    )
    in_streams = [
        sum_stream(in_grad_mine, in_grad_theirs, orders[2 + at], cols=halves(units, at))
        for at in (0, 1)
    ]
    streams += in_streams
    step(streams, after=[grad_first])
    grad_one, attn_low, out_grad_mine, out_grad_other, part_sums = part_norm(
        grad_first,
        normed_one,
        spread_one,
        attn_out,
        vectors,
        gated,
        after=states(streams),
    )
    out_grad_theirs = other(out_grad_other)
    grad_context0, grad_context1, means0, means1, head_sums = part_heads(
        attn_low, gated, outs, packs, head_width
    )

    def out_part(given, at):
        side = at.start // half
        rows = slice(at.start - side * half, at.stop - side * half)
        cols = slice(side * half, (side + 1) * half)
        return sum(ref[rows, cols].astype(F32) for ref in given), None

    out_stream = Stream((out_grad_mine, out_grad_theirs), (width, half), out_part, orders[4])
    streams = [*streams[:2], out_stream]
    step(streams, after=[grad_context0])
    *mixed1, qkv_grad_other, bias_sums1 = attend_back(
        meta,
        hidden,
        qkv1,
        grad_context1,
        logs1,
        means1,
        packs[1],
        head_width,
        after=states(streams),
    )
    qkv_grad_theirs = other(qkv_grad_other)
    ffn_gathers = [Gather(streams[at : at + 1], orders[(6, 11)[at]]) for at in (0, 1)]
    streams = [*ffn_gathers, *in_streams, out_stream]
    step(streams, after=[mixed1[0]])
    *mixed0, qkv_grad_mine, bias_sums0 = attend_back(
        meta,
        hidden,
        qkv0,
        grad_context0,
        logs0,
        means0,
        packs[0],
        head_width,
        after=states(streams) + [mixed1[0]],
    )
    step(streams, after=[mixed0[0]])
    small = pack_sums(
        part_sums,
        turn_sums,
        head_sums,
        (bias_sums0, bias_sums1),
        (unit_sums0, unit_sums1),
        after=states(streams),
    )
    late = late_streams(
        (qkv_grad_mine, qkv_grad_theirs), (small[0], other(small[1])), orders[4:6]
    )
    step(late)
    grad_hidden = add_back(
        grad_one, mixed0 + mixed1, qkv_own + qkv_other, after=states(streams + late)
    )
    step([*ffn_gathers, *in_streams, out_stream, *late], after=[grad_hidden])
    gathers = [Gather(in_streams[at : at + 1], orders[7 + at]) for at in (0, 1)]
    if dp_size == 16:
        quad = Quad(late[0], out_stream, late[1], orders[9:11])
        step([*ffn_gathers, *gathers, quad])
        step([*gathers, quad], after=[gather.arrived for gather in ffn_gathers])
        step([*gathers, quad])
        step([*gathers, quad])
        late = quad.gathers()
    else:
        while late[0].stage < len(late[0].order):
            step(late)
        while out_stream.stage < len(out_stream.order):
            step([out_stream])
        late = [Gather([late[0], out_stream], orders[9]), Gather([late[1]], orders[10])]
        for gather in gathers:
            while not gather.last():
                step([gather])
        for gather in ffn_gathers:
            while not gather.last():
                step([gather])
        while not late[0].last():
            step(late)
    grad_ffn_out_weight = finish(ffn_gathers, sides, by_cols=False)
    grad_in_weight = finish(gathers, sides, by_cols=True)
    grad_qkv_weight, grad_out_weight, small = finish_late(
        late, sides, 2 * head_width, small[0].shape
    )
    (
        grad_out_bias,
        grad_ln1_gain,
        grad_ln1_bias,
        gate_one,
        grad_ffn_out_bias,
        grad_ln2_gain,
        grad_ln2_bias,
        gate_two,
    ) = small[:8]
    unit_rows = units // width
    return (
        layer_out,
        grad_hidden,
        grad_qkv_weight,
        small[8].reshape(2, half),
        grad_out_weight,
        grad_out_bias,
        grad_ln1_gain,
        grad_ln1_bias,
        grad_in_weight,
        small[10 : 10 + unit_rows].reshape(-1),
        grad_ffn_out_weight,
        grad_ffn_out_bias,
        grad_ln2_gain,
        grad_ln2_bias,
        jnp.sum(small[9, :half].reshape(own_heads, head_width), 1) * head_flags / head_gate,
        small[10 + unit_rows : 10 + 2 * unit_rows].reshape(-1) * ffn_flags / ffn_gate,
        (gate_one + gate_two) * hidden_flags,
    )


def solution(mesh):
    placed = (
        P("dp", None),
        P("dp", None),
        P("dp", None, None),
        P("dp", None, None),
        P(None, None, "head"),
        P(None, "head"),
        P("head", None),
        P(),
        P(),
        P(),
        P(None, "head"),
        P("head"),
        P("head", None),
        P(),
        P(),
        P(),
        P("head"),
        P("head"),
        P("head"),
        P("head"),
        P(),
        P(),
    )
    return jax.shard_map(
        partial(per_device, mesh.shape["dp"]),
        mesh=mesh,
        in_specs=placed,
        out_specs=(
            P(("dp", "head"), None),
            P(("dp", "head"), None),
            P(None, None, "head"),
            P(None, "head"),
            P("head", None),
            P(),
            P(),
            P(),
            P(None, "head"),
            P("head"),
            P("head", None),
            P(),
            P(),
            P(),
            P("head"),
            P("head"),
            P(),
        ),
        check_vma=False,
    )
```
